32 devices in a mesh: grp: 8 (over y, x, core), ep: 4 (over z).
Axes of the slice: x: 2, y: 2, z: 4, core: 2. Of those that a mesh axis runs over, the one named last changes fastest.
Arguments:
- residual_in: bfloat16 [4096, 2048], P(('grp', 'ep')), may hold values from -6 to 6
- attention_gain: bfloat16 [2048], replicated, may hold values from 0.5 to 1.5
- query_weight: bfloat16 [2048, 2048], P('grp', 'ep'), may hold values from -0.125 to 0.125
- query_bias: bfloat16 [2048], P('ep'), may hold values from -1.5 to 1.5
- key_weight: bfloat16 [2048, 2048], P('grp', 'ep'), may hold values from -0.125 to 0.125
- key_bias: bfloat16 [2048], P('ep'), may hold values from -1.5 to 1.5
- value_weight: bfloat16 [2048, 2048], P('grp', 'ep'), may hold values from -0.125 to 0.125
- value_bias: bfloat16 [2048], P('ep'), may hold values from -1.5 to 1.5
- output_weight: bfloat16 [2048, 2048], P('ep', 'grp'), may hold values from -1 to 1
- feedforward_gain: bfloat16 [2048], replicated, may hold values from 0.5 to 1.5
- router_weight: bfloat16 [2048, 8], replicated, may hold values from -0.0625 to 0.0625
- shared_logit_weight: bfloat16 [2048], replicated, may hold values from -0.125 to 0.125
- shared_gate_weight: bfloat16 [2048, 5632], P('grp', 'ep'), may hold values from -0.125 to 0.125
- shared_up_weight: bfloat16 [2048, 5632], P('grp', 'ep'), may hold values from -0.125 to 0.125
- shared_down_weight: bfloat16 [5632, 2048], P('ep', 'grp'), may hold values from -0.21875 to 0.21875
- expert_gate: bfloat16 [8, 2048, 1408], P('ep', 'grp'), may hold values from -0.125 to 0.125
- expert_up: bfloat16 [8, 2048, 1408], P('ep', 'grp'), may hold values from -0.125 to 0.125
- expert_down: bfloat16 [8, 1408, 2048], P('ep', 'grp'), may hold values from -0.875 to 0.875
- cotangent: bfloat16 [4096, 2048], P(('grp', 'ep')), may hold values from -6 to 6
- expert_index: int32 [4096, 4], P(('grp', 'ep')), may hold values from 0 to 7, all different within a row; in each aligned block of 128 rows (0 to 127, 128 to 255, ...) at most 96 rows name the same one
- token_live: int32 [4096], P(('grp', 'ep')), may hold values 0 or 1
- document_lengths: int32 [2, 4], replicated, may hold values from 1 to 1024, 2048 in all within a row
Outputs:
- layer_out: bfloat16 [4096, 2048], P(('grp', 'ep'))
- input_grad: float32 [4096, 2048], P(('grp', 'ep'))
- attention_gain_grad: float32 [2048], replicated
- query_weight_grad: float32 [2048, 2048], P('grp', 'ep')
- query_bias_grad: float32 [2048], P('ep')
- key_weight_grad: float32 [2048, 2048], P('grp', 'ep')
- key_bias_grad: float32 [2048], P('ep')
- value_weight_grad: float32 [2048, 2048], P('grp', 'ep')
- value_bias_grad: float32 [2048], P('ep')
- output_weight_grad: float32 [2048, 2048], P('ep', 'grp')
- feedforward_gain_grad: float32 [2048], replicated
- router_weight_grad: float32 [2048, 8], replicated
- shared_logit_grad: float32 [2048], replicated
- shared_gate_grad: float32 [2048, 5632], P('grp', 'ep')
- shared_up_grad: float32 [2048, 5632], P('grp', 'ep')
- shared_down_grad: float32 [5632, 2048], P('ep', 'grp')
- expert_gate_grad: float32 [8, 2048, 1408], P('ep', 'grp')
- expert_up_grad: float32 [8, 2048, 1408], P('ep', 'grp')
- expert_down_grad: float32 [8, 1408, 2048], P('ep', 'grp')
The draws below stay inside these ranges and needn't reach their ends.
Inputs may be any that keep to these rules, and one draw needn't show every extreme that they name: `expert_index`: each row names 4 different experts; among the rows of one device no expert is named more than 96 times, a bound that some block reaches there. `document_lengths`: each row sums to 2048, and its largest entry is 1024.
All inputs are finite; a program needn't handle non-finite values. No bound on the sum of `token_live` on one device may be relied on, other than what follows from the above.
Results may differ from the reference program's by a relative error of at most 0.024.
Values may be sent and summed in bfloat16 or wider, within the bound.
A program may use at most 320 MiB of HBM per device.

```python
import math
import jax
import jax.numpy as jnp
import numpy as np
from jax import lax

D = 2048
HEADS = 16
HDIM = 128
FFE = 1408
FFS = 5632
TOP = 4
TOK_DEV = 128
SEQS = 2
DOCS = 4
WINDOW = 1024
EXPERTS = 8
CAP = 96
TOKENS = 4096
SEQ = 2048


def place_ends(entries, own_key, smallest, top_value):
    spot = [jax.random.randint(jax.random.fold_in(own_key, axis), (), 0, length) for axis, length in enumerate(entries.shape)]
    longest = entries.shape.index(max(entries.shape))
    neighbour = spot[:longest] + [(spot[longest] + 1) % entries.shape[longest]] + spot[longest + 1:]
    return entries.at[tuple(spot)].set(smallest).at[tuple(neighbour)].set(top_value)


def block_scale(key, shape, split, smallest, high):
    def one(dim, shards_of):
        draws = jax.random.uniform(jax.random.fold_in(jax.random.fold_in(key, 6), dim), (shards_of,), jnp.float32, smallest / len(split), high / len(split))
        return jnp.repeat(jnp.exp(draws), shape[dim] // shards_of).reshape((-1,) + (1,) * (len(shape) - dim - 1))

    level = one(*split[0])
    for cut in split[1:]:
        level = level * one(*cut)
    return level


def profile(amount, total, most, skew):
    weights = [(1 << 20) // math.isqrt(grade ** skew) + 1 for grade in range(2, amount + 1)]
    surplus, counts = total - most - (amount - 1), [1] * (amount - 1)
    while surplus > 0:
        movable = [i for i in range(amount - 1) if counts[i] < most]
        mass, remaining = sum([weights[i] for i in movable]), surplus
        for i in movable:
            more = min(most - counts[i], max(1, remaining * weights[i] // mass), surplus)
            counts[i] = counts[i] + more
            surplus = surplus - more
    return np.array([most] + counts)


def uneven_parts(key, count, total, most, slope):
    if count == 2:
        one = jax.random.randint(key, (), max(1, total - most), min(most, total - 1) + 1)
        return jnp.stack([one, total - one])
    sizes = jnp.asarray(profile(count, total, most, slope), jnp.int32)
    twos = (count - 1) // 2
    giver, taker = sizes[1:1 + 2 * twos:2], sizes[2:2 + 2 * twos:2]
    room = jnp.minimum(giver - 1, most - taker)
    moved = jax.random.randint(jax.random.fold_in(key, 1), (twos,), 0, 1 << 20) % (room + 1)
    sizes = sizes.at[1:1 + 2 * twos:2].set(giver - moved).at[2:2 + 2 * twos:2].set(taker + moved)
    return sizes[jax.random.permutation(jax.random.fold_in(key, 2), count)]


def routed_block(stream_key, own, number, rows, count, top, most, slope):
    order = jax.random.permutation(stream_key, count)
    heavy_load, common = portions_of(count, rows * top, most, slope, True), portions_of(count, rows * top, most, slope, False)
    places = jnp.arange(count)

    def named(sizes, turn):
        used = int((sizes > 0).sum())
        fixed = max(1, used // 4)
        passed = fixed + (places - fixed + turn * (used - fixed)) % max(1, count - fixed)
        return jnp.zeros((count,), jnp.int32).at[order[jnp.where(places < fixed, places, passed)]].set(jnp.asarray(sizes, jnp.int32))

    sizes = jnp.where(number % 4 == 0, named(heavy_load, number // 4), named(common, number - number // 4 - 1))
    mixed = jax.random.permutation(jax.random.fold_in(own, 3), count)
    donor, taker = mixed[0:count // 2 * 2:2], mixed[1:count // 2 * 2:2]
    slack = jnp.minimum(sizes[donor] - 1, most - sizes[taker]) // 2
    slack = jnp.where((donor == order[0]) | (taker == order[0]) | (sizes[taker] == 0), 0, jnp.maximum(slack, 0))
    passed = jax.random.randint(jax.random.fold_in(own, 4), (count // 2,), 0, 1 << 20) % (slack + 1)
    sizes = sizes.at[donor].add(-passed).at[taker].add(passed)
    labels = jnp.searchsorted(jnp.cumsum(sizes), jnp.arange(rows * top), side="right").astype(jnp.int32)
    grid = labels.reshape(top, rows).T
    grid = grid[jax.random.permutation(jax.random.fold_in(own, 1), rows)]
    turn = jax.random.randint(jax.random.fold_in(own, 2), (rows, 1), 0, top)
    return jnp.take_along_axis(grid, (jnp.arange(top)[None, :] + turn) % top, axis=1)


def portions_of(count, total, limit, skew, full):
    weights = [(1 << 20) // math.isqrt(grade ** skew) + 1 for grade in range(1, count + 1)]
    largest = limit if full else min(limit, max(-(-total // count), total * weights[0] // sum(weights)))
    least = 1 if total - largest >= count - 1 else 0
    given, spare = [largest] + [least] * (count - 1), total - largest - least * (count - 1)
    while spare > 0:
        movable = [i for i in range(1, count) if given[i] < largest] or [i for i in range(1, count) if given[i] < limit]
        mass, remaining = sum([weights[i] for i in movable]), spare
        for i in movable:
            more = min(limit - given[i], max(1, remaining * weights[i] // mass), spare)
            given[i] = given[i] + more
            spare = spare - more
    return np.array(given)


def bell_draw(key, shape, width, most, shards=(), held_as=jnp.bfloat16):
    factor_of = block_scale(key, shape, shards, -0.22, 0.18) if shards else 1.0
    array = jax.random.normal(key, shape, jnp.float32) * width * factor_of
    return jnp.minimum(jnp.maximum(array, -most), most).astype(held_as)


def setup_inputs(seed: int = 0) -> dict:
    keys = jax.random.split(jax.random.key(seed), 23)
    residual_in = bell_draw(keys[0], (TOKENS, D), 1.0, 6.0, ((0, 32),))
    attention_gain = jnp.clip(1.0 + 0.1 * jax.random.normal(keys[1], (D,), jnp.float32), 0.5, 1.5).astype(jnp.bfloat16)
    query_weight = bell_draw(keys[2], (D, D), D ** -0.5, 0.125, ((0, 8), (1, 4)))
    query_bias = bell_draw(keys[3], (D,), 0.3, 1.5, ((0, 4),))
    key_weight = bell_draw(keys[4], (D, D), D ** -0.5, 0.125, ((0, 8), (1, 4)))
    key_bias = bell_draw(keys[5], (D,), 0.3, 1.5, ((0, 4),))
    value_weight = bell_draw(keys[6], (D, D), D ** -0.5, 0.125, ((0, 8), (1, 4)))
    value_bias = bell_draw(keys[7], (D,), 0.3, 1.5, ((0, 4),))
    output_weight = bell_draw(keys[8], (D, D), (D // 64) ** -0.5, 1.0, ((0, 4), (1, 8)))
    feedforward_gain = jnp.clip(1.0 + 0.1 * jax.random.normal(keys[9], (D,), jnp.float32), 0.5, 1.5).astype(jnp.bfloat16)
    router_weight = bell_draw(keys[10], (D, EXPERTS), (4 * D) ** -0.5, 0.0625)
    shared_logit_weight = bell_draw(keys[11], (D,), D ** -0.5, 0.125)
    shared_gate_weight = bell_draw(keys[12], (D, FFS), D ** -0.5, 0.125, ((0, 8), (1, 4)))
    shared_up_weight = bell_draw(keys[13], (D, FFS), D ** -0.5, 0.125, ((0, 8), (1, 4)))
    shared_down_weight = bell_draw(keys[14], (FFS, D), (FFS // 8) ** -0.5, 0.21875, ((0, 4), (1, 8)))
    expert_gate = bell_draw(keys[15], (EXPERTS, D, FFE), D ** -0.5, 0.125, ((0, 4), (1, 8)))
    expert_up = bell_draw(keys[16], (EXPERTS, D, FFE), D ** -0.5, 0.125, ((0, 4), (1, 8)))
    expert_down = bell_draw(keys[17], (EXPERTS, FFE, D), (FFE // 32) ** -0.5, 0.875, ((0, 4), (1, 8)))
    cotangent = bell_draw(keys[18], (TOKENS, D), 1.0, 6.0, ((0, 32),))
    expert_index_keys = jax.random.split(jax.random.fold_in(keys[19], 1), TOKENS // TOK_DEV)
    expert_index_turns = jax.random.permutation(jax.random.fold_in(keys[19], 3), TOKENS // TOK_DEV)
    expert_index = jax.vmap(lambda own, number: routed_block(jax.random.fold_in(keys[19], 2), own, number, TOK_DEV, EXPERTS, TOP, CAP, 1))(expert_index_keys, expert_index_turns).reshape((TOKENS, TOP))
    token_live = place_ends((jax.random.randint(keys[20], (TOKENS,), 0, 8) < 7).astype(jnp.int32), jax.random.fold_in(keys[20], 1), 0, 1)
    document_lengths = jax.vmap(lambda own: uneven_parts(own, DOCS, SEQ, SEQ // 2, 2))(jax.random.split(keys[21], SEQS)).reshape((SEQS, DOCS)).astype(jnp.int32)
    return dict(residual_in=residual_in, attention_gain=attention_gain, query_weight=query_weight, query_bias=query_bias, key_weight=key_weight, key_bias=key_bias, value_weight=value_weight, value_bias=value_bias, output_weight=output_weight, feedforward_gain=feedforward_gain, router_weight=router_weight, shared_logit_weight=shared_logit_weight, shared_gate_weight=shared_gate_weight, shared_up_weight=shared_up_weight, shared_down_weight=shared_down_weight, expert_gate=expert_gate, expert_up=expert_up, expert_down=expert_down, cotangent=cotangent, expert_index=expert_index, token_live=token_live, document_lengths=document_lengths)


@jax.custom_vjp
def low(v):
    return lax.optimization_barrier(v.astype(jnp.bfloat16)).astype(jnp.float32)

@jax.custom_vjp
def low_back(v):
    return v

def low_keep(v):
    return (low(v), None)

def low_pass(kept, grad):
    return (grad,)

def back_keep(v):
    return (v, None)

def back_low(kept, grad):
    return (low(grad),)
low.defvjp(low_keep, low_pass)
low_back.defvjp(back_keep, back_low)
EPS = 1e-06
ROPE_BASE = 1000000.0
MASKED = -1e+30
HIGH = lax.Precision.HIGHEST

def matmul(left, right):
    return jnp.dot(left, right, precision=HIGH)

def rms_norm(values, gain):
    scale = lax.rsqrt(lax.optimization_barrier(jnp.mean(values * values, axis=-1, keepdims=True)) + EPS)
    return values * scale * gain

def doc_layout(document_lengths, count):
    index = jnp.arange(count, dtype=jnp.int32)
    seq_of = (index // SEQ).astype(jnp.int32)
    place = (index % SEQ).astype(jnp.int32)
    lengths = document_lengths[seq_of]
    ends = jnp.cumsum(lengths, axis=1).astype(jnp.int32)
    doc = lax.optimization_barrier(jnp.sum((ends <= place[:, None]).astype(jnp.int32), axis=1)).astype(jnp.int32)
    earlier = jnp.arange(DOCS, dtype=jnp.int32)[None, :] < doc[:, None]
    before = lax.optimization_barrier(jnp.sum(jnp.where(earlier, lengths, 0), axis=1)).astype(jnp.int32)
    return ((seq_of * DOCS + doc).astype(jnp.int32), (place - before).astype(jnp.int32))

def rope(values, position):
    half = HDIM // 2
    freq = ROPE_BASE ** (-(jnp.arange(half, dtype=jnp.float32) * 2.0 / HDIM))
    angle = position.astype(jnp.float32)[:, None] * freq[None, :]
    cosine = jnp.cos(angle)[:, None, :]
    sine = jnp.sin(angle)[:, None, :]
    first = values[..., :half]
    second = values[..., half:]
    return jnp.concatenate([first * cosine - second * sine, second * cosine + first * sine], axis=-1)

def attention(query, key, value, docid):
    total = query.shape[0]
    block = math.gcd(512, total)
    reach = -(-WINDOW // block) * block
    key_pad = jnp.pad(key, ((reach, 0), (0, 0), (0, 0)))
    value_pad = jnp.pad(value, ((reach, 0), (0, 0), (0, 0)))
    doc_pad = jnp.concatenate([jnp.full((reach,), -1, dtype=jnp.int32), docid.astype(jnp.int32)])
    scale = HDIM ** (-0.5)

    def one_block(start):
        query_block = lax.dynamic_slice_in_dim(query, start, block, 0)
        key_block = lax.dynamic_slice_in_dim(key_pad, start, reach + block, 0)
        value_block = lax.dynamic_slice_in_dim(value_pad, start, reach + block, 0)
        query_doc = lax.dynamic_slice_in_dim(docid.astype(jnp.int32), start, block, 0)
        key_doc = lax.dynamic_slice_in_dim(doc_pad, start, reach + block, 0)
        query_place = start + jnp.arange(block, dtype=jnp.int32)
        key_place = start - reach + jnp.arange(reach + block, dtype=jnp.int32)
        distance = query_place[:, None] - key_place[None, :]
        allowed = (distance >= 0) & (distance < WINDOW) & (query_doc[:, None] == key_doc[None, :])
        scores = low_back(jnp.einsum('qhd,khd->hqk', query_block, key_block, precision=HIGH) * scale)
        scores = jnp.where(allowed[None, :, :], scores, MASKED)
        top = lax.optimization_barrier(jnp.max(scores, axis=-1, keepdims=True))
        weights = jnp.exp(scores - top)
        weights = weights / lax.optimization_barrier(jnp.sum(weights, axis=-1, keepdims=True))
        return jnp.einsum('hqk,khd->qhd', low(weights), value_block, precision=HIGH)
    starts = jnp.arange(0, total, block, dtype=jnp.int32)
    blocks = lax.map(jax.checkpoint(one_block), starts)
    return blocks.reshape(total, HEADS, HDIM)

def layer(params, chosen, docid, position):
    hidden_in, attention_gain, query_weight, query_bias, key_weight, key_bias, value_weight, value_bias, output_weight, feedforward_gain, router_weight, shared_logit_weight, shared_gate_weight, shared_up_weight, shared_down_weight, expert_gate, expert_up, expert_down = params
    count = hidden_in.shape[0]
    normed_one = low(rms_norm(hidden_in, attention_gain))
    query_lin = low_back(matmul(normed_one, query_weight) + query_bias)
    key_lin = low_back(matmul(normed_one, key_weight) + key_bias)
    value_lin = low_back(matmul(normed_one, value_weight) + value_bias)
    query = low(rope(query_lin.reshape(count, HEADS, HDIM), position))
    key = low(rope(key_lin.reshape(count, HEADS, HDIM), position))
    value = low(value_lin).reshape(count, HEADS, HDIM)
    attended = low(low_back(attention(query, key, value, docid).reshape(count, D)))
    mixed = hidden_in + low_back(matmul(attended, output_weight))
    normed_two = low(rms_norm(mixed, feedforward_gain))
    router_probs = jax.nn.softmax(matmul(normed_two, router_weight), axis=-1)
    gate_of = lax.optimization_barrier(jnp.sum(chosen * router_probs[:, None, :], axis=1))
    routed = jnp.zeros_like(mixed)
    for expert in range(EXPERTS):
        expert_rows = low_back(normed_two)
        gate_pre = low_back(matmul(expert_rows, expert_gate[expert]))
        up_pre = low_back(matmul(expert_rows, expert_up[expert]))
        active = low(jax.nn.silu(gate_pre) * up_pre)
        result = low(low_back(matmul(active, expert_down[expert])))
        routed = routed + gate_of[:, expert:expert + 1] * result
    shared_gate_pre = low_back(matmul(normed_two, shared_gate_weight))
    shared_up_pre = low_back(matmul(normed_two, shared_up_weight))
    shared_active = low(jax.nn.silu(shared_gate_pre) * shared_up_pre)
    shared_out = low_back(matmul(shared_active, shared_down_weight))
    shared_scale = jax.nn.sigmoid(matmul(normed_two, shared_logit_weight[:, None]))
    return mixed + routed + shared_scale * shared_out

def reference(residual_in, attention_gain, query_weight, query_bias, key_weight, key_bias, value_weight, value_bias, output_weight, feedforward_gain, router_weight, shared_logit_weight, shared_gate_weight, shared_up_weight, shared_down_weight, expert_gate, expert_up, expert_down, cotangent, expert_index, token_live, document_lengths):
    count = residual_in.shape[0]
    docid, position = doc_layout(document_lengths, count)
    chosen = ((expert_index[:, :, None] == jnp.arange(EXPERTS, dtype=jnp.int32)[None, None, :]) & (token_live[:, None, None] > 0)).astype(jnp.float32)
    floats = tuple((item.astype(jnp.float32) for item in (residual_in, attention_gain, query_weight, query_bias, key_weight, key_bias, value_weight, value_bias, output_weight, feedforward_gain, router_weight, shared_logit_weight, shared_gate_weight, shared_up_weight, shared_down_weight, expert_gate, expert_up, expert_down)))

    def forward(*params):
        return layer(params, chosen, docid, position)
    layer_out, pull = jax.vjp(forward, *floats)
    grads = pull(cotangent.astype(jnp.float32))
    return (layer_out.astype(jnp.bfloat16), grads[0], grads[1], grads[2], grads[3], grads[4], grads[5], grads[6], grads[7], grads[8], grads[9], grads[10], grads[11], grads[12], grads[13], grads[14], grads[15], grads[16], grads[17])
```

```python
import jax
import jax.numpy as jnp
from jax import lax
from jax.sharding import PartitionSpec as P

HDIM = 128
SEQS = 2
DOCS = 4
WINDOW = 1024
EPS = 1e-06
ROPE_BASE = 1000000.0
MASKED = -1e30
F32 = jnp.float32
BF16 = jnp.bfloat16


def dot(left, right):
    return jnp.dot(left, right, preferred_element_type=F32)


def dot_last(left, right):
    return lax.dot_general(left, right, (((1,), (1,)), ((), ())), preferred_element_type=F32)


def dot_first(left, right):
    return lax.dot_general(left, right, (((0,), (0,)), ((), ())), preferred_element_type=F32)


def across(block, mask):
    count = lax.axis_size("grp")
    return lax.ppermute(block, "grp", [(i, i ^ mask) for i in range(count)])


def quad_bits():
    return [1 << b for b in range((lax.axis_size("grp") // 2).bit_length() - 1)]


def flip_columns(values, quad):
    quads = lax.axis_size("grp") // 2
    axis = values.ndim - 1
    block = values.shape[axis] // quads
    return jnp.concatenate(
        [
            lax.dynamic_slice_in_dim(values, (quad ^ key) * block, block, axis)
            for key in range(quads)
        ],
        axis=axis,
    )


def gather_quads(pieces, order):
    pieces = dict(pieces)
    for bit in order:
        for key, piece in list(pieces.items()):
            pieces[key | bit] = across(piece, 2 * bit)
    return pieces


def reduce_quads(pieces, order):
    pieces = {key: piece.astype(BF16) for key, piece in pieces.items()}
    for bit in order:
        for key in [key for key in pieces if key & bit]:
            arrived = across(pieces.pop(key), 2 * bit)
            kept = pieces[key ^ bit]
            pieces[key ^ bit] = (kept.astype(F32) + arrived.astype(F32)).astype(BF16)
    return pieces


def together(*values):
    return lax.optimization_barrier(values)


def sum_everywhere(values, masks_grp, masks_ep):
    for mask in masks_grp:
        values = values + across(values, mask)
    count = lax.axis_size("ep")
    for mask in masks_ep:
        values = values + lax.ppermute(values, "ep", [(i, i ^ mask) for i in range(count)])
    return values


def in_order(pieces, axis):
    return jnp.concatenate([pieces[key] for key in sorted(pieces)], axis=axis)


def place_quads(pieces, quad, axis):
    size = pieces[0].shape[axis]
    shape = list(pieces[0].shape)
    shape[axis] = size * len(pieces)
    whole = jnp.zeros(shape, pieces[0].dtype)
    for key in sorted(pieces):
        whole = lax.dynamic_update_slice_in_dim(whole, pieces[key], (quad ^ key) * size, axis)
    return whole


def take_quads(whole, quad, quads, axis):
    size = whole.shape[axis] // quads
    return {
        key: lax.dynamic_slice_in_dim(whole, (quad ^ key) * size, size, axis)
        for key in range(quads)
    }


def merge_core(kept, arrived, core, axis):
    first = jnp.where(core == 0, kept, arrived)
    second = jnp.where(core == 0, arrived, kept)
    return jnp.concatenate([first, second], axis=axis)


def split_core(values, core, axis):
    half = values.shape[axis] // 2
    first = lax.slice_in_dim(values, 0, half, axis=axis)
    second = lax.slice_in_dim(values, half, 2 * half, axis=axis)
    return jnp.where(core == 0, first, second), jnp.where(core == 0, second, first)


def gather_rows(values):
    own = lax.all_gather(values, "ep", axis=0, tiled=True)
    return jnp.concatenate([own, across(own, 1)], axis=0)


def spread_rows(values):
    half = values.shape[0] // 2
    arrived = across(values[half:], 1)
    mine = (values[:half].astype(F32) + arrived.astype(F32)).astype(BF16)
    return lax.psum_scatter(mine, "ep", scatter_dimension=0, tiled=True).astype(F32)


def norm_scale(values):
    return lax.rsqrt(jnp.mean(values * values, axis=-1, keepdims=True) + EPS)


def norm_backward(grad_normed, unit, scale, gain):
    grad_unit = grad_normed * gain
    inner = jnp.mean(grad_unit * unit, axis=-1, keepdims=True)
    return scale * (grad_unit - unit * inner), jnp.sum(grad_normed * unit, axis=0)


def swish_slope(values):
    sigma = jax.nn.sigmoid(values)
    return sigma * (1.0 + values * (1.0 - sigma))


def doc_layout(document_lengths, seq_len, index):
    valid = index >= 0
    safe = jnp.maximum(index, 0)
    seq_of = safe // seq_len
    place = safe % seq_len
    seq_count = document_lengths.shape[0]
    picker = (seq_of[:, None] == jnp.arange(seq_count, dtype=jnp.int32)[None, :]).astype(jnp.int32)
    lengths = jnp.sum(picker[:, :, None] * document_lengths[None, :, :], axis=1)
    ends = jnp.cumsum(lengths, axis=1)
    doc = jnp.sum((ends <= place[:, None]).astype(jnp.int32), axis=1)
    earlier = jnp.arange(DOCS, dtype=jnp.int32)[None, :] < doc[:, None]
    before = jnp.sum(jnp.where(earlier, lengths, 0), axis=1)
    return jnp.where(valid, seq_of * DOCS + doc, -1), place - before


def rope_tables(position):
    half = HDIM // 2
    freq = ROPE_BASE ** (-(jnp.arange(half, dtype=F32) * 2.0 / HDIM))
    angle = position.astype(F32)[:, None] * freq[None, :]
    return jnp.cos(angle)[:, None, :], jnp.sin(angle)[:, None, :]


def rotate(values, cosine, sine):
    half = values.shape[-1] // 2
    first, second = values[..., :half], values[..., half:]
    return jnp.concatenate(
        [first * cosine - second * sine, second * cosine + first * sine], axis=-1
    )


def unrotate(grads, cosine, sine):
    return rotate(grads, cosine, -sine)


def masked_scores(query, keys_all, allowed):
    raw = jnp.einsum("qhd,khd->hqk", query, keys_all, preferred_element_type=F32) * HDIM ** (-0.5)
    return jnp.where(allowed[None, :, :], raw, MASKED)


def two_parts(values):
    high = values.astype(BF16)
    return high, (values - high.astype(F32)).astype(BF16)


def local(
    residual_in,
    attention_gain,
    query_weight,
    query_bias,
    key_weight,
    key_bias,
    value_weight,
    value_bias,
    output_weight,
    feedforward_gain,
    router_weight,
    shared_logit_weight,
    shared_gate_weight,
    shared_up_weight,
    shared_down_weight,
    expert_gate,
    expert_up,
    expert_down,
    cotangent,
    expert_index,
    token_live,
    document_lengths,
):
    ep_count = lax.axis_size("ep")
    grp_count = lax.axis_size("grp")
    quads = grp_count // 2
    rows_dev, width = residual_in.shape
    group_rows = rows_dev * ep_count
    pair_rows = 2 * group_rows
    seq_len = group_rows * grp_count // SEQS
    expert_count = expert_gate.shape[0] * ep_count
    ffe = expert_gate.shape[2]
    ffs_half = shared_gate_weight.shape[1] // 2
    grp = lax.axis_index("grp")
    ep = lax.axis_index("ep")
    core = grp % 2
    quad = grp // 2
    back = -(-WINDOW // pair_rows)
    heads = query_weight.shape[1] // HDIM // 2
    head_width = heads * HDIM
    up_order = quad_bits()
    down_order = up_order[::-1]

    hidden_in = residual_in.astype(F32)
    grad_out = cotangent.astype(F32)
    gain_one = attention_gain.astype(F32)
    gain_two = feedforward_gain.astype(F32)
    router_all = jnp.concatenate([router_weight, shared_logit_weight[:, None]], axis=1)
    router_flipped = flip_columns(router_all.T, quad).T

    scale_one = norm_scale(hidden_in)
    unit_one = hidden_in * scale_one
    normed_one = (unit_one * gain_one).astype(BF16)
    rows_one = gather_rows(flip_columns(normed_one, quad))

    cut = len(up_order) // 2
    up_one, up_two = up_order[:cut], up_order[cut:]
    down_one, down_two = down_order[: len(down_order) - cut], down_order[len(down_order) - cut :]
    qk_keep, qk_other = zip(
        *[split_core(weight, core, 1) for weight in (query_weight, key_weight, value_weight)]
    )
    qkv_keep, qkv_other = jnp.concatenate(qk_keep, 1), jnp.concatenate(qk_other, 1)
    qkv_block = merge_core(qkv_keep, across(qkv_other, 1), core, 0)
    qkv_cut = qkv_block.shape[1] // 2
    qkv_a = gather_quads({0: qkv_block[:, :qkv_cut]}, up_order)
    qkv_b = gather_quads({0: qkv_block[:, qkv_cut:]}, down_order)
    qkv_full = jnp.concatenate([in_order(qkv_a, 0), in_order(qkv_b, 0)], axis=1)

    o_keep, o_other = split_core(output_weight, core, 0)
    o_block = merge_core(o_keep, across(o_other, 1), core, 1)
    sg_keep, sg_other = split_core(shared_gate_weight, core, 1)
    su_keep, su_other = split_core(shared_up_weight, core, 1)
    gu_keep = jnp.concatenate([sg_keep, su_keep], axis=1)
    gu_other = jnp.concatenate([sg_other, su_other], axis=1)
    gu_block = merge_core(gu_keep, across(gu_other, 1), core, 0)
    sd_keep, sd_other = split_core(shared_down_weight, core, 0)
    sd_block = merge_core(sd_keep, across(sd_other, 1), core, 1)

    def expert_block(weight):
        keep, other = split_core(weight, core, 0)
        return merge_core(keep[0], across(other[0], 1), core, 0)

    eg_block, eu_block, ed_block = [
        expert_block(weight) for weight in (expert_gate, expert_up, expert_down)
    ]
    ed_cut = width // 2
    eda_block, edb_block = ed_block[:, :ed_cut], ed_block[:, ed_cut:]

    o_some = gather_quads({0: o_block}, down_one)
    gu_some = gather_quads({0: gu_block}, up_one)
    sd_some = gather_quads({0: sd_block}, down_one)
    (
        rows_one, qkv_full, o_some, gu_some, sd_some, eg_block, eu_block, eda_block, edb_block,
        cot_low,
    ) = together(
        rows_one, qkv_full, o_some, gu_some, sd_some, eg_block, eu_block, eda_block, edb_block,
        cotangent,
    )

    experts = jnp.arange(expert_count, dtype=jnp.int32)
    chosen = (
        (expert_index[:, :, None] == experts[None, None, :]) & (token_live[:, None, None] > 0)
    ).any(axis=1)
    chosen = chosen.astype(BF16)
    cot_rows = gather_rows(
        jnp.concatenate([cot_low, jnp.pad(chosen, ((0, 0), (0, 128 - expert_count)))], axis=1)
    )
    chosen = chosen.astype(F32)

    o_pieces = gather_quads(o_some, down_two)
    gu_pieces = gather_quads(gu_some, up_two)
    sd_pieces = gather_quads(sd_some, down_two)
    bias = jnp.concatenate(
        [split_core(b, core, 0)[0] for b in (query_bias, key_bias, value_bias)]
    ).astype(F32)
    lin = dot(rows_one, qkv_full) + bias[None, :]

    def pair_places(steps):
        count = jnp.arange(group_rows, dtype=jnp.int32)
        first = (grp - 2 * steps) * group_rows
        other = ((grp ^ 1) - 2 * steps) * group_rows
        return jnp.concatenate([first + count, other + count])

    query_place = pair_places(0)
    key_place = jnp.concatenate([pair_places(step) for step in range(back, -1, -1)])
    query_doc, query_position = doc_layout(document_lengths, seq_len, query_place)
    key_doc, _ = doc_layout(document_lengths, seq_len, key_place)
    cosine, sine = rope_tables(query_position)
    query, key, value = [
        lin[:, part * head_width : (part + 1) * head_width].reshape(pair_rows, heads, HDIM)
        for part in range(3)
    ]
    query = rotate(query, cosine, sine).astype(BF16)
    key = rotate(key, cosine, sine).astype(BF16)
    value = value.astype(BF16)

    seq_groups = grp_count // SEQS

    def shifted(block, steps):
        route = [
            (i, i + 2 * steps)
            for i in range(grp_count)
            if 0 <= i + 2 * steps < grp_count and i // seq_groups == (i + 2 * steps) // seq_groups
        ]
        return lax.ppermute(block, "grp", route)

    key_value = jnp.concatenate([key, value], axis=1)
    key_value_all = jnp.concatenate(
        [shifted(key_value, step) for step in range(back, 0, -1)] + [key_value], axis=0
    )
    keys_all, values_all = key_value_all[:, :heads], key_value_all[:, heads:]
    distance = query_place[:, None] - key_place[None, :]
    allowed = (distance >= 0) & (distance < WINDOW) & (query_doc[:, None] == key_doc[None, :])
    scores = masked_scores(query, keys_all, allowed)
    top = jnp.max(scores, axis=-1, keepdims=True)
    weights = jnp.exp(scores - top)
    total = jnp.sum(weights, axis=-1, keepdims=True)
    log_total = top + jnp.log(total)
    probs = weights / total
    attended = jnp.einsum(
        "hqk,khd->qhd", probs.astype(BF16), values_all, preferred_element_type=F32
    )
    attended = attended.astype(BF16).reshape(pair_rows, head_width)
    (
        attended, o_pieces, gu_pieces, sd_pieces, eg_block, eu_block, eda_block, edb_block, cot_rows,
    ) = together(
        attended, o_pieces, gu_pieces, sd_pieces, eg_block, eu_block, eda_block, edb_block, cot_rows,
    )
    o_full = place_quads(o_pieces, quad, 1)
    gu_full = in_order(gu_pieces, 0)
    sd_full = place_quads(sd_pieces, quad, 1)
    cot_rows, chosen_rows = cot_rows[:, :width], cot_rows[:, width : width + expert_count]
    chosen_rows = chosen_rows.astype(F32)
    eg_some = gather_quads({0: eg_block}, up_one)
    eu_some = gather_quads({0: eu_block}, down_one)
    eda_some = gather_quads({0: eda_block}, up_one)
    edb_some = gather_quads({0: edb_block}, down_one)
    mixed = hidden_in + spread_rows(dot(attended, o_full).astype(BF16))
    mixed, eg_some, eu_some, eda_some, edb_some = together(
        mixed, eg_some, eu_some, eda_some, edb_some
    )
    eg_pieces = gather_quads(eg_some, up_two)
    eu_pieces = gather_quads(eu_some, down_two)

    scale_two = norm_scale(mixed)
    unit_two = mixed * scale_two
    normed_two = (unit_two * gain_two).astype(BF16)
    rows_two = gather_rows(flip_columns(normed_two, quad))
    rows_two, eg_pieces, eu_pieces, eda_some, edb_some = together(
        rows_two, eg_pieces, eu_pieces, eda_some, edb_some
    )
    eg_full = in_order(eg_pieces, 0)
    eu_full = in_order(eu_pieces, 0)
    ed_full = jnp.concatenate(
        [
            place_quads(gather_quads(eda_some, up_two), quad, 0),
            place_quads(gather_quads(edb_some, down_two), quad, 0),
        ],
        axis=1,
    )

    def router(rows, weight):
        logits = dot(rows, weight)
        return jax.nn.softmax(logits[:, :expert_count], axis=-1), jax.nn.sigmoid(
            logits[:, expert_count:]
        )

    probs_rows, shared_scale_rows = router(rows_two, router_flipped)
    router_probs, shared_scale = router(normed_two, router_all)
    mine = (experts == ep * 2 + core).astype(F32)[None, :]
    gate = jnp.sum(probs_rows * chosen_rows * mine, axis=1, keepdims=True)

    gu_pre = dot(rows_two, gu_full)
    sg_pre, su_pre = gu_pre[:, :ffs_half], gu_pre[:, ffs_half:]
    shared_active = (jax.nn.silu(sg_pre) * su_pre).astype(BF16)
    shared_part = dot(shared_active, sd_full)
    cot_float = cot_rows.astype(F32)
    grad_shared_out = (shared_scale_rows * cot_float).astype(BF16)
    shared_dot = jnp.sum(cot_float * shared_part, axis=1, keepdims=True)
    grad_shared_active = dot_last(grad_shared_out, sd_full)
    grad_gu = jnp.concatenate(
        [
            (grad_shared_active * su_pre * swish_slope(sg_pre)).astype(BF16),
            (grad_shared_active * jax.nn.silu(sg_pre)).astype(BF16),
        ],
        axis=1,
    )
    grad_rows_shared = dot_last(grad_gu, gu_full)

    gate_pre = dot(rows_two, eg_full)
    up_pre = dot(rows_two, eu_full)
    active = (jax.nn.silu(gate_pre) * up_pre).astype(BF16)
    result = dot(active, ed_full).astype(BF16).astype(F32)
    grad_gate = jnp.sum(cot_float * result, axis=1, keepdims=True)
    forward_part = gate * result + shared_scale_rows * shared_part
    grad_result = (gate * cot_float).astype(BF16)
    grad_active = dot_last(grad_result, ed_full)
    grad_gate_pre = (grad_active * up_pre * swish_slope(gate_pre)).astype(BF16)
    grad_up_pre = (grad_active * jax.nn.silu(gate_pre)).astype(BF16)
    grad_rows = (dot_last(grad_gate_pre, eg_full) + dot_last(grad_up_pre, eu_full)).astype(BF16)
    grad_part = (grad_rows.astype(F32) + grad_rows_shared).astype(BF16)
    extra = jnp.concatenate(
        [part * mine.astype(BF16) for value in (grad_gate, shared_dot) for part in two_parts(value)],
        axis=1,
    )
    extra = jnp.pad(extra, ((0, 0), (0, 128 - extra.shape[1])))
    block = width // quads

    def row_grads(rows, grads):
        return {k: dot_first(rows[:, k * block : (k + 1) * block], grads) for k in range(quads)}

    def column_grads(acts, grads):
        return {k: dot_first(acts, part) for k, part in take_quads(grads, quad, quads, 1).items()}

    sd_grad = reduce_quads(column_grads(shared_active, grad_shared_out), down_one)
    gu_grad = reduce_quads(row_grads(rows_two, grad_gu), up_one)
    ed_grad = take_quads(dot_first(active, grad_result).astype(BF16), quad, quads, 0)
    eda_grad = reduce_quads({k: v[:, :ed_cut] for k, v in ed_grad.items()}, up_one)
    edb_grad = reduce_quads({k: v[:, ed_cut:] for k, v in ed_grad.items()}, down_one)
    spread = spread_rows(jnp.concatenate([grad_part, extra], axis=1))
    eg_grad = row_grads(rows_two, grad_gate_pre)
    eu_grad = row_grads(rows_two, grad_up_pre)
    spread, sd_grad, gu_grad, eda_grad, edb_grad, eg_grad, eu_grad, forward_part = together(
        spread, sd_grad, gu_grad, eda_grad, edb_grad,
        {k: v.astype(BF16) for k, v in eg_grad.items()},
        {k: v.astype(BF16) for k, v in eu_grad.items()},
        forward_part.astype(BF16),
    )
    grad_normed_two = flip_columns(spread[:, :width], quad)
    side = spread[:, width : width + 4 * expert_count].reshape(rows_dev, 4, expert_count)
    grad_gate_own = side[:, 0] + side[:, 1]
    shared_dot_own = jnp.sum(side[:, 2] + side[:, 3], axis=1, keepdims=True)

    grad_logit = shared_dot_own * shared_scale * (1.0 - shared_scale)
    grad_probs = grad_gate_own * chosen
    grad_logits = router_probs * (
        grad_probs - jnp.sum(router_probs * grad_probs, axis=-1, keepdims=True)
    )
    grad_router = jnp.concatenate([grad_logits, grad_logit], axis=1)
    router_grad = dot_first(normed_two.astype(F32), grad_router)
    grad_normed_two = grad_normed_two + dot_last(grad_router, router_all.astype(F32))
    grad_norm_part, ff_gain_grad = norm_backward(grad_normed_two, unit_two, scale_two, gain_two)
    grad_mixed = grad_out + grad_norm_part
    grad_branch = gather_rows(grad_mixed.astype(BF16))
    eg_grad = reduce_quads(eg_grad, up_one)
    eu_grad = reduce_quads(eu_grad, down_one)
    ep_masks = [1 << b for b in range(ep_count.bit_length() - 1)]
    grp_masks = [1 << b for b in range(grp_count.bit_length() - 1)]
    grad_branch, eg_grad, eu_grad, sd_grad, gu_grad, eda_grad, edb_grad, forward_part = together(
        grad_branch, eg_grad, eu_grad, sd_grad, gu_grad, eda_grad, edb_grad, forward_part
    )
    layer_sum = spread_rows(forward_part)
    layer_out = (mixed + layer_sum).astype(BF16)
    sd_grad = reduce_quads(sd_grad, down_two)[0]
    gu_grad = reduce_quads(gu_grad, up_two)[0]
    ed_grad = jnp.concatenate(
        [reduce_quads(eda_grad, up_two)[0], reduce_quads(edb_grad, down_two)[0]], axis=1
    )
    early = sum_everywhere(
        jnp.concatenate([ff_gain_grad[None], router_grad.T], axis=0), grp_masks, ep_masks
    )
    ff_gain_grad, router_grad = early[0], early[1:]
    o_grad = {k: v.astype(BF16) for k, v in column_grads(attended, grad_branch).items()}

    grad_attended = dot_last(grad_branch, o_full).astype(BF16).reshape(pair_rows, heads, HDIM)
    scores_again = masked_scores(query, keys_all, allowed)
    probs_again = jnp.exp(scores_again - log_total)
    grad_probs_att = jnp.einsum(
        "qhd,khd->hqk", grad_attended, values_all, preferred_element_type=F32
    )
    inner = jnp.sum(probs_again * grad_probs_att, axis=-1, keepdims=True)
    grad_scores = (probs_again * (grad_probs_att - inner)).astype(BF16)
    grad_query = jnp.einsum(
        "hqk,khd->qhd", grad_scores, keys_all, preferred_element_type=F32
    ) * HDIM ** (-0.5)
    grad_keys_all = jnp.einsum(
        "hqk,qhd->khd", grad_scores, query, preferred_element_type=F32
    ) * HDIM ** (-0.5)
    grad_values_all = jnp.einsum(
        "hqk,qhd->khd", probs_again.astype(BF16), grad_attended, preferred_element_type=F32
    )
    grad_kv_all = jnp.concatenate([grad_keys_all, grad_values_all], axis=1)
    (
        grad_kv_all, layer_out, sd_grad, gu_grad, ed_grad, ff_gain_grad, router_grad, eg_grad,
        eu_grad, o_grad,
    ) = together(
        grad_kv_all, layer_out, sd_grad, gu_grad, ed_grad, ff_gain_grad, router_grad, eg_grad,
        eu_grad, o_grad,
    )
    grad_kv = grad_kv_all[back * pair_rows :]
    for step in range(1, back + 1):
        first = (back - step) * pair_rows
        sent = grad_kv_all[first : first + pair_rows].astype(BF16)
        grad_kv = grad_kv + shifted(sent, -step).astype(F32)
    grad_lin = jnp.concatenate(
        [
            unrotate(grad_query, cosine, sine),
            unrotate(grad_kv[:, :heads], cosine, sine),
            grad_kv[:, heads:],
        ],
        axis=1,
    )
    grad_lin = grad_lin.astype(BF16).reshape(pair_rows, 3 * head_width)
    partial = dot_last(grad_lin, qkv_full)
    gain_rows = flip_columns(gain_one, quad)
    att_gain_part = jnp.sum(partial * rows_one.astype(F32), axis=0) / gain_rows
    bias_part = jnp.sum(grad_lin.astype(F32), axis=0)
    late = jnp.concatenate([flip_columns(att_gain_part, quad), bias_part])
    late = sum_everywhere(late, grp_masks[1:], [])
    att_gain_grad = sum_everywhere(late[:width], grp_masks[:1], ep_masks)
    bias_mine = merge_core(
        late[width:].reshape(3, head_width),
        across(late[width:], 1).reshape(3, head_width),
        core,
        1,
    )
    grad_normed_one = flip_columns(spread_rows(partial.astype(BF16)), quad)
    grad_norm_one, _ = norm_backward(grad_normed_one, unit_one, scale_one, gain_one)
    input_grad = grad_mixed + grad_norm_one

    def back_to_cores(summed, cut_axis, join_axis):
        keep, other = split_core(summed, core, cut_axis)
        return merge_core(keep, across(other, 1), core, join_axis).astype(F32)

    def back_to_experts(summed):
        keep, other = split_core(summed, core, 0)
        arrived = across(other, 1)
        return jnp.stack(
            [jnp.where(core == 0, keep, arrived), jnp.where(core == 0, arrived, keep)]
        ).astype(F32)

    eg_grad = reduce_quads(eg_grad, up_two)[0]
    eu_grad = reduce_quads(eu_grad, down_two)[0]
    o_grad = reduce_quads(o_grad, down_order)[0]
    qkv_a_grad = reduce_quads(row_grads(rows_one, grad_lin[:, :qkv_cut]), up_order)[0]
    qkv_b_grad = reduce_quads(row_grads(rows_one, grad_lin[:, qkv_cut:]), down_order)[0]
    qkv_grad = jnp.concatenate([qkv_a_grad, qkv_b_grad], axis=1)
    q_grad, k_grad, v_grad = [
        back_to_cores(qkv_grad[:, part * head_width : (part + 1) * head_width], 0, 1)
        for part in range(3)
    ]
    return (
        layer_out,
        input_grad,
        att_gain_grad,
        q_grad,
        bias_mine[0],
        k_grad,
        bias_mine[1],
        v_grad,
        bias_mine[2],
        back_to_cores(o_grad, 1, 0),
        ff_gain_grad,
        router_grad[:expert_count].T,
        router_grad[expert_count],
        back_to_cores(gu_grad[:, :ffs_half], 0, 1),
        back_to_cores(gu_grad[:, ffs_half:], 0, 1),
        back_to_cores(sd_grad, 1, 0),
        back_to_experts(eg_grad),
        back_to_experts(eu_grad),
        back_to_experts(ed_grad),
    )


def solution(mesh):
    tokens = P(("grp", "ep"), None)
    rows, columns, experts = P("grp", "ep"), P("ep", "grp"), P("ep", "grp", None)
    in_specs = (
        tokens, P(), rows, P("ep"), rows, P("ep"), rows, P("ep"), columns, P(), P(), P(),
        rows, rows, columns, experts, experts, experts, tokens, tokens, P(("grp", "ep")), P(),
    )
    out_specs = (
        tokens, tokens, P(), rows, P("ep"), rows, P("ep"), rows, P("ep"), columns, P(), P(), P(),
        rows, rows, columns, experts, experts, experts,
    )
    return jax.shard_map(local, mesh=mesh, in_specs=in_specs, out_specs=out_specs, check_vma=False)
```

```python
import functools

import jax
import jax.numpy as jnp
from jax import lax
from jax.experimental import pallas as pl
from jax.experimental.pallas import tpu as pltpu
from jax.sharding import PartitionSpec as P

HDIM = 128
SEQS = 2
DOCS = 4
WINDOW = 1024
EPS = 1e-06
ROPE_BASE = 1000000.0
MASKED = -1e30
F32 = jnp.float32
BF16 = jnp.bfloat16
TILE = 256
LANES = 128
MIB = 1 << 20


def dot(left, right):
    return jnp.dot(left, right, preferred_element_type=F32)


def dot_last(left, right):
    return lax.dot_general(left, right, (((1,), (1,)), ((), ())), preferred_element_type=F32)


def dot_first(left, right):
    return lax.dot_general(left, right, (((0,), (0,)), ((), ())), preferred_element_type=F32)


def across(block, mask):
    count = lax.axis_size("grp")
    return lax.ppermute(block, "grp", [(i, i ^ mask) for i in range(count)])


def quad_bits():
    return [1 << b for b in range((lax.axis_size("grp") // 2).bit_length() - 1)]


def flip_columns(values, quad):
    quads = lax.axis_size("grp") // 2
    axis = values.ndim - 1
    block = values.shape[axis] // quads
    return jnp.concatenate(
        [
            lax.dynamic_slice_in_dim(values, (quad ^ key) * block, block, axis)
            for key in range(quads)
        ],
        axis=axis,
    )


def gather_quads(pieces, order):
    pieces = dict(pieces)
    for bit in order:
        for key, piece in list(pieces.items()):
            pieces[key | bit] = across(piece, 2 * bit)
    return pieces


def send_quads(pieces, bit, keys):
    return {key: across(pieces[key], 2 * bit) for key in keys}


def add_quads(pieces, arrived, bit):
    return {
        key: (piece.astype(F32) + arrived[key | bit].astype(F32)).astype(BF16)
        for key, piece in pieces.items()
        if not key & bit
    }


def reduce_quads(pieces, order):
    for bit in order:
        arrived = send_quads(pieces, bit, [key for key in pieces if key & bit])
        pieces = add_quads(pieces, arrived, bit)
    return pieces


def together(*values):
    return lax.optimization_barrier(values)


def sum_everywhere(values, masks_grp, masks_ep):
    for mask in masks_grp:
        values = values + across(values, mask)
    count = lax.axis_size("ep")
    for mask in masks_ep:
        values = values + lax.ppermute(values, "ep", [(i, i ^ mask) for i in range(count)])
    return values


def gather_rest(pieces, order):
    found = {}
    for key, piece in pieces.items():
        if key:
            found.update({key | k: v for k, v in gather_quads({0: piece}, order).items()})
    return found


def listed(pieces):
    return [pieces[key] for key in sorted(pieces)]


def place_quads(pieces, quad, axis):
    size = pieces[0].shape[axis]
    shape = list(pieces[0].shape)
    shape[axis] = size * len(pieces)
    whole = jnp.zeros(shape, pieces[0].dtype)
    for key in sorted(pieces):
        whole = lax.dynamic_update_slice_in_dim(whole, pieces[key], (quad ^ key) * size, axis)
    return whole


def take_quads(whole, quad, quads, axis):
    size = whole.shape[axis] // quads
    return {
        key: lax.dynamic_slice_in_dim(whole, (quad ^ key) * size, size, axis)
        for key in range(quads)
    }


def merge_core(kept, arrived, core, axis):
    first = jnp.where(core == 0, kept, arrived)
    second = jnp.where(core == 0, arrived, kept)
    return jnp.concatenate([first, second], axis=axis)


def split_core(values, core, axis):
    half = values.shape[axis] // 2
    first = lax.slice_in_dim(values, 0, half, axis=axis)
    second = lax.slice_in_dim(values, half, 2 * half, axis=axis)
    return jnp.where(core == 0, first, second), jnp.where(core == 0, second, first)


def norm_scale(values):
    return lax.rsqrt(jnp.mean(values * values, axis=-1, keepdims=True) + EPS)


def norm_backward(grad_normed, unit, scale, gain):
    grad_unit = grad_normed * gain
    inner = jnp.mean(grad_unit * unit, axis=-1, keepdims=True)
    return scale * (grad_unit - unit * inner), jnp.sum(grad_normed * unit, axis=0)


def doc_layout(document_lengths, seq_len, index):
    valid = index >= 0
    safe = jnp.maximum(index, 0)
    seq_of = safe // seq_len
    place = safe % seq_len
    seq_count = document_lengths.shape[0]
    picker = (seq_of[:, None] == jnp.arange(seq_count, dtype=jnp.int32)[None, :]).astype(jnp.int32)
    lengths = jnp.sum(picker[:, :, None] * document_lengths[None, :, :], axis=1)
    ends = jnp.cumsum(lengths, axis=1)
    doc = jnp.sum((ends <= place[:, None]).astype(jnp.int32), axis=1)
    earlier = jnp.arange(DOCS, dtype=jnp.int32)[None, :] < doc[:, None]
    before = jnp.sum(jnp.where(earlier, lengths, 0), axis=1)
    return jnp.where(valid, seq_of * DOCS + doc, -1), place - before


def rope_tables(position):
    half = HDIM // 2
    freq = ROPE_BASE ** (-(jnp.arange(half, dtype=F32) * 2.0 / HDIM))
    angle = position.astype(F32)[:, None] * freq[None, :]
    cosine, sine = jnp.cos(angle), jnp.sin(angle)
    return jnp.concatenate([cosine, cosine], axis=1), jnp.concatenate([-sine, sine], axis=1)


def turn(values, cosine, sine):
    return values * cosine + pltpu.roll(values, HDIM // 2, 1) * sine


def call(kernel, grid, ins, outs, shapes, limit, flops, scratch=(), name=None):
    moved = 0
    for shape in shapes:
        moved += shape.size * shape.dtype.itemsize

    def run(*args):
        total = moved + sum(a.size * a.dtype.itemsize for a in args)
        return pl.pallas_call(
            kernel,
            grid=grid,
            in_specs=ins,
            out_specs=outs,
            out_shape=shapes,
            scratch_shapes=scratch,
            compiler_params=pltpu.CompilerParams(vmem_limit_bytes=limit * MIB),
            cost_estimate=pl.CostEstimate(
                flops=flops, bytes_accessed=total, transcendentals=0
            ),
            name=name,
        )(*args)

    return run


def whole(shape):
    return pl.BlockSpec(shape, lambda *_: (0,) * len(shape), pipeline_mode=pl.Buffered(1))


def rows_spec(columns, tile=TILE):
    return pl.BlockSpec((tile, columns), lambda i: (i, 0))


def shaped(rows, columns, dtype):
    return jax.ShapeDtypeStruct((rows, columns), dtype)


def sum_pieces(x, refs):
    block = x.shape[1] // len(refs)
    total = dot(x[:, :block], refs[0][...])
    for key in range(1, len(refs)):
        total = total + dot(x[:, key * block : (key + 1) * block], refs[key][...])
    return total


def project_kernel(heads, quads, x_ref, bias_ref, cos_ref, sin_ref, *rest):
    wa_refs, wb_refs, (q_ref, kv_ref) = rest[:quads], rest[quads : 2 * quads], rest[2 * quads :]
    x = x_ref[...]
    lin = jnp.concatenate([sum_pieces(x, wa_refs), sum_pieces(x, wb_refs)], axis=1) + bias_ref[...]
    cosine, sine = cos_ref[...], sin_ref[...]
    for head in range(3 * heads):
        part = lin[:, head * HDIM : (head + 1) * HDIM]
        if head < 2 * heads:
            part = turn(part, cosine, sine)
        if head < heads:
            q_ref[:, head * HDIM : (head + 1) * HDIM] = part.astype(BF16)
        else:
            kv_ref[:, (head - heads) * HDIM : (head - heads + 1) * HDIM] = part.astype(BF16)


def project(x, wa, wb, bias, cosine, sine, heads):
    rows, width = x.shape
    quads, (block, cut) = len(wa), wa[0].shape
    return call(
        functools.partial(project_kernel, heads, quads),
        (rows // TILE,),
        [rows_spec(width), whole((1, 2 * cut))]
        + [rows_spec(HDIM)] * 2
        + [whole((block, cut))] * (2 * quads),
        [rows_spec(heads * HDIM), rows_spec(2 * heads * HDIM)],
        [shaped(rows, heads * HDIM, BF16), shaped(rows, 2 * heads * HDIM, BF16)],
        32,
        4 * rows * width * cut,
        name="project",
    )(x, bias, cosine, sine, *wa, *wb)


def window_keys(before_refs, own_ref, place, pair_rows, step):
    parts = []
    start = step * TILE
    reach = -WINDOW + start
    for back, ref in enumerate(before_refs):
        first = -(len(before_refs) - back) * pair_rows
        low = max(reach - first, 0)
        if low < pair_rows:
            parts.append(ref[low:, place])
    parts.append(own_ref[max(reach, 0) : start + TILE, place])
    return jnp.concatenate(parts, axis=0) if len(parts) > 1 else parts[0]


def probabilities(query, keys, key_place, low, high, peak):
    scores = dot_last(query, keys) * HDIM ** (-0.5)
    scores = jnp.where((key_place >= low) & (key_place <= high), scores, MASKED)
    if peak is None:
        top = jnp.max(scores, axis=1, keepdims=True)
        weights = jnp.exp(scores - top)
        total = jnp.sum(weights, axis=1, keepdims=True)
        return weights / total, top + jnp.log(total)
    return jnp.exp(scores - peak), peak


def attend_kernel(back, pair_rows, heads, q_ref, *rest):
    before, (own_ref, place_ref, low_ref, high_ref, out_ref, log_ref) = rest[:back], rest[back:]
    for head in range(heads):
        cols = slice(head * HDIM, (head + 1) * HDIM)
        value_cols = slice((heads + head) * HDIM, (heads + head + 1) * HDIM)
        for step in range(pair_rows // TILE):
            rows = slice(step * TILE, (step + 1) * TILE)
            first = back * pair_rows - WINDOW + step * TILE
            places = place_ref[:, max(first, 0) : back * pair_rows + (step + 1) * TILE]
            keys = window_keys(before, own_ref, cols, pair_rows, step)
            values = window_keys(before, own_ref, value_cols, pair_rows, step)
            probs, logs = probabilities(
                q_ref[rows, cols], keys, places, low_ref[rows, :], high_ref[rows, :], None
            )
            out_ref[rows, cols] = dot(probs.astype(BF16), values).astype(BF16)
            log_ref[rows, cols] = jnp.broadcast_to(logs, (TILE, HDIM))


def attend(query, before, own, places, low, high):
    rows, columns = query.shape
    heads = columns // HDIM
    back = len(before)
    return call(
        functools.partial(attend_kernel, back, rows, heads),
        (),
        [pl.BlockSpec(memory_space=pltpu.VMEM)] * (5 + back),
        [pl.BlockSpec(memory_space=pltpu.VMEM)] * 2,
        [shaped(rows, columns, BF16), shaped(rows, columns, F32)],
        40,
        4 * rows * columns * (WINDOW + TILE),
        name="attend",
    )(query, *before, own, places, low, high)


def attend_back_kernel(back, pair_rows, heads, q_ref, grad_ref, log_ref, *rest):
    before = rest[:back]
    own_ref, place_ref, low_ref, high_ref, cos_ref, sin_ref = rest[back : back + 6]
    dq_ref, own_out = rest[back + 6 : back + 8]
    before_out = rest[back + 8 : 2 * back + 8]
    total_ref = rest[-1]
    total_ref[...] = jnp.zeros_like(total_ref)
    for head in range(heads):
        cols = slice(head * HDIM, (head + 1) * HDIM)
        value_cols = slice((heads + head) * HDIM, (heads + head + 1) * HDIM)
        for step in range(pair_rows // TILE):
            rows = slice(step * TILE, (step + 1) * TILE)
            first = max(back * pair_rows - WINDOW + step * TILE, 0)
            last = back * pair_rows + (step + 1) * TILE
            keys = window_keys(before, own_ref, cols, pair_rows, step)
            values = window_keys(before, own_ref, value_cols, pair_rows, step)
            query, grad = q_ref[rows, cols], grad_ref[rows, cols]
            peak = jnp.concatenate([log_ref[rows, cols]] * ((last - first) // HDIM), axis=1)
            probs, _ = probabilities(
                query, keys, place_ref[:, first:last], low_ref[rows, :], high_ref[rows, :], peak
            )
            grad_probs = dot_last(grad, values)
            inner = jnp.sum(probs * grad_probs, axis=1, keepdims=True)
            grad_scores = (probs * (grad_probs - inner)).astype(BF16)
            grad_query = dot(grad_scores, keys) * HDIM ** (-0.5)
            dq_ref[rows, cols] = turn(grad_query, cos_ref[rows, :], -sin_ref[rows, :]).astype(BF16)
            total_ref[first:last, cols] += dot_first(grad_scores, query) * HDIM ** (-0.5)
            total_ref[first:last, value_cols] += dot_first(probs.astype(BF16), grad)
    own_out[...] = total_ref[back * pair_rows :, :]
    for step in range(back):
        before_out[step][...] = total_ref[step * pair_rows : (step + 1) * pair_rows, :].astype(BF16)


def attend_back(query, grad, logs, before, own, places, low, high, cosine, sine):
    rows, columns = query.shape
    back = len(before)
    return call(
        functools.partial(attend_back_kernel, back, rows, columns // HDIM),
        (),
        [pl.BlockSpec(memory_space=pltpu.VMEM)] * (9 + back),
        [pl.BlockSpec(memory_space=pltpu.VMEM)] * (2 + back),
        [shaped(rows, columns, BF16), shaped(rows, 2 * columns, F32)]
        + [shaped(rows, 2 * columns, BF16)] * back,
        48,
        10 * rows * columns * (WINDOW + TILE),
        scratch=[pltpu.VMEM(((back + 1) * rows, 2 * columns), F32)],
        name="attend_back",
    )(query, grad, logs, *before, own, places, low, high, cosine, sine)


def collect_kernel(heads, back, quads, dq_ref, own_ref, cos_ref, sin_ref, x_ref, *rest):
    arrived, wa_refs, wb_refs = rest[:back], rest[back : back + quads], rest[back + quads : back + 2 * quads]
    out_ref, part_ref, gain_ref, bias_ref = rest[back + 2 * quads :]
    columns = heads * HDIM
    total = own_ref[...]
    for ref in arrived:
        total = total + ref[...].astype(F32)
    cosine, sine = cos_ref[...], -sin_ref[...]
    heads_out = [dq_ref[...]]
    for head in range(2 * heads):
        part = total[:, head * HDIM : (head + 1) * HDIM]
        if head < heads:
            part = turn(part, cosine, sine)
        heads_out.append(part.astype(BF16))
    grads = jnp.concatenate(heads_out, axis=1)
    out_ref[...] = grads

    @pl.when(pl.program_id(0) == 0)
    def _():
        gain_ref[...] = jnp.zeros_like(gain_ref)
        bias_ref[...] = jnp.zeros_like(bias_ref)

    bias_ref[...] += jnp.sum(grads.astype(F32), axis=0, keepdims=True)
    cut = 3 * columns // 2
    block = x_ref.shape[1] // quads
    for key in range(quads):
        cols = slice(key * block, (key + 1) * block)
        part = dot_last(grads[:, :cut], wa_refs[key][...]) + dot_last(grads[:, cut:], wb_refs[key][...])
        part_ref[:, cols] = part.astype(BF16)
        gain_ref[:, cols] += jnp.sum(part * x_ref[:, cols].astype(F32), axis=0, keepdims=True)


def collect(grad_query, own, cosine, sine, x, arrived, wa, wb):
    rows, columns = grad_query.shape
    width = x.shape[1]
    quads, (block, cut) = len(wa), wa[0].shape
    fixed = lambda i: (0, 0)
    return call(
        functools.partial(collect_kernel, columns // HDIM, len(arrived), quads),
        (rows // TILE,),
        [rows_spec(columns), rows_spec(2 * columns)]
        + [rows_spec(HDIM)] * 2
        + [rows_spec(width)]
        + [rows_spec(2 * columns)] * len(arrived)
        + [whole((block, cut))] * (2 * quads),
        [
            rows_spec(3 * columns),
            rows_spec(width),
            pl.BlockSpec((1, width), fixed),
            pl.BlockSpec((1, 3 * columns), fixed),
        ],
        [
            shaped(rows, 3 * columns, BF16),
            shaped(rows, width, BF16),
            shaped(1, width, F32),
            shaped(1, 3 * columns, F32),
        ],
        32,
        4 * rows * width * cut,
        name="collect",
    )(grad_query, own, cosine, sine, x, *arrived, *wa, *wb)


def expert_kernel(routed, quads, x_ref, wd_ref, cot_ref, scale_ref, *rest):
    if routed:
        wg_refs, wu_refs, rest = rest[:quads], rest[quads : 2 * quads], rest[2 * quads :]
        part_in, grad_in, dot_in, lane_ref = rest[:4]
        rest = rest[4:]
    else:
        wgu_refs, rest = rest[:quads], rest[quads:]
    x = x_ref[...]
    hidden, width = wd_ref.shape
    if routed:
        gate_pre = sum_pieces(x, wg_refs)
        up_pre = sum_pieces(x, wu_refs)
    else:
        pre = sum_pieces(x, wgu_refs)
        gate_pre, up_pre = pre[:, :hidden], pre[:, hidden:]
    sigma = jax.nn.sigmoid(gate_pre)
    swish = gate_pre * sigma
    active = (swish * up_pre).astype(BF16)
    rest[0][...] = active
    cot = cot_ref[...].astype(F32)
    scale = scale_ref[...]
    grad_result = (scale * cot).astype(BF16)
    rest[1][...] = grad_result
    grad_active = dot_last(grad_result, wd_ref[...])
    grad_up = grad_active * swish
    grad_gate = grad_active * up_pre * (sigma * (1.0 + gate_pre * (1.0 - sigma)))
    result = dot(active, wd_ref[...])
    if routed:
        result = result.astype(BF16).astype(F32)
    inner = jnp.sum(cot * result, axis=1, keepdims=True)
    part = scale * result
    block = width // quads
    if not routed:
        part_ref, grad_ref, inner_ref, both_ref = rest[2:]
        both = jnp.concatenate([grad_gate, grad_up], axis=1).astype(BF16)
        both_ref[...] = both
        part_ref[...] = part.astype(BF16)
        for key in range(quads):
            grad = dot_last(both, wgu_refs[key][...])
            grad_ref[:, key * block : (key + 1) * block] = grad.astype(BF16)
        inner_ref[...] = inner
        return
    part_ref, grad_ref, gate_ref, up_ref = rest[2:]
    grad_gate, grad_up = grad_gate.astype(BF16), grad_up.astype(BF16)
    gate_ref[...] = grad_gate
    up_ref[...] = grad_up
    part_ref[...] = (part + part_in[...].astype(F32)).astype(BF16)
    for key in range(quads):
        cols = slice(key * block, (key + 1) * block)
        grad = dot_last(grad_gate, wg_refs[key][...]) + dot_last(grad_up, wu_refs[key][...])
        grad = grad.astype(BF16).astype(F32) + grad_in[:, cols].astype(F32)
        grad_ref[:, cols] = grad.astype(BF16)
    lane = lane_ref[...]
    extra = jnp.zeros((x.shape[0], LANES), F32)
    for slot, value in enumerate((inner, dot_in[...])):
        high = value.astype(BF16).astype(F32)
        extra = extra + jnp.where(lane == 2 * slot, high, 0.0)
        extra = extra + jnp.where(lane == 2 * slot + 1, value - high, 0.0)
    grad_ref[:, width:] = extra.astype(BF16)


def expert(x, pieces, wd, cot, scale, routed=()):
    rows, width = x.shape
    hidden = wd.shape[0]
    quads = len(pieces) // 2 if routed else len(pieces)
    ins = [rows_spec(width), whole((hidden, width)), rows_spec(width), rows_spec(1)]
    ins += [whole(piece.shape) for piece in pieces]
    outs = [rows_spec(hidden), rows_spec(width), rows_spec(width)]
    shapes = [shaped(rows, hidden, BF16), shaped(rows, width, BF16), shaped(rows, width, BF16)]
    if routed:
        ins += [rows_spec(width), rows_spec(width), rows_spec(1), whole((1, LANES))]
        outs += [rows_spec(width + LANES), rows_spec(hidden), rows_spec(hidden)]
        shapes += [shaped(rows, width + LANES, BF16)] + [shaped(rows, hidden, BF16)] * 2
    else:
        outs += [rows_spec(width), rows_spec(1), rows_spec(2 * hidden)]
        shapes += [shaped(rows, width, BF16), shaped(rows, 1, F32), shaped(rows, 2 * hidden, BF16)]
    return call(
        functools.partial(expert_kernel, bool(routed), quads),
        (rows // TILE,),
        ins,
        outs,
        shapes,
        60,
        12 * rows * width * hidden,
        name="expert" if routed else "shared",
    )(x, wd, cot, scale, *pieces, *routed)


def local(
    residual_in,
    attention_gain,
    query_weight,
    query_bias,
    key_weight,
    key_bias,
    value_weight,
    value_bias,
    output_weight,
    feedforward_gain,
    router_weight,
    shared_logit_weight,
    shared_gate_weight,
    shared_up_weight,
    shared_down_weight,
    expert_gate,
    expert_up,
    expert_down,
    cotangent,
    expert_index,
    token_live,
    document_lengths,
):
    ep_count = lax.axis_size("ep")
    grp_count = lax.axis_size("grp")
    quads = grp_count // 2
    rows_dev, width = residual_in.shape
    group_rows = rows_dev * ep_count
    pair_rows = 2 * group_rows
    seq_len = group_rows * grp_count // SEQS
    expert_count = expert_gate.shape[0] * ep_count
    ffe = expert_gate.shape[2]
    ffs_half = shared_gate_weight.shape[1] // 2
    grp = lax.axis_index("grp")
    ep = lax.axis_index("ep")
    core = grp % 2
    quad = grp // 2
    back = -(-WINDOW // pair_rows)
    heads = query_weight.shape[1] // HDIM // 2
    head_width = heads * HDIM
    up_order = quad_bits()
    down_order = up_order[::-1]

    block = width // quads
    cut = len(up_order) // 2
    up_one, up_two = up_order[:cut], up_order[cut:]
    down_one, down_two = down_order[: len(down_order) - cut], down_order[len(down_order) - cut :]
    ep_masks = [1 << b for b in range(ep_count.bit_length() - 1)]
    quad_masks = [2 * bit for bit in up_order]
    seq_groups = grp_count // SEQS
    experts = jnp.arange(expert_count, dtype=jnp.int32)
    ed_cut = width // 2

    def shifted(values, steps):
        route = [
            (i, i + 2 * steps)
            for i in range(grp_count)
            if 0 <= i + 2 * steps < grp_count and i // seq_groups == (i + 2 * steps) // seq_groups
        ]
        return lax.ppermute(values, "grp", route)

    def gathered(values):
        return lax.all_gather(values, "ep", axis=0, tiled=True)

    def scattered(values):
        return lax.psum_scatter(values, "ep", scatter_dimension=0, tiled=True).astype(F32)

    def core_sum(values):
        keep, other = split_core(values, core, 0)
        return (keep.astype(F32) + across(other, 1).astype(F32)).astype(BF16)

    def row_grads(rows, grads):
        return {
            k: dot_first(rows[:, k * block : (k + 1) * block], grads).astype(BF16)
            for k in range(quads)
        }

    def column_grads(acts, grads):
        return {
            k: dot_first(acts, part).astype(BF16)
            for k, part in take_quads(grads, quad, quads, 1).items()
        }

    hidden_in = residual_in.astype(F32)
    grad_out = cotangent.astype(F32)
    gain_one = attention_gain.astype(F32)
    gain_two = feedforward_gain.astype(F32)
    router_all = jnp.concatenate([router_weight, shared_logit_weight[:, None]], axis=1)
    router_flipped = flip_columns(router_all.T, quad).T
    scale_one = norm_scale(hidden_in)
    unit_one = hidden_in * scale_one
    normed_one = (unit_one * gain_one).astype(BF16)
    group_one = gathered(flip_columns(normed_one, quad))

    qk_keep, qk_other = zip(
        *[split_core(weight, core, 1) for weight in (query_weight, key_weight, value_weight)]
    )
    qkv_keep, qkv_other = jnp.concatenate(qk_keep, 1), jnp.concatenate(qk_other, 1)
    qkv_block = merge_core(qkv_keep, across(qkv_other, 1), core, 0)
    qkv_cut = qkv_block.shape[1] // 2
    qkv_a = {0: qkv_block[:, :qkv_cut]}
    qkv_b = {0: qkv_block[:, qkv_cut:]}
    (
        qkv_a, qkv_b, output_weight, shared_gate_weight, shared_up_weight, shared_down_weight,
        expert_gate, expert_up, expert_down,
    ) = together(
        qkv_a, qkv_b, output_weight, shared_gate_weight, shared_up_weight, shared_down_weight,
        expert_gate, expert_up, expert_down,
    )
    qkv_a_one, qkv_a_two = gather_quads(qkv_a, up_one), gather_quads(qkv_a, up_two)
    qkv_b_one, qkv_b_two = gather_quads(qkv_b, down_one), gather_quads(qkv_b, down_two)

    o_keep, o_other = split_core(output_weight, core, 0)
    o_block = merge_core(o_keep, across(o_other, 1), core, 1)
    sg_keep, sg_other = split_core(shared_gate_weight, core, 1)
    su_keep, su_other = split_core(shared_up_weight, core, 1)
    gu_keep = jnp.concatenate([sg_keep, su_keep], axis=1)
    gu_other = jnp.concatenate([sg_other, su_other], axis=1)
    gu_block = merge_core(gu_keep, across(gu_other, 1), core, 0)
    sd_keep, sd_other = split_core(shared_down_weight, core, 0)
    sd_block = merge_core(sd_keep, across(sd_other, 1), core, 1)

    def expert_block(weight):
        keep, other = split_core(weight, core, 0)
        return merge_core(keep[0], across(other[0], 1), core, 0)

    eg_block, eu_block, ed_block = [
        expert_block(weight) for weight in (expert_gate, expert_up, expert_down)
    ]
    eda_block, edb_block = ed_block[:, :ed_cut], ed_block[:, ed_cut:]

    (
        qkv_a_one, qkv_a_two, qkv_b_one, qkv_b_two, o_block, gu_block, sd_block, eg_block, eu_block,
        eda_block, edb_block,
    ) = together(
        qkv_a_one, qkv_a_two, qkv_b_one, qkv_b_two, o_block, gu_block, sd_block, eg_block, eu_block,
        eda_block, edb_block,
    )
    qkv_a_rest = gather_rest(qkv_a_one, up_two)
    qkv_b_rest = gather_rest(qkv_b_one, down_two)
    o_one, o_two = gather_quads({0: o_block}, down_one), gather_quads({0: o_block}, down_two)
    sd_one, sd_two = gather_quads({0: sd_block}, down_one), gather_quads({0: sd_block}, down_two)
    (
        group_one, qkv_a, qkv_b, o_one, o_two, sd_one, sd_two, gu_block, eg_block, eu_block,
        eda_block, edb_block, cotangent,
    ) = together(
        group_one, qkv_a_one | qkv_a_two | qkv_a_rest, qkv_b_one | qkv_b_two | qkv_b_rest, o_one,
        o_two, sd_one, sd_two, gu_block, eg_block, eu_block, eda_block, edb_block, cotangent,
    )

    rows_one = merge_core(group_one, across(group_one, 1), core, 0)
    gu_two = gather_quads({0: gu_block}, up_two)
    o_rest = gather_rest(o_one, down_two)
    chosen = (
        (expert_index[:, :, None] == experts[None, None, :]) & (token_live[:, None, None] > 0)
    ).any(axis=1)
    chosen = chosen.astype(BF16)
    cot_group = gathered(
        jnp.concatenate([cotangent, jnp.pad(chosen, ((0, 0), (0, LANES - expert_count)))], axis=1)
    )
    chosen = chosen.astype(F32)
    qkv_a, qkv_b = listed(qkv_a), listed(qkv_b)
    bias = jnp.concatenate(
        [split_core(b, core, 0)[0] for b in (query_bias, key_bias, value_bias)]
    ).astype(F32)
    key_place = (quad - back) * pair_rows + jnp.arange((back + 1) * pair_rows, dtype=jnp.int32)
    query_place = key_place[back * pair_rows :]
    _, position = doc_layout(document_lengths, seq_len, query_place)
    low = jnp.maximum(query_place - position, query_place - WINDOW + 1)[:, None]
    high, key_place = query_place[:, None], key_place[None, :]
    cosine, sine = rope_tables(position)
    query, key_value = project(rows_one, qkv_a, qkv_b, bias[None, :], cosine, sine, heads)

    before = [shifted(key_value, step) for step in range(back, 0, -1)]
    query, before, gu_two, o_rest, sd_one, edb_block = together(
        query, before, gu_two, o_rest, sd_one, edb_block
    )
    sd_rest = gather_rest(sd_one, down_two)
    edb_one = gather_quads({0: edb_block}, down_one)
    attended, log_total = attend(query, before, key_value, key_place, low, high)
    o_full = place_quads(o_one | o_two | o_rest, quad, 1)
    branch = dot(attended, o_full).astype(BF16)
    branch, cot_group, sd_rest, edb_one = together(branch, cot_group, sd_rest, edb_one)
    branch = core_sum(branch)
    branch, gu_block, eu_block, eda_block, cot_group = together(
        branch, gu_block, eu_block, eda_block, cot_group
    )
    branch_sum = scattered(branch)
    cot_other = across(cot_group, 1)
    gu_one = gather_quads({0: gu_block}, up_one)
    eda_one, eda_two = gather_quads({0: eda_block}, up_one), gather_quads({0: eda_block}, up_two)
    eu_one = gather_quads({0: eu_block}, down_one)
    branch_sum, cot_other, gu_one, eda_one, eda_two, eu_one, eg_block, edb_block = together(
        branch_sum, cot_other, gu_one, eda_one, eda_two, eu_one, eg_block, edb_block
    )

    eg_one = gather_quads({0: eg_block}, up_one)
    edb_two, edb_rest = gather_quads({0: edb_block}, down_two), gather_rest(edb_one, down_two)
    gu_rest, eda_rest = gather_rest(gu_one, up_two), gather_rest(eda_one, up_two)
    mixed = hidden_in + branch_sum
    scale_two = norm_scale(mixed)
    unit_two = mixed * scale_two
    normed_two = (unit_two * gain_two).astype(BF16)
    group_two = gathered(flip_columns(normed_two, quad))
    cot_rows = merge_core(cot_group, cot_other, core, 0)
    sd_full = place_quads(sd_one | sd_two | sd_rest, quad, 1)
    group_two, eg_one, edb_two, edb_rest, gu_rest, eda_rest = together(
        group_two, eg_one, edb_two, edb_rest, gu_rest, eda_rest
    )
    rows_two = merge_core(group_two, across(group_two, 1), core, 0)
    (
        rows_two, cot_rows, sd_full, eg_one, edb_two, edb_rest, gu_rest, eda_rest, eu_one, eu_block,
        eg_block,
    ) = together(
        rows_two, cot_rows, sd_full, eg_one, edb_two, edb_rest, gu_rest, eda_rest, eu_one, eu_block,
        eg_block,
    )
    eu_two, eg_two = gather_quads({0: eu_block}, down_two), gather_quads({0: eg_block}, up_two)
    gu_pieces = listed(gu_one | gu_two | gu_rest)
    ed_full = jnp.concatenate(
        [
            place_quads(eda_one | eda_two | eda_rest, quad, 0),
            place_quads(edb_one | edb_two | edb_rest, quad, 0),
        ],
        axis=1,
    )

    def router(rows, weight):
        logits = dot(rows, weight)
        return jax.nn.softmax(logits[:, :expert_count], axis=-1), jax.nn.sigmoid(
            logits[:, expert_count:]
        )

    chosen_rows = cot_rows[:, width : width + expert_count].astype(F32)
    probs_rows, shared_scale_rows = router(rows_two, router_flipped)
    router_probs, shared_scale = router(normed_two, router_all)
    mine = (experts == ep * 2 + core).astype(F32)[None, :]
    gate = jnp.sum(probs_rows * chosen_rows * mine, axis=1, keepdims=True)

    shared_active, grad_shared_out, part, grad_part, shared_dot, grad_gu = expert(
        rows_two, gu_pieces, sd_full, cot_rows, shared_scale_rows
    )
    grad_gu, grad_part, eu_two, eg_two, eu_one, eg_one = together(
        grad_gu, grad_part, eu_two, eg_two, eu_one, eg_one
    )
    eu_rest, eg_rest = gather_rest(eu_one, down_two), gather_rest(eg_one, up_two)
    gu_grad = row_grads(rows_two, grad_gu)
    sd_grad = column_grads(shared_active, grad_shared_out)
    grad_part, eg_pieces, eu_pieces, ed_full, gu_grad, sd_grad = together(
        grad_part, eg_one | eg_two | eg_rest, eu_one | eu_two | eu_rest, ed_full, gu_grad, sd_grad
    )
    up_keys = [key for key in gu_grad if key & up_one[0]]
    down_keys = [key for key in gu_grad if key & down_one[0]]
    gu_sent = send_quads(gu_grad, up_one[0], up_keys)
    sd_sent = send_quads(sd_grad, down_one[0], down_keys)

    lanes = jnp.arange(LANES, dtype=jnp.int32)
    lanes = jnp.where(lanes % expert_count == ep * 2 + core, lanes // expert_count, -1)[None, :]
    active, grad_result, forward_part, packed, grad_gate_pre, grad_up_pre = expert(
        rows_two,
        listed(eg_pieces) + listed(eu_pieces),
        ed_full,
        cot_rows,
        gate,
        (part, grad_part, shared_dot, lanes),
    )
    packed, gu_grad, gu_sent, sd_grad, sd_sent = together(packed, gu_grad, gu_sent, sd_grad, sd_sent)
    packed = core_sum(packed)
    gu_grad = reduce_quads(add_quads(gu_grad, gu_sent, up_one[0]), up_one[1:])
    sd_grad = reduce_quads(add_quads(sd_grad, sd_sent, down_one[0]), down_one[1:])
    packed, gu_grad, sd_grad, active, grad_gate_pre, grad_up_pre = together(
        packed, gu_grad, sd_grad, active, grad_gate_pre, grad_up_pre
    )
    spread = scattered(packed)
    ed_grad = take_quads(dot_first(active, grad_result).astype(BF16), quad, quads, 0)
    eda_grad = {k: v[:, :ed_cut] for k, v in ed_grad.items()}
    edb_grad = {k: v[:, ed_cut:] for k, v in ed_grad.items()}
    gu_grad = reduce_quads(gu_grad, up_two)[0]
    sd_grad = reduce_quads(sd_grad, down_two)[0]
    eda_sent = send_quads(eda_grad, up_one[0], up_keys)
    edb_sent = send_quads(edb_grad, down_one[0], down_keys)
    eg_grad = row_grads(rows_two, grad_gate_pre)
    eu_grad = row_grads(rows_two, grad_up_pre)
    spread, gu_grad, sd_grad, eg_grad, eu_grad = together(spread, gu_grad, sd_grad, eg_grad, eu_grad)

    grad_normed_two = flip_columns(spread[:, :width], quad)
    side = spread[:, width : width + 4 * expert_count].reshape(rows_dev, 4, expert_count)
    grad_gate_own = side[:, 0] + side[:, 1]
    shared_dot_own = jnp.sum(side[:, 2] + side[:, 3], axis=1, keepdims=True)
    grad_logit = shared_dot_own * shared_scale * (1.0 - shared_scale)
    grad_probs = grad_gate_own * chosen
    grad_logits = router_probs * (
        grad_probs - jnp.sum(router_probs * grad_probs, axis=-1, keepdims=True)
    )
    grad_router = jnp.concatenate([grad_logits, grad_logit], axis=1)
    router_grad = dot_first(normed_two.astype(F32), grad_router)
    grad_normed_two = grad_normed_two + dot_last(grad_router, router_all.astype(F32))
    grad_norm_part, ff_gain_grad = norm_backward(grad_normed_two, unit_two, scale_two, gain_two)
    grad_mixed = grad_out + grad_norm_part
    branch_low, eda_grad, eda_sent, edb_grad, edb_sent, eg_grad, eu_grad, forward_part = together(
        grad_mixed.astype(BF16), eda_grad, eda_sent, edb_grad, edb_sent, eg_grad, eu_grad,
        forward_part,
    )
    group_branch = gathered(branch_low)
    half = len(up_keys) // 2
    eg_sent = send_quads(eg_grad, up_one[0], up_keys[:half])
    eu_sent = send_quads(eu_grad, down_one[0], down_keys[:half])
    eda_grad = reduce_quads(add_quads(eda_grad, eda_sent, up_one[0]), up_one[1:])
    edb_grad = reduce_quads(add_quads(edb_grad, edb_sent, down_one[0]), down_one[1:])
    forward_sum = core_sum(forward_part)
    group_branch, forward_sum, eg_grad, eg_sent, eu_grad, eu_sent, eda_grad, edb_grad = together(
        group_branch, forward_sum, eg_grad, eg_sent, eu_grad, eu_sent, eda_grad, edb_grad
    )
    grad_branch = merge_core(group_branch, across(group_branch, 1), core, 0)
    eg_sent |= send_quads(eg_grad, up_one[0], up_keys[half:])
    eu_sent |= send_quads(eu_grad, down_one[0], down_keys[half:])

    layer_sum = scattered(forward_sum)
    grad_attended = dot_last(grad_branch, o_full).astype(BF16)
    grad_query, grad_own, *grad_before = attend_back(
        query, grad_attended, log_total, before, key_value, key_place, low, high, cosine, sine
    )
    grad_query, grad_before, eg_grad, eg_sent, eu_grad, eu_sent, eda_grad, edb_grad = together(
        grad_query, grad_before, eg_grad, eg_sent, eu_grad, eu_sent, eda_grad, edb_grad
    )
    arrived = [shifted(sent, step - back) for step, sent in enumerate(grad_before)]
    eg_grad = reduce_quads(add_quads(eg_grad, eg_sent, up_one[0]), up_one[1:])
    eu_grad = reduce_quads(add_quads(eu_grad, eu_sent, down_one[0]), down_one[1:])
    eg_grad = reduce_quads(eg_grad, up_two)[0]
    o_grad = column_grads(attended, grad_branch)
    arrived, o_grad, layer_sum, eg_grad, eu_grad, eda_grad, edb_grad = together(
        arrived, o_grad, layer_sum, eg_grad, eu_grad, eda_grad, edb_grad
    )
    layer_out = (mixed + layer_sum).astype(BF16)
    eda_grad = reduce_quads(eda_grad, up_two)[0]
    edb_grad = reduce_quads(edb_grad, down_two)[0]
    grad_lin, partial, att_gain_part, bias_part = collect(
        grad_query, grad_own, cosine, sine, rows_one, arrived, qkv_a, qkv_b
    )
    grad_lin_a, grad_lin_b = grad_lin[:, :qkv_cut], grad_lin[:, qkv_cut:]
    partial_sum = core_sum(partial)

    att_gain_part = flip_columns(att_gain_part[0], quad) / gain_one
    late = jnp.concatenate(
        [bias_part[0], att_gain_part, ff_gain_grad, router_grad.T.reshape(-1)]
    )
    qkv_a_grad = row_grads(rows_one, grad_lin_a)
    qkv_b_grad = row_grads(rows_one, grad_lin_b)
    partial_sum, qkv_a_grad, qkv_b_grad, late, eda_grad, edb_grad, eu_grad = together(
        partial_sum, qkv_a_grad, qkv_b_grad, late, eda_grad, edb_grad, eu_grad
    )
    grad_normed_one = scattered(partial_sum)
    eu_grad = reduce_quads(eu_grad, down_two)[0]
    o_grad = reduce_quads(o_grad, down_order)[0]
    qkv_a_grad = reduce_quads(qkv_a_grad, up_order)[0]
    qkv_b_grad = reduce_quads(qkv_b_grad, down_order)[0]
    qkv_grad = jnp.concatenate([qkv_a_grad, qkv_b_grad], axis=1)
    late = sum_everywhere(late, quad_masks, [])
    bias_part = late[: 3 * head_width]
    bias_mine = merge_core(
        bias_part.reshape(3, head_width), across(bias_part, 1).reshape(3, head_width), core, 1
    )
    late = sum_everywhere(late[3 * head_width :], [1], ep_masks)
    att_gain_grad, ff_gain_grad = late[:width], late[width : 2 * width]
    router_grad = late[2 * width :].reshape(expert_count + 1, width)
    grad_norm_one, _ = norm_backward(
        flip_columns(grad_normed_one, quad), unit_one, scale_one, gain_one
    )
    input_grad = grad_mixed + grad_norm_one

    def back_to_cores(summed, cut_axis, join_axis):
        keep, other = split_core(summed, core, cut_axis)
        return merge_core(keep, across(other, 1), core, join_axis).astype(F32)

    def back_to_experts(summed):
        keep, other = split_core(summed, core, 0)
        arrived = across(other, 1)
        return jnp.stack(
            [jnp.where(core == 0, keep, arrived), jnp.where(core == 0, arrived, keep)]
        ).astype(F32)

    ed_grad = jnp.concatenate([eda_grad, edb_grad], axis=1)
    q_grad, k_grad, v_grad = [
        back_to_cores(qkv_grad[:, part * head_width : (part + 1) * head_width], 0, 1)
        for part in range(3)
    ]
    return (
        layer_out,
        input_grad,
        att_gain_grad,
        q_grad,
        bias_mine[0],
        k_grad,
        bias_mine[1],
        v_grad,
        bias_mine[2],
        back_to_cores(o_grad, 1, 0),
        ff_gain_grad,
        router_grad[:expert_count].T,
        router_grad[expert_count],
        back_to_cores(gu_grad[:, :ffs_half], 0, 1),
        back_to_cores(gu_grad[:, ffs_half:], 0, 1),
        back_to_cores(sd_grad, 1, 0),
        back_to_experts(eg_grad),
        back_to_experts(eu_grad),
        back_to_experts(ed_grad),
    )


def solution(mesh):
    tokens = P(("grp", "ep"), None)
    rows, columns, experts = P("grp", "ep"), P("ep", "grp"), P("ep", "grp", None)
    in_specs = (
        tokens, P(), rows, P("ep"), rows, P("ep"), rows, P("ep"), columns, P(), P(), P(),
        rows, rows, columns, experts, experts, experts, tokens, tokens, P(("grp", "ep")), P(),
    )
    out_specs = (
        tokens, tokens, P(), rows, P("ep"), rows, P("ep"), rows, P("ep"), columns, P(), P(), P(),
        rows, rows, columns, experts, experts, experts,
    )
    return jax.shard_map(local, mesh=mesh, in_specs=in_specs, out_specs=out_specs, check_vma=False)
```

```python
import functools

import jax
import jax.numpy as jnp
from jax import lax
from jax.experimental import pallas as pl
from jax.experimental.pallas import tpu as pltpu
from jax.sharding import PartitionSpec as P

HDIM = 128
SEQS = 2
DOCS = 4
WINDOW = 1024
EPS = 1e-06
ROPE_BASE = 1000000.0
MASKED = -1e30
F32 = jnp.float32
BF16 = jnp.bfloat16
TILE = 256
LANES = 128
MIB = 1 << 20


def dot(left, right):
    return jnp.dot(left, right, preferred_element_type=F32)


def dot_last(left, right):
    return lax.dot_general(left, right, (((1,), (1,)), ((), ())), preferred_element_type=F32)


def dot_first(left, right):
    return lax.dot_general(left, right, (((0,), (0,)), ((), ())), preferred_element_type=F32)


def across(block, mask):
    count = lax.axis_size("grp")
    return lax.ppermute(block, "grp", [(i, i ^ mask) for i in range(count)])


def quad_bits():
    return [1 << b for b in range((lax.axis_size("grp") // 2).bit_length() - 1)]


def flip_columns(values, quad):
    quads = lax.axis_size("grp") // 2
    axis = values.ndim - 1
    block = values.shape[axis] // quads
    return jnp.concatenate(
        [
            lax.dynamic_slice_in_dim(values, (quad ^ key) * block, block, axis)
            for key in range(quads)
        ],
        axis=axis,
    )


def gather_quads(pieces, order):
    pieces = dict(pieces)
    for bit in order:
        for key, piece in list(pieces.items()):
            pieces[key | bit] = across(piece, 2 * bit)
    return pieces


def send_quads(pieces, bit, keys):
    return {key: across(pieces[key], 2 * bit) for key in keys}


def add_quads(pieces, arrived, bit):
    return {
        key: (piece.astype(F32) + arrived[key | bit].astype(F32)).astype(BF16)
        for key, piece in pieces.items()
        if not key & bit
    }


def reduce_quads(pieces, order):
    for bit in order:
        arrived = send_quads(pieces, bit, [key for key in pieces if key & bit])
        pieces = add_quads(pieces, arrived, bit)
    return pieces


def together(*values):
    return lax.optimization_barrier(values)


def sum_everywhere(values, masks_grp, masks_ep):
    for mask in masks_grp:
        values = values + across(values, mask)
    count = lax.axis_size("ep")
    for mask in masks_ep:
        values = values + lax.ppermute(values, "ep", [(i, i ^ mask) for i in range(count)])
    return values


def gather_rest(pieces, order):
    found = {}
    for key, piece in pieces.items():
        if key:
            found.update({key | k: v for k, v in gather_quads({0: piece}, order).items()})
    return found


def listed(pieces):
    return [pieces[key] for key in sorted(pieces)]


def place_quads(pieces, quad, axis, whole=None, other=0):
    size = pieces[0].shape[axis] if whole is None else whole.shape[axis] // (lax.axis_size("grp") // 2)
    if whole is None:
        shape = list(pieces[0].shape)
        shape[axis] = size * len(pieces)
        whole = jnp.zeros(shape, pieces[0].dtype)
    for key in sorted(pieces):
        start = [other, other]
        start[axis] = (quad ^ key) * size
        whole = lax.dynamic_update_slice(whole, pieces[key], start)
    return whole


def take_quads(whole, quad, quads, axis):
    size = whole.shape[axis] // quads
    return {
        key: lax.dynamic_slice_in_dim(whole, (quad ^ key) * size, size, axis)
        for key in range(quads)
    }


def merge_core(kept, arrived, core, axis):
    first = jnp.where(core == 0, kept, arrived)
    second = jnp.where(core == 0, arrived, kept)
    return jnp.concatenate([first, second], axis=axis)


def split_core(values, core, axis):
    half = values.shape[axis] // 2
    first = lax.slice_in_dim(values, 0, half, axis=axis)
    second = lax.slice_in_dim(values, half, 2 * half, axis=axis)
    return jnp.where(core == 0, first, second), jnp.where(core == 0, second, first)


def norm_scale(values):
    return lax.rsqrt(jnp.mean(values * values, axis=-1, keepdims=True) + EPS)


def norm_backward(grad_normed, unit, scale, gain):
    grad_unit = grad_normed * gain
    inner = jnp.mean(grad_unit * unit, axis=-1, keepdims=True)
    return scale * (grad_unit - unit * inner), jnp.sum(grad_normed * unit, axis=0)


def doc_layout(document_lengths, seq_len, index):
    valid = index >= 0
    safe = jnp.maximum(index, 0)
    seq_of = safe // seq_len
    place = safe % seq_len
    seq_count = document_lengths.shape[0]
    picker = (seq_of[:, None] == jnp.arange(seq_count, dtype=jnp.int32)[None, :]).astype(jnp.int32)
    lengths = jnp.sum(picker[:, :, None] * document_lengths[None, :, :], axis=1)
    ends = jnp.cumsum(lengths, axis=1)
    doc = jnp.sum((ends <= place[:, None]).astype(jnp.int32), axis=1)
    earlier = jnp.arange(DOCS, dtype=jnp.int32)[None, :] < doc[:, None]
    before = jnp.sum(jnp.where(earlier, lengths, 0), axis=1)
    return jnp.where(valid, seq_of * DOCS + doc, -1), place - before


def rope_tables(position):
    half = HDIM // 2
    freq = ROPE_BASE ** (-(jnp.arange(half, dtype=F32) * 2.0 / HDIM))
    angle = position.astype(F32)[:, None] * freq[None, :]
    cosine, sine = jnp.cos(angle), jnp.sin(angle)
    return jnp.concatenate([cosine, cosine], axis=1), jnp.concatenate([-sine, sine], axis=1)


def turn(values, cosine, sine):
    return values * cosine + pltpu.roll(values, HDIM // 2, 1) * sine


def call(kernel, grid, ins, outs, shapes, limit, flops, scratch=(), name=None):
    moved = 0
    for shape in shapes:
        moved += shape.size * shape.dtype.itemsize

    def run(*args):
        total = moved + sum(a.size * a.dtype.itemsize for a in args)
        return pl.pallas_call(
            kernel,
            grid=grid,
            in_specs=ins,
            out_specs=outs,
            out_shape=shapes,
            scratch_shapes=scratch,
            compiler_params=pltpu.CompilerParams(vmem_limit_bytes=limit * MIB),
            cost_estimate=pl.CostEstimate(
                flops=flops, bytes_accessed=total, transcendentals=0
            ),
            name=name,
        )(*args)

    return run


def whole(shape):
    return pl.BlockSpec(shape, lambda *_: (0,) * len(shape), pipeline_mode=pl.Buffered(1))


def rows_spec(columns, tile=TILE):
    return pl.BlockSpec((tile, columns), lambda i: (i, 0))


def shaped(rows, columns, dtype):
    return jax.ShapeDtypeStruct((rows, columns), dtype)


def sum_pieces(x, refs):
    block = x.shape[1] // len(refs)
    total = dot(x[:, :block], refs[0][...])
    for key in range(1, len(refs)):
        total = total + dot(x[:, key * block : (key + 1) * block], refs[key][...])
    return total


def project_kernel(heads, quads, x_ref, bias_ref, cos_ref, sin_ref, *rest):
    wa_refs, wb_refs, (q_ref, kv_ref) = rest[:quads], rest[quads : 2 * quads], rest[2 * quads :]
    x = x_ref[...]
    lin = jnp.concatenate([sum_pieces(x, wa_refs), sum_pieces(x, wb_refs)], axis=1) + bias_ref[...]
    cosine, sine = cos_ref[...], sin_ref[...]
    for head in range(3 * heads):
        part = lin[:, head * HDIM : (head + 1) * HDIM]
        if head < 2 * heads:
            part = turn(part, cosine, sine)
        if head < heads:
            q_ref[:, head * HDIM : (head + 1) * HDIM] = part.astype(BF16)
        else:
            kv_ref[:, (head - heads) * HDIM : (head - heads + 1) * HDIM] = part.astype(BF16)


def project(x, wa, wb, bias, cosine, sine, heads):
    rows, width = x.shape
    quads, (block, cut) = len(wa), wa[0].shape
    return call(
        functools.partial(project_kernel, heads, quads),
        (rows // TILE,),
        [rows_spec(width), whole((1, 2 * cut))]
        + [rows_spec(HDIM)] * 2
        + [whole((block, cut))] * (2 * quads),
        [rows_spec(heads * HDIM), rows_spec(2 * heads * HDIM)],
        [shaped(rows, heads * HDIM, BF16), shaped(rows, 2 * heads * HDIM, BF16)],
        32,
        4 * rows * width * cut,
        name="project",
    )(x, bias, cosine, sine, *wa, *wb)


def window_keys(before_refs, own_ref, place, pair_rows, step):
    parts = []
    start = step * TILE
    reach = -WINDOW + start
    for back, ref in enumerate(before_refs):
        first = -(len(before_refs) - back) * pair_rows
        low = max(reach - first, 0)
        if low < pair_rows:
            parts.append(ref[low:, place])
    parts.append(own_ref[max(reach, 0) : start + TILE, place])
    return jnp.concatenate(parts, axis=0) if len(parts) > 1 else parts[0]


def probabilities(query, keys, key_place, low, high, peak):
    scores = dot_last(query, keys) * HDIM ** (-0.5)
    scores = jnp.where((key_place >= low) & (key_place <= high), scores, MASKED)
    if peak is None:
        top = jnp.max(scores, axis=1, keepdims=True)
        weights = jnp.exp(scores - top)
        total = jnp.sum(weights, axis=1, keepdims=True)
        return weights / total, top + jnp.log(total)
    return jnp.exp(scores - peak), peak


def attend_kernel(back, pair_rows, heads, q_ref, *rest):
    before, (own_ref, place_ref, low_ref, high_ref, out_ref, log_ref) = rest[:back], rest[back:]
    for head in range(heads):
        cols = slice(head * HDIM, (head + 1) * HDIM)
        value_cols = slice((heads + head) * HDIM, (heads + head + 1) * HDIM)
        for step in range(pair_rows // TILE):
            rows = slice(step * TILE, (step + 1) * TILE)
            first = back * pair_rows - WINDOW + step * TILE
            places = place_ref[:, max(first, 0) : back * pair_rows + (step + 1) * TILE]
            keys = window_keys(before, own_ref, cols, pair_rows, step)
            values = window_keys(before, own_ref, value_cols, pair_rows, step)
            probs, logs = probabilities(
                q_ref[rows, cols], keys, places, low_ref[rows, :], high_ref[rows, :], None
            )
            out_ref[rows, cols] = dot(probs.astype(BF16), values).astype(BF16)
            log_ref[rows, cols] = jnp.broadcast_to(logs, (TILE, HDIM))


def attend(query, before, own, places, low, high):
    rows, columns = query.shape
    heads = columns // HDIM
    back = len(before)
    return call(
        functools.partial(attend_kernel, back, rows, heads),
        (),
        [pl.BlockSpec(memory_space=pltpu.VMEM)] * (5 + back),
        [pl.BlockSpec(memory_space=pltpu.VMEM)] * 2,
        [shaped(rows, columns, BF16), shaped(rows, columns, F32)],
        40,
        4 * rows * columns * (WINDOW + TILE),
        name="attend",
    )(query, *before, own, places, low, high)


def attend_back_kernel(back, pair_rows, heads, q_ref, grad_ref, log_ref, *rest):
    before = rest[:back]
    own_ref, place_ref, low_ref, high_ref, cos_ref, sin_ref = rest[back : back + 6]
    dq_ref, own_out = rest[back + 6 : back + 8]
    before_out = rest[back + 8 : 2 * back + 8]
    total_ref = rest[-1]
    total_ref[...] = jnp.zeros_like(total_ref)
    for head in range(heads):
        cols = slice(head * HDIM, (head + 1) * HDIM)
        value_cols = slice((heads + head) * HDIM, (heads + head + 1) * HDIM)
        for step in range(pair_rows // TILE):
            rows = slice(step * TILE, (step + 1) * TILE)
            first = max(back * pair_rows - WINDOW + step * TILE, 0)
            last = back * pair_rows + (step + 1) * TILE
            keys = window_keys(before, own_ref, cols, pair_rows, step)
            values = window_keys(before, own_ref, value_cols, pair_rows, step)
            query, grad = q_ref[rows, cols], grad_ref[rows, cols]
            peak = jnp.concatenate([log_ref[rows, cols]] * ((last - first) // HDIM), axis=1)
            probs, _ = probabilities(
                query, keys, place_ref[:, first:last], low_ref[rows, :], high_ref[rows, :], peak
            )
            grad_probs = dot_last(grad, values)
            inner = jnp.sum(probs * grad_probs, axis=1, keepdims=True)
            grad_scores = (probs * (grad_probs - inner)).astype(BF16)
            grad_query = dot(grad_scores, keys) * HDIM ** (-0.5)
            dq_ref[rows, cols] = turn(grad_query, cos_ref[rows, :], -sin_ref[rows, :]).astype(BF16)
            total_ref[first:last, cols] += dot_first(grad_scores, query) * HDIM ** (-0.5)
            total_ref[first:last, value_cols] += dot_first(probs.astype(BF16), grad)
    own_out[...] = total_ref[back * pair_rows :, :]
    for step in range(back):
        before_out[step][...] = total_ref[step * pair_rows : (step + 1) * pair_rows, :].astype(BF16)


def attend_back(query, grad, logs, before, own, places, low, high, cosine, sine):
    rows, columns = query.shape
    back = len(before)
    return call(
        functools.partial(attend_back_kernel, back, rows, columns // HDIM),
        (),
        [pl.BlockSpec(memory_space=pltpu.VMEM)] * (9 + back),
        [pl.BlockSpec(memory_space=pltpu.VMEM)] * (2 + back),
        [shaped(rows, columns, BF16), shaped(rows, 2 * columns, F32)]
        + [shaped(rows, 2 * columns, BF16)] * back,
        48,
        10 * rows * columns * (WINDOW + TILE),
        scratch=[pltpu.VMEM(((back + 1) * rows, 2 * columns), F32)],
        name="attend_back",
    )(query, grad, logs, *before, own, places, low, high, cosine, sine)


def collect_kernel(heads, back, quads, dq_ref, own_ref, cos_ref, sin_ref, x_ref, *rest):
    arrived, wa_refs, wb_refs = rest[:back], rest[back : back + quads], rest[back + quads : back + 2 * quads]
    out_ref, part_ref, gain_ref, bias_ref = rest[back + 2 * quads :]
    columns = heads * HDIM
    total = own_ref[...]
    for ref in arrived:
        total = total + ref[...].astype(F32)
    cosine, sine = cos_ref[...], -sin_ref[...]
    heads_out = [dq_ref[...]]
    for head in range(2 * heads):
        part = total[:, head * HDIM : (head + 1) * HDIM]
        if head < heads:
            part = turn(part, cosine, sine)
        heads_out.append(part.astype(BF16))
    grads = jnp.concatenate(heads_out, axis=1)
    out_ref[...] = grads

    @pl.when(pl.program_id(0) == 0)
    def _():
        gain_ref[...] = jnp.zeros_like(gain_ref)
        bias_ref[...] = jnp.zeros_like(bias_ref)

    bias_ref[...] += jnp.sum(grads.astype(F32), axis=0, keepdims=True)
    cut = 3 * columns // 2
    block = x_ref.shape[1] // quads
    for key in range(quads):
        cols = slice(key * block, (key + 1) * block)
        part = dot_last(grads[:, :cut], wa_refs[key][...]) + dot_last(grads[:, cut:], wb_refs[key][...])
        part_ref[:, cols] = part.astype(BF16)
        gain_ref[:, cols] += jnp.sum(part * x_ref[:, cols].astype(F32), axis=0, keepdims=True)


def collect(grad_query, own, cosine, sine, x, arrived, wa, wb):
    rows, columns = grad_query.shape
    width = x.shape[1]
    quads, (block, cut) = len(wa), wa[0].shape
    fixed = lambda i: (0, 0)
    return call(
        functools.partial(collect_kernel, columns // HDIM, len(arrived), quads),
        (rows // TILE,),
        [rows_spec(columns), rows_spec(2 * columns)]
        + [rows_spec(HDIM)] * 2
        + [rows_spec(width)]
        + [rows_spec(2 * columns)] * len(arrived)
        + [whole((block, cut))] * (2 * quads),
        [
            rows_spec(3 * columns),
            rows_spec(width),
            pl.BlockSpec((1, width), fixed),
            pl.BlockSpec((1, 3 * columns), fixed),
        ],
        [
            shaped(rows, 3 * columns, BF16),
            shaped(rows, width, BF16),
            shaped(1, width, F32),
            shaped(1, 3 * columns, F32),
        ],
        60,
        4 * rows * width * cut,
        name="collect",
    )(grad_query, own, cosine, sine, x, *arrived, *wa, *wb)


def expert_kernel(routed, quads, x_ref, wd_ref, cot_ref, scale_ref, *rest):
    if routed:
        wg_refs, wu_refs, rest = rest[:quads], rest[quads : 2 * quads], rest[2 * quads :]
        part_in, grad_in, dot_in, lane_ref = rest[:4]
        rest = rest[4:]
    else:
        wgu_refs, rest = rest[:quads], rest[quads:]
    x = x_ref[...]
    hidden, width = wd_ref.shape
    if routed:
        gate_pre = sum_pieces(x, wg_refs)
        up_pre = sum_pieces(x, wu_refs)
    else:
        pre = sum_pieces(x, wgu_refs)
        gate_pre, up_pre = pre[:, :hidden], pre[:, hidden:]
    sigma = jax.nn.sigmoid(gate_pre)
    swish = gate_pre * sigma
    active = (swish * up_pre).astype(BF16)
    rest[0][...] = active
    cot = cot_ref[...].astype(F32)
    scale = scale_ref[...]
    grad_result = (scale * cot).astype(BF16)
    rest[1][...] = grad_result
    grad_active = dot_last(grad_result, wd_ref[...])
    grad_up = grad_active * swish
    grad_gate = grad_active * up_pre * (sigma * (1.0 + gate_pre * (1.0 - sigma)))
    result = dot(active, wd_ref[...])
    if routed:
        result = result.astype(BF16).astype(F32)
    inner = jnp.sum(cot * result, axis=1, keepdims=True)
    part = scale * result
    block = width // quads
    if not routed:
        part_ref, grad_ref, inner_ref, both_ref = rest[2:]
        both = jnp.concatenate([grad_gate, grad_up], axis=1).astype(BF16)
        both_ref[...] = both
        part_ref[...] = part.astype(BF16)
        for key in range(quads):
            grad = dot_last(both, wgu_refs[key][...])
            grad_ref[:, key * block : (key + 1) * block] = grad.astype(BF16)
        inner_ref[...] = inner
        return
    part_ref, grad_ref, gate_ref, up_ref = rest[2:]
    grad_gate, grad_up = grad_gate.astype(BF16), grad_up.astype(BF16)
    gate_ref[...] = grad_gate
    up_ref[...] = grad_up
    part_ref[...] = (part + part_in[...].astype(F32)).astype(BF16)
    for key in range(quads):
        cols = slice(key * block, (key + 1) * block)
        grad = dot_last(grad_gate, wg_refs[key][...]) + dot_last(grad_up, wu_refs[key][...])
        grad = grad.astype(BF16).astype(F32) + grad_in[:, cols].astype(F32)
        grad_ref[:, cols] = grad.astype(BF16)
    lane = lane_ref[...]
    extra = jnp.zeros((x.shape[0], LANES), F32)
    for slot, value in enumerate((inner, dot_in[...])):
        high = value.astype(BF16).astype(F32)
        extra = extra + jnp.where(lane == 2 * slot, high, 0.0)
        extra = extra + jnp.where(lane == 2 * slot + 1, value - high, 0.0)
    grad_ref[:, width:] = extra.astype(BF16)


def expert(x, pieces, wd, cot, scale, routed=()):
    rows, width = x.shape
    hidden = wd.shape[0]
    quads = len(pieces) // 2 if routed else len(pieces)
    ins = [rows_spec(width), whole((hidden, width)), rows_spec(width), rows_spec(1)]
    ins += [whole(piece.shape) for piece in pieces]
    outs = [rows_spec(hidden), rows_spec(width), rows_spec(width)]
    shapes = [shaped(rows, hidden, BF16), shaped(rows, width, BF16), shaped(rows, width, BF16)]
    if routed:
        ins += [rows_spec(width), rows_spec(width), rows_spec(1), whole((1, LANES))]
        outs += [rows_spec(width + LANES), rows_spec(hidden), rows_spec(hidden)]
        shapes += [shaped(rows, width + LANES, BF16)] + [shaped(rows, hidden, BF16)] * 2
    else:
        outs += [rows_spec(width), rows_spec(1), rows_spec(2 * hidden)]
        shapes += [shaped(rows, width, BF16), shaped(rows, 1, F32), shaped(rows, 2 * hidden, BF16)]
    return call(
        functools.partial(expert_kernel, bool(routed), quads),
        (rows // TILE,),
        ins,
        outs,
        shapes,
        60,
        12 * rows * width * hidden,
        name="expert" if routed else "shared",
    )(x, wd, cot, scale, *pieces, *routed)


def local(
    residual_in,
    attention_gain,
    query_weight,
    query_bias,
    key_weight,
    key_bias,
    value_weight,
    value_bias,
    output_weight,
    feedforward_gain,
    router_weight,
    shared_logit_weight,
    shared_gate_weight,
    shared_up_weight,
    shared_down_weight,
    expert_gate,
    expert_up,
    expert_down,
    cotangent,
    expert_index,
    token_live,
    document_lengths,
):
    ep_count = lax.axis_size("ep")
    grp_count = lax.axis_size("grp")
    quads = grp_count // 2
    rows_dev, width = residual_in.shape
    group_rows = rows_dev * ep_count
    pair_rows = 2 * group_rows
    seq_len = group_rows * grp_count // SEQS
    expert_count = expert_gate.shape[0] * ep_count
    ffe = expert_gate.shape[2]
    ffs_half = shared_gate_weight.shape[1] // 2
    grp = lax.axis_index("grp")
    ep = lax.axis_index("ep")
    core = grp % 2
    quad = grp // 2
    back = -(-WINDOW // pair_rows)
    heads = query_weight.shape[1] // HDIM // 2
    head_width = heads * HDIM
    up_order = quad_bits()
    down_order = up_order[::-1]

    block = width // quads
    cut = len(up_order) // 2
    up_one, up_two = up_order[:cut], up_order[cut:]
    down_one, down_two = down_order[: len(down_order) - cut], down_order[len(down_order) - cut :]
    ep_masks = [1 << b for b in range(ep_count.bit_length() - 1)]
    quad_masks = [2 * bit for bit in up_order]
    seq_groups = grp_count // SEQS
    experts = jnp.arange(expert_count, dtype=jnp.int32)
    ed_cut = width // 2

    def shifted(values, steps):
        route = [
            (i, i + 2 * steps)
            for i in range(grp_count)
            if 0 <= i + 2 * steps < grp_count and i // seq_groups == (i + 2 * steps) // seq_groups
        ]
        return lax.ppermute(values, "grp", route)

    def gathered(values):
        return lax.all_gather(values, "ep", axis=0, tiled=True)

    def scattered(values):
        return lax.psum_scatter(values, "ep", scatter_dimension=0, tiled=True).astype(F32)

    def core_sum(values):
        keep, other = split_core(values, core, 0)
        return (keep.astype(F32) + across(other, 1).astype(F32)).astype(BF16)

    def row_grads(rows, grads, keys=range(quads)):
        return {
            k: dot_first(rows[:, k * block : (k + 1) * block], grads).astype(BF16) for k in keys
        }

    def column_grads(acts, grads):
        return {
            k: dot_first(acts, part).astype(BF16)
            for k, part in take_quads(grads, quad, quads, 1).items()
        }

    hidden_in = residual_in.astype(F32)
    grad_out = cotangent.astype(F32)
    gain_one = attention_gain.astype(F32)
    gain_two = feedforward_gain.astype(F32)
    router_all = jnp.concatenate([router_weight, shared_logit_weight[:, None]], axis=1)
    router_flipped = flip_columns(router_all.T, quad).T
    scale_one = norm_scale(hidden_in)
    unit_one = hidden_in * scale_one
    normed_one = (unit_one * gain_one).astype(BF16)
    group_one = gathered(flip_columns(normed_one, quad))

    qk_keep, qk_other = zip(
        *[split_core(weight, core, 1) for weight in (query_weight, key_weight, value_weight)]
    )
    qkv_keep, qkv_other = jnp.concatenate(qk_keep, 1), jnp.concatenate(qk_other, 1)
    qkv_block = merge_core(qkv_keep, across(qkv_other, 1), core, 0)
    qkv_cut = qkv_block.shape[1] // 2
    qkv_a = {0: qkv_block[:, :qkv_cut]}
    qkv_b = {0: qkv_block[:, qkv_cut:]}
    (
        qkv_a, qkv_b, output_weight, shared_gate_weight, shared_up_weight, shared_down_weight,
        expert_gate, expert_up, expert_down,
    ) = together(
        qkv_a, qkv_b, output_weight, shared_gate_weight, shared_up_weight, shared_down_weight,
        expert_gate, expert_up, expert_down,
    )
    qkv_a_one, qkv_a_two = gather_quads(qkv_a, up_one), gather_quads(qkv_a, up_two)
    qkv_b_one, qkv_b_two = gather_quads(qkv_b, down_one), gather_quads(qkv_b, down_two)

    o_keep, o_other = split_core(output_weight, core, 0)
    o_block = merge_core(o_keep, across(o_other, 1), core, 1)
    sg_keep, sg_other = split_core(shared_gate_weight, core, 1)
    su_keep, su_other = split_core(shared_up_weight, core, 1)
    gu_keep = jnp.concatenate([sg_keep, su_keep], axis=1)
    gu_other = jnp.concatenate([sg_other, su_other], axis=1)
    gu_block = merge_core(gu_keep, across(gu_other, 1), core, 0)
    sd_keep, sd_other = split_core(shared_down_weight, core, 0)
    sd_block = merge_core(sd_keep, across(sd_other, 1), core, 1)

    def expert_block(weight):
        keep, other = split_core(weight, core, 0)
        return merge_core(keep[0], across(other[0], 1), core, 0)

    eg_block, eu_block, ed_block = [
        expert_block(weight) for weight in (expert_gate, expert_up, expert_down)
    ]
    eda_block, edb_block = ed_block[:, :ed_cut], ed_block[:, ed_cut:]

    (
        qkv_a_one, qkv_a_two, qkv_b_one, qkv_b_two, o_block, gu_block, sd_block, eg_block, eu_block,
        eda_block, edb_block,
    ) = together(
        qkv_a_one, qkv_a_two, qkv_b_one, qkv_b_two, o_block, gu_block, sd_block, eg_block, eu_block,
        eda_block, edb_block,
    )
    qkv_a_rest = gather_rest(qkv_a_one, up_two)
    qkv_b_rest = gather_rest(qkv_b_one, down_two)
    o_one, o_two = gather_quads({0: o_block}, down_one), gather_quads({0: o_block}, down_two)
    sd_one, sd_two = gather_quads({0: sd_block}, down_one), gather_quads({0: sd_block}, down_two)
    chosen = (
        (expert_index[:, :, None] == experts[None, None, :]) & (token_live[:, None, None] > 0)
    ).any(axis=1)
    cot_packed = jnp.concatenate(
        [cotangent, jnp.pad(chosen.astype(BF16), ((0, 0), (0, LANES - expert_count)))], axis=1
    )
    chosen = chosen.astype(F32)
    bias = jnp.concatenate(
        [split_core(b, core, 0)[0] for b in (query_bias, key_bias, value_bias)]
    ).astype(F32)[None, :]
    key_place = (quad - back) * pair_rows + jnp.arange((back + 1) * pair_rows, dtype=jnp.int32)
    query_place = key_place[back * pair_rows :]
    _, position = doc_layout(document_lengths, seq_len, query_place)
    low = jnp.maximum(query_place - position, query_place - WINDOW + 1)[:, None]
    high, key_place = query_place[:, None], key_place[None, :]
    cosine, sine = rope_tables(position)
    (
        group_one, qkv_a, qkv_b, o_one, o_two, sd_one, sd_two, gu_block, eg_block, eu_block,
        eda_block, edb_block, cot_packed, bias, cosine, sine, low, high,
    ) = together(
        group_one, qkv_a_one | qkv_a_two | qkv_a_rest, qkv_b_one | qkv_b_two | qkv_b_rest, o_one,
        o_two, sd_one, sd_two, gu_block, eg_block, eu_block, eda_block, edb_block, cot_packed, bias,
        cosine, sine, low, high,
    )

    rows_one = merge_core(group_one, across(group_one, 1), core, 0)
    gu_two = gather_quads({0: gu_block}, up_two)
    o_rest, sd_rest = gather_rest(o_one, down_two), gather_rest(sd_one, down_two)
    cot_group = gathered(cot_packed)
    qkv_a, qkv_b = listed(qkv_a), listed(qkv_b)
    query, key_value = project(rows_one, qkv_a, qkv_b, bias, cosine, sine, heads)

    query, key_value, o_rest, sd_rest = together(query, key_value, o_rest, sd_rest)
    before = [shifted(key_value, step) for step in range(back, 0, -1)]
    o_full = place_quads(o_one | o_two | o_rest, quad, 1)
    query, before, gu_two, edb_block, o_full = together(query, before, gu_two, edb_block, o_full)
    edb_one, edb_two = gather_quads({0: edb_block}, down_one), gather_quads({0: edb_block}, down_two)
    attended, log_total = attend(query, before, key_value, key_place, low, high)
    branch = dot(attended, o_full).astype(BF16)
    branch, cot_group, edb_one, edb_two = together(branch, cot_group, edb_one, edb_two)
    branch = core_sum(branch)
    branch, gu_block, eu_block, eda_block, cot_group = together(
        branch, gu_block, eu_block, eda_block, cot_group
    )
    branch_sum = scattered(branch)
    cot_other = across(cot_group, 1)
    gu_one = gather_quads({0: gu_block}, up_one)
    eda_one, eda_two = gather_quads({0: eda_block}, up_one), gather_quads({0: eda_block}, up_two)
    eu_one = gather_quads({0: eu_block}, down_one)
    sd_full = place_quads(sd_one | sd_two | sd_rest, quad, 1)
    ed_full = jnp.zeros((eda_block.shape[0] * quads, width), BF16)
    ed_full = place_quads(edb_one | edb_two, quad, 0, ed_full, ed_cut)
    branch_sum, cot_other, gu_one, eda_one, eda_two, eu_one, eg_block, edb_one, sd_full, ed_full = (
        together(
            branch_sum, cot_other, gu_one, eda_one, eda_two, eu_one, eg_block, edb_one, sd_full,
            ed_full,
        )
    )

    eg_one = gather_quads({0: eg_block}, up_one)
    edb_rest = gather_rest(edb_one, down_two)
    gu_rest, eda_rest = gather_rest(gu_one, up_two), gather_rest(eda_one, up_two)
    mixed = hidden_in + branch_sum
    scale_two = norm_scale(mixed)
    unit_two = mixed * scale_two
    normed_two = (unit_two * gain_two).astype(BF16)
    group_two = gathered(flip_columns(normed_two, quad))
    cot_rows = merge_core(cot_group, cot_other, core, 0)
    ed_full = place_quads(eda_one | eda_two, quad, 0, ed_full)
    (
        group_two, eg_one, edb_rest, gu_rest, eda_rest, eu_block, eg_block, eu_one, cot_rows,
        ed_full,
    ) = together(
        group_two, eg_one, edb_rest, gu_rest, eda_rest, eu_block, eg_block, eu_one, cot_rows,
        ed_full,
    )
    eu_two, eg_two = gather_quads({0: eu_block}, down_two), gather_quads({0: eg_block}, up_two)
    eu_rest, eg_rest = gather_rest(eu_one, down_two), gather_rest(eg_one, up_two)
    rows_two = merge_core(group_two, across(group_two, 1), core, 0)
    gu_pieces = listed(gu_one | gu_two | gu_rest)

    def router(rows, weight):
        logits = dot(rows, weight)
        return jax.nn.softmax(logits[:, :expert_count], axis=-1), jax.nn.sigmoid(
            logits[:, expert_count:]
        )

    chosen_rows = cot_rows[:, width : width + expert_count].astype(F32)
    probs_rows, shared_scale_rows = router(rows_two, router_flipped)
    router_probs, shared_scale = router(normed_two, router_all)
    mine = (experts == ep * 2 + core).astype(F32)[None, :]
    gate = jnp.sum(probs_rows * chosen_rows * mine, axis=1, keepdims=True)

    shared_active, grad_shared_out, part, grad_part, shared_dot, grad_gu = expert(
        rows_two, gu_pieces, sd_full, cot_rows, shared_scale_rows
    )
    grad_part, part, eu_two, eg_two, eu_rest, eg_rest, eda_rest, edb_rest, ed_full = together(
        grad_part, part, eu_two, eg_two, eu_rest, eg_rest, eda_rest, edb_rest, ed_full
    )
    ed_full = place_quads(eda_rest, quad, 0, ed_full)
    ed_full = place_quads(edb_rest, quad, 0, ed_full, ed_cut)
    gu_cut = 2 * ffs_half * 3 // 4 // LANES * LANES
    gua_grad = row_grads(rows_two, grad_gu[:, :gu_cut])
    gub_grad = row_grads(rows_two, grad_gu[:, gu_cut:])
    sd_grad = column_grads(shared_active, grad_shared_out)
    grad_part, eg_pieces, eu_pieces, ed_full, gua_grad, gub_grad, sd_grad = together(
        grad_part, eg_one | eg_two | eg_rest, eu_one | eu_two | eu_rest, ed_full, gua_grad,
        gub_grad, sd_grad,
    )
    up_keys = [key for key in gua_grad if key & up_one[0]]
    down_keys = [key for key in gua_grad if key & down_one[0]]
    gua_sent = send_quads(gua_grad, up_one[0], up_keys)
    gub_sent = send_quads(gub_grad, down_one[0], down_keys)
    sd_sent = send_quads(sd_grad, down_one[0], down_keys)

    lanes = jnp.arange(LANES, dtype=jnp.int32)
    lanes = jnp.where(lanes % expert_count == ep * 2 + core, lanes // expert_count, -1)[None, :]
    active, grad_result, forward_part, packed, grad_gate_pre, grad_up_pre = expert(
        rows_two,
        listed(eg_pieces) + listed(eu_pieces),
        ed_full,
        cot_rows,
        gate,
        (part, grad_part, shared_dot, lanes),
    )
    packed, forward_part, gua_sent, gub_sent, sd_sent, gua_grad, gub_grad, sd_grad = together(
        packed, forward_part, gua_sent, gub_sent, sd_sent, gua_grad, gub_grad, sd_grad
    )
    packed = core_sum(packed)
    (
        packed, gua_grad, gub_grad, sd_grad, active, grad_result, grad_gate_pre, grad_up_pre,
    ) = together(
        packed, gua_grad, gub_grad, sd_grad, active, grad_result, grad_gate_pre, grad_up_pre,
    )
    spread = scattered(packed)
    gua_grad = reduce_quads(add_quads(gua_grad, gua_sent, up_one[0]), up_one[1:])
    gub_grad = reduce_quads(add_quads(gub_grad, gub_sent, down_one[0]), down_one[1:])
    sd_grad = reduce_quads(add_quads(sd_grad, sd_sent, down_one[0]), down_one[1:])
    ed_grad = take_quads(dot_first(active, grad_result).astype(BF16), quad, quads, 0)
    eda_grad = {k: v[:, :ed_cut] for k, v in ed_grad.items()}
    edb_grad = {k: v[:, ed_cut:] for k, v in ed_grad.items()}
    gua_grad = reduce_quads(gua_grad, up_two)[0]
    gub_grad = reduce_quads(gub_grad, down_two)[0]
    sd_grad = reduce_quads(sd_grad, down_two)[0]
    eda_sent = send_quads(eda_grad, up_one[0], up_keys)
    edb_sent = send_quads(edb_grad, down_one[0], down_keys)
    half = len(up_keys) // 2
    keys = range(quads)
    eg_grad = row_grads(rows_two, grad_gate_pre, up_keys)
    eu_grad = row_grads(rows_two, grad_up_pre, down_keys[:half])
    spread, eg_grad, eu_grad = together(spread, eg_grad, eu_grad)

    grad_normed_two = flip_columns(spread[:, :width], quad)
    side = spread[:, width : width + 4 * expert_count].reshape(rows_dev, 4, expert_count)
    grad_gate_own = side[:, 0] + side[:, 1]
    shared_dot_own = jnp.sum(side[:, 2] + side[:, 3], axis=1, keepdims=True)
    grad_logit = shared_dot_own * shared_scale * (1.0 - shared_scale)
    grad_probs = grad_gate_own * chosen
    grad_logits = router_probs * (
        grad_probs - jnp.sum(router_probs * grad_probs, axis=-1, keepdims=True)
    )
    grad_router = jnp.concatenate([grad_logits, grad_logit], axis=1)
    router_grad = dot_first(normed_two.astype(F32), grad_router)
    grad_normed_two = grad_normed_two + dot_last(grad_router, router_all.astype(F32))
    grad_norm_part, ff_gain_grad = norm_backward(grad_normed_two, unit_two, scale_two, gain_two)
    grad_mixed = grad_out + grad_norm_part
    (
        branch_low, eda_grad, eda_sent, edb_grad, edb_sent, gua_grad, gub_grad, sd_grad,
        grad_gate_pre, grad_up_pre, eg_grad, eu_grad, forward_part,
    ) = together(
        grad_mixed.astype(BF16), eda_grad, eda_sent, edb_grad, edb_sent, gua_grad, gub_grad, sd_grad,
        grad_gate_pre, grad_up_pre, eg_grad, eu_grad, forward_part,
    )
    group_branch = gathered(branch_low)
    eg_sent = send_quads(eg_grad, up_one[0], up_keys[:half])
    eu_sent = send_quads(eu_grad, down_one[0], down_keys[:half])
    eda_grad = reduce_quads(add_quads(eda_grad, eda_sent, up_one[0]), up_one[1:])
    edb_grad = reduce_quads(add_quads(edb_grad, edb_sent, down_one[0]), down_one[1:])
    eda_grad = reduce_quads(eda_grad, up_two)[0]
    edb_grad = reduce_quads(edb_grad, down_two)[0]
    eg_grad |= row_grads(rows_two, grad_gate_pre, [k for k in keys if k not in eg_grad])
    eu_grad |= row_grads(rows_two, grad_up_pre, [k for k in keys if k not in eu_grad])
    group_branch, forward_part, eg_grad, eg_sent, eu_grad, eu_sent, eda_grad, edb_grad = together(
        group_branch, forward_part, eg_grad, eg_sent, eu_grad, eu_sent, eda_grad, edb_grad
    )
    grad_branch = merge_core(group_branch, across(group_branch, 1), core, 0)
    eg_sent |= send_quads(eg_grad, up_one[0], up_keys[half:])
    eu_sent |= send_quads(eu_grad, down_one[0], down_keys[half:])

    layer_sum = scattered(core_sum(forward_part))
    grad_attended = dot_last(grad_branch, o_full).astype(BF16)
    grad_query, grad_own, *grad_before = attend_back(
        query, grad_attended, log_total, before, key_value, key_place, low, high, cosine, sine
    )
    def back_to_cores(summed, cut_axis, join_axis):
        keep, other = split_core(summed, core, cut_axis)
        return merge_core(keep, across(other, 1), core, join_axis).astype(F32)

    def back_to_experts(summed):
        keep, other = split_core(summed, core, 0)
        arrived = across(other, 1)
        return jnp.stack(
            [jnp.where(core == 0, keep, arrived), jnp.where(core == 0, arrived, keep)]
        ).astype(F32)

    (
        grad_query, grad_before, grad_branch, eg_grad, eu_grad, gua_grad, gub_grad, sd_grad,
        eda_grad, edb_grad,
    ) = together(
        grad_query, grad_before, grad_branch, eg_grad, eu_grad, gua_grad, gub_grad, sd_grad,
        eda_grad, edb_grad,
    )
    arrived = [shifted(sent, step - back) for step, sent in enumerate(grad_before)]
    eg_grad = reduce_quads(add_quads(eg_grad, eg_sent, up_one[0]), up_one[1:])
    eu_grad = reduce_quads(add_quads(eu_grad, eu_sent, down_one[0]), down_one[1:])
    eg_rest = send_quads(eg_grad, up_two[0], [key for key in eg_grad if key & up_two[0]])
    gu_grad = jnp.concatenate([gua_grad, gub_grad], axis=1)
    sg_grad = back_to_cores(gu_grad[:, :ffs_half], 0, 1)
    su_grad = back_to_cores(gu_grad[:, ffs_half:], 0, 1)
    sd_grad = back_to_cores(sd_grad, 1, 0)
    o_grad = column_grads(attended, grad_branch)
    o_sent = send_quads(o_grad, down_order[0], down_keys)
    arrived, eg_grad, eu_grad, o_grad, sg_grad, su_grad, sd_grad, eda_grad, edb_grad = together(
        arrived, eg_grad, eu_grad, o_grad, sg_grad, su_grad, sd_grad, eda_grad, edb_grad
    )
    eu_keys = [key for key in eu_grad if key & down_two[0]]
    eu_cut = eu_block.shape[0] // 2
    eu_rest = send_quads({key: eu_grad[key][:eu_cut] for key in eu_keys}, down_two[0], eu_keys)
    grad_lin, partial, att_gain_part, bias_part = collect(
        grad_query, grad_own, cosine, sine, rows_one, arrived, qkv_a, qkv_b
    )
    partial, eg_rest, eu_rest, eu_grad, o_grad, o_sent = together(
        partial, eg_rest, eu_rest, eu_grad, o_grad, o_sent
    )
    partial_sum = core_sum(partial)

    (
        partial_sum, grad_lin, att_gain_part, bias_part, eg_grad, eg_rest, eu_grad, o_grad, o_sent,
    ) = together(
        partial_sum, grad_lin, att_gain_part, bias_part, eg_grad, eg_rest, eu_grad, o_grad, o_sent,
    )
    grad_normed_one = scattered(partial_sum)
    eu_last = send_quads({key: eu_grad[key][eu_cut:] for key in eu_keys}, down_two[0], eu_keys)
    grad_lin_a, grad_lin_b = grad_lin[:, :qkv_cut], grad_lin[:, qkv_cut:]
    qkv_a_grad = reduce_quads(row_grads(rows_one, grad_lin_a), up_order)[0]
    qkv_b_grad = reduce_quads(row_grads(rows_one, grad_lin_b), down_order)[0]
    o_grad = add_quads(o_grad, o_sent, down_order[0])
    o_grad = reduce_quads(o_grad, down_order[1:])[0]
    att_gain_part = flip_columns(att_gain_part[0], quad) / gain_one
    late = jnp.concatenate([bias_part[0], att_gain_part, ff_gain_grad, router_grad.T.reshape(-1)])
    late = sum_everywhere(late, quad_masks, [])
    bias_part = late[: 3 * head_width]
    late = sum_everywhere(late[3 * head_width :], [1], ep_masks)
    (
        grad_normed_one, o_grad, qkv_a_grad, qkv_b_grad, bias_part, late, eu_last, eg_grad, eg_rest,
        eda_grad, edb_grad, layer_sum,
    ) = together(
        grad_normed_one, o_grad, qkv_a_grad, qkv_b_grad, bias_part, late, eu_last, eg_grad, eg_rest,
        eda_grad, edb_grad, layer_sum,
    )
    eg_grad = reduce_quads(add_quads(eg_grad, eg_rest, up_two[0]), up_two[1:])[0]
    eg_grad = back_to_experts(eg_grad)
    ed_grad = back_to_experts(jnp.concatenate([eda_grad, edb_grad], axis=1))
    layer_out = (mixed + layer_sum).astype(BF16)
    bias_mine = merge_core(
        bias_part.reshape(3, head_width), across(bias_part, 1).reshape(3, head_width), core, 1
    )
    eu_rest = {key: jnp.concatenate([eu_rest[key], eu_last[key]], axis=0) for key in eu_rest}
    eu_grad = reduce_quads(add_quads(eu_grad, eu_rest, down_two[0]), down_two[1:])[0]
    qkv_grad = jnp.concatenate([qkv_a_grad, qkv_b_grad], axis=1)
    att_gain_grad, ff_gain_grad = late[:width], late[width : 2 * width]
    router_grad = late[2 * width :].reshape(expert_count + 1, width)
    grad_norm_one, _ = norm_backward(
        flip_columns(grad_normed_one, quad), unit_one, scale_one, gain_one
    )
    input_grad = grad_mixed + grad_norm_one
    q_grad, k_grad, v_grad = [
        back_to_cores(qkv_grad[:, part * head_width : (part + 1) * head_width], 0, 1)
        for part in range(3)
    ]
    return (
        layer_out,
        input_grad,
        att_gain_grad,
        q_grad,
        bias_mine[0],
        k_grad,
        bias_mine[1],
        v_grad,
        bias_mine[2],
        back_to_cores(o_grad, 1, 0),
        ff_gain_grad,
        router_grad[:expert_count].T,
        router_grad[expert_count],
        sg_grad,
        su_grad,
        sd_grad,
        eg_grad,
        back_to_experts(eu_grad),
        ed_grad,
    )


def solution(mesh):
    tokens = P(("grp", "ep"), None)
    rows, columns, experts = P("grp", "ep"), P("ep", "grp"), P("ep", "grp", None)
    in_specs = (
        tokens, P(), rows, P("ep"), rows, P("ep"), rows, P("ep"), columns, P(), P(), P(),
        rows, rows, columns, experts, experts, experts, tokens, tokens, P(("grp", "ep")), P(),
    )
    out_specs = (
        tokens, tokens, P(), rows, P("ep"), rows, P("ep"), rows, P("ep"), columns, P(), P(), P(),
        rows, rows, columns, experts, experts, experts,
    )
    return jax.shard_map(local, mesh=mesh, in_specs=in_specs, out_specs=out_specs, check_vma=False)
```

```python
import functools

import jax
import jax.numpy as jnp
from jax import lax
from jax.experimental import pallas as pl
from jax.experimental.pallas import tpu as pltpu
from jax.sharding import PartitionSpec as P

HDIM = 128
SEQS = 2
DOCS = 4
WINDOW = 1024
EPS = 1e-06
ROPE_BASE = 1000000.0
MASKED = -1e30
F32 = jnp.float32
BF16 = jnp.bfloat16
TILE = 256
LANES = 128
MIB = 1 << 20


def dot(left, right):
    return jnp.dot(left, right, preferred_element_type=F32)


def dot_last(left, right):
    return lax.dot_general(left, right, (((1,), (1,)), ((), ())), preferred_element_type=F32)


def dot_first(left, right):
    return lax.dot_general(left, right, (((0,), (0,)), ((), ())), preferred_element_type=F32)


def across(block, mask):
    count = lax.axis_size("grp")
    return lax.ppermute(block, "grp", [(i, i ^ mask) for i in range(count)])


def quad_bits():
    return [1 << b for b in range((lax.axis_size("grp") // 2).bit_length() - 1)]


def flip_columns(values, quad):
    quads = lax.axis_size("grp") // 2
    axis = values.ndim - 1
    block = values.shape[axis] // quads
    return jnp.concatenate(
        [
            lax.dynamic_slice_in_dim(values, (quad ^ key) * block, block, axis)
            for key in range(quads)
        ],
        axis=axis,
    )


def gather_quads(pieces, order):
    pieces = dict(pieces)
    for bit in order:
        for key, piece in list(pieces.items()):
            pieces[key | bit] = across(piece, 2 * bit)
    return pieces


def add_low(left, right):
    return (left.astype(F32) + right.astype(F32)).astype(BF16)


def first_sum(parts, arrived):
    half = parts[0].shape[0]
    if len(arrived) == 1:
        arrived = (arrived[0][:half], arrived[0][half:])
    return add_low(parts[0], arrived[0]), add_low(parts[1], arrived[1])


def rest_parts(kept, arrived, order):
    for bit in order[2:]:
        stack = add_rows(kept, arrived)
        half = stack.shape[0] // 2
        kept, arrived = stack[:half], across(stack[half:], 2 * bit)
    return kept, arrived


def together(*values):
    return lax.optimization_barrier(values)


def sum_everywhere(values, masks_grp, masks_ep):
    for mask in masks_grp:
        values = values + across(values, mask)
    count = lax.axis_size("ep")
    for mask in masks_ep:
        values = values + lax.ppermute(values, "ep", [(i, i ^ mask) for i in range(count)])
    return values


def gather_rest(pieces, order):
    found = {}
    for key, piece in pieces.items():
        if key:
            found.update({key | k: v for k, v in gather_quads({0: piece}, order).items()})
    return found


def listed(pieces):
    return [pieces[key] for key in sorted(pieces)]


def place_quads(pieces, quad, axis, whole=None, other=0):
    size = pieces[0].shape[axis] if whole is None else whole.shape[axis] // (lax.axis_size("grp") // 2)
    if whole is None:
        shape = list(pieces[0].shape)
        shape[axis] = size * len(pieces)
        whole = jnp.zeros(shape, pieces[0].dtype)
    for key in sorted(pieces):
        start = [other, other]
        start[axis] = (quad ^ key) * size
        whole = lax.dynamic_update_slice(whole, pieces[key], start)
    return whole


def take_quads(whole, quad, quads, axis):
    size = whole.shape[axis] // quads
    return {
        key: lax.dynamic_slice_in_dim(whole, (quad ^ key) * size, size, axis)
        for key in range(quads)
    }


def merge_core(kept, arrived, core, axis):
    first = jnp.where(core == 0, kept, arrived)
    second = jnp.where(core == 0, arrived, kept)
    return jnp.concatenate([first, second], axis=axis)


def split_core(values, core, axis):
    half = values.shape[axis] // 2
    first = lax.slice_in_dim(values, 0, half, axis=axis)
    second = lax.slice_in_dim(values, half, 2 * half, axis=axis)
    return jnp.where(core == 0, first, second), jnp.where(core == 0, second, first)


def norm_scale(values):
    return lax.rsqrt(jnp.mean(values * values, axis=-1, keepdims=True) + EPS)


def norm_backward(grad_normed, unit, scale, gain):
    grad_unit = grad_normed * gain
    inner = jnp.mean(grad_unit * unit, axis=-1, keepdims=True)
    return scale * (grad_unit - unit * inner), jnp.sum(grad_normed * unit, axis=0)


def doc_layout(document_lengths, seq_len, index):
    valid = index >= 0
    safe = jnp.maximum(index, 0)
    seq_of = safe // seq_len
    place = safe % seq_len
    seq_count = document_lengths.shape[0]
    picker = (seq_of[:, None] == jnp.arange(seq_count, dtype=jnp.int32)[None, :]).astype(jnp.int32)
    lengths = jnp.sum(picker[:, :, None] * document_lengths[None, :, :], axis=1)
    ends = jnp.cumsum(lengths, axis=1)
    doc = jnp.sum((ends <= place[:, None]).astype(jnp.int32), axis=1)
    earlier = jnp.arange(DOCS, dtype=jnp.int32)[None, :] < doc[:, None]
    before = jnp.sum(jnp.where(earlier, lengths, 0), axis=1)
    return jnp.where(valid, seq_of * DOCS + doc, -1), place - before


def rope_tables(position):
    half = HDIM // 2
    freq = ROPE_BASE ** (-(jnp.arange(half, dtype=F32) * 2.0 / HDIM))
    angle = position.astype(F32)[:, None] * freq[None, :]
    cosine, sine = jnp.cos(angle), jnp.sin(angle)
    return jnp.concatenate([cosine, cosine], axis=1), jnp.concatenate([-sine, sine], axis=1)


def turn(values, cosine, sine):
    return values * cosine + pltpu.roll(values, HDIM // 2, 1) * sine


def call(kernel, grid, ins, outs, shapes, limit, flops, scratch=(), name=None, scalars=0):
    moved = 0
    for shape in shapes:
        moved += shape.size * shape.dtype.itemsize

    def run(*args):
        total = moved + sum(a.size * a.dtype.itemsize for a in args)
        if flops == 0:
            total = 0
        return pl.pallas_call(
            kernel,
            grid_spec=pltpu.PrefetchScalarGridSpec(
                num_scalar_prefetch=scalars,
                grid=grid,
                in_specs=ins,
                out_specs=outs,
                scratch_shapes=scratch,
            ),
            out_shape=shapes,
            compiler_params=pltpu.CompilerParams(vmem_limit_bytes=limit * MIB),
            cost_estimate=pl.CostEstimate(
                flops=flops, bytes_accessed=total, transcendentals=0
            ),
            name=name,
        )(*args)

    return run


def whole(shape):
    return pl.BlockSpec(shape, lambda *_: (0,) * len(shape), pipeline_mode=pl.Buffered(1))


def rows_spec(columns, tile=TILE):
    return pl.BlockSpec((tile, columns), lambda i, *_: (i, 0))


def turned(step, core, count):
    return (step + (count // 2) * core) % count


def turned_spec(columns, count):
    return pl.BlockSpec((TILE, columns), lambda i, core: (turned(i, core[0], count), 0))


def halves_specs(columns, count):
    half = count // 2
    specs = [
        pl.BlockSpec((TILE, columns), lambda i, core: (jnp.minimum(i, half), 0)),
        pl.BlockSpec((TILE, columns), lambda i, core: (jnp.maximum(i - half, 0), 0)),
    ]
    return specs, [shaped((half + 1) * TILE, columns, BF16), shaped(half * TILE, columns, BF16)]


def add_kernel(left_ref, right_ref, out_ref):
    out_ref[...] = (left_ref[...].astype(F32) + right_ref[...].astype(F32)).astype(BF16)


def add_rows(left, right):
    rows, columns = right.shape
    tile = rows // 4 if rows % 64 == 0 else rows
    return call(
        add_kernel,
        (rows // tile,),
        [rows_spec(columns, tile)] * 2,
        [rows_spec(columns, tile)],
        [shaped(rows, columns, BF16)],
        16,
        0,
        name="add_rows",
    )(left, right)[0]


def finish_kernel(core_ref, kept_ref, arrived_ref, mine_ref, other_ref):
    total = (kept_ref[...].astype(F32) + arrived_ref[...].astype(F32)).astype(BF16)

    @pl.when(pl.program_id(0) == 0)
    def _():
        other_ref[...] = total

    @pl.when(pl.program_id(0) == 1)
    def _():
        mine_ref[...] = total


def finish(core, kept, arrived, axis):
    rows, columns = kept.shape
    size = (rows // 2, columns) if axis == 0 else (rows, columns // 2)
    if size[0] % 16 or (axis == 1 and size[1] % LANES):
        return split_core(add_low(kept, arrived), core[0], axis)

    def index(i, core):
        half = jnp.where(i == 0, 1 - core[0], core[0])
        return (half, 0) if axis == 0 else (0, half)

    return call(
        finish_kernel,
        (2,),
        [pl.BlockSpec(size, index)] * 2,
        [pl.BlockSpec(size, lambda i, core: (0, 0))] * 2,
        [shaped(*size, BF16)] * 2,
        24,
        0,
        name="finish",
        scalars=1,
    )(core, kept, arrived)


def merge_kernel(core_ref, mine_ref, arrived_ref, out_ref):
    own = pl.program_id(0) == core_ref[0]

    @pl.when(own)
    def _():
        out_ref[...] = mine_ref[...].astype(F32).reshape(out_ref.shape)

    @pl.when(~own)
    def _():
        out_ref[...] = arrived_ref[...].astype(F32).reshape(out_ref.shape)


def merge(core, mine, arrived, axis, part=0, parts=1):
    rows, columns = mine.shape
    columns = columns // parts
    if axis is None:
        shape, size, index = (2, rows, columns), (1, rows, columns), lambda i, core: (i, 0, 0)
    elif axis == 0:
        shape, size, index = (2 * rows, columns), (rows, columns), lambda i, core: (i, 0)
    else:
        shape, size, index = (rows, 2 * columns), (rows, columns), lambda i, core: (0, i)
    return call(
        merge_kernel,
        (2,),
        [pl.BlockSpec((rows, columns), lambda i, core: (0, part))] * 2,
        [pl.BlockSpec(size, index)],
        [jax.ShapeDtypeStruct(shape, F32)],
        24,
        0,
        name="merge",
        scalars=1,
    )(core[None], mine, arrived)[0]


def shaped(rows, columns, dtype):
    return jax.ShapeDtypeStruct((rows, columns), dtype)


def sum_pieces(x, refs):
    block = x.shape[1] // len(refs)
    total = dot(x[:, :block], refs[0][...])
    for key in range(1, len(refs)):
        total = total + dot(x[:, key * block : (key + 1) * block], refs[key][...])
    return total


def project_kernel(heads, quads, x_ref, bias_ref, cos_ref, sin_ref, *rest):
    wa_refs, wb_refs, (q_ref, kv_ref) = rest[:quads], rest[quads : 2 * quads], rest[2 * quads :]
    x = x_ref[...]
    lin = jnp.concatenate([sum_pieces(x, wa_refs), sum_pieces(x, wb_refs)], axis=1) + bias_ref[...]
    cosine, sine = cos_ref[...], sin_ref[...]
    for head in range(3 * heads):
        part = lin[:, head * HDIM : (head + 1) * HDIM]
        if head < 2 * heads:
            part = turn(part, cosine, sine)
        if head < heads:
            q_ref[:, head * HDIM : (head + 1) * HDIM] = part.astype(BF16)
        else:
            kv_ref[:, (head - heads) * HDIM : (head - heads + 1) * HDIM] = part.astype(BF16)


def project(x, wa, wb, bias, cosine, sine, heads):
    rows, width = x.shape
    quads, (block, cut) = len(wa), wa[0].shape
    return call(
        functools.partial(project_kernel, heads, quads),
        (rows // TILE,),
        [rows_spec(width), whole((1, 2 * cut))]
        + [rows_spec(HDIM)] * 2
        + [whole((block, cut))] * (2 * quads),
        [rows_spec(heads * HDIM), rows_spec(2 * heads * HDIM)],
        [shaped(rows, heads * HDIM, BF16), shaped(rows, 2 * heads * HDIM, BF16)],
        32,
        4 * rows * width * cut,
        name="project",
    )(x, bias, cosine, sine, *wa, *wb)


def window_keys(before_refs, own_ref, place, pair_rows, step):
    parts = []
    start = step * TILE
    reach = -WINDOW + start
    for back, ref in enumerate(before_refs):
        first = -(len(before_refs) - back) * pair_rows
        low = max(reach - first, 0)
        if low < pair_rows:
            parts.append(ref[low:, place])
    parts.append(own_ref[max(reach, 0) : start + TILE, place])
    return jnp.concatenate(parts, axis=0) if len(parts) > 1 else parts[0]


def probabilities(query, keys, key_place, low, high, peak):
    scores = dot_last(query, keys) * HDIM ** (-0.5)
    scores = jnp.where((key_place >= low) & (key_place <= high), scores, MASKED)
    if peak is None:
        top = jnp.max(scores, axis=1, keepdims=True)
        weights = jnp.exp(scores - top)
        total = jnp.sum(weights, axis=1, keepdims=True)
        return weights / total, top + jnp.log(total)
    return jnp.exp(scores - peak), peak


def attend_kernel(back, pair_rows, heads, q_ref, *rest):
    before, (own_ref, place_ref, low_ref, high_ref, out_ref, log_ref) = rest[:back], rest[back:]
    for head in range(heads):
        cols = slice(head * HDIM, (head + 1) * HDIM)
        value_cols = slice((heads + head) * HDIM, (heads + head + 1) * HDIM)
        for step in range(pair_rows // TILE):
            rows = slice(step * TILE, (step + 1) * TILE)
            first = back * pair_rows - WINDOW + step * TILE
            places = place_ref[:, max(first, 0) : back * pair_rows + (step + 1) * TILE]
            keys = window_keys(before, own_ref, cols, pair_rows, step)
            values = window_keys(before, own_ref, value_cols, pair_rows, step)
            probs, logs = probabilities(
                q_ref[rows, cols], keys, places, low_ref[rows, :], high_ref[rows, :], None
            )
            out_ref[rows, cols] = dot(probs.astype(BF16), values).astype(BF16)
            log_ref[rows, cols] = jnp.broadcast_to(logs, (TILE, HDIM))


def attend(query, before, own, places, low, high):
    rows, columns = query.shape
    heads = columns // HDIM
    back = len(before)
    return call(
        functools.partial(attend_kernel, back, rows, heads),
        (),
        [pl.BlockSpec(memory_space=pltpu.VMEM)] * (5 + back),
        [pl.BlockSpec(memory_space=pltpu.VMEM)] * 2,
        [shaped(rows, columns, BF16), shaped(rows, columns, F32)],
        40,
        4 * rows * columns * (WINDOW + TILE),
        name="attend",
    )(query, *before, own, places, low, high)


def attend_back_kernel(back, pair_rows, heads, q_ref, grad_ref, log_ref, *rest):
    before = rest[:back]
    own_ref, place_ref, low_ref, high_ref, cos_ref, sin_ref = rest[back : back + 6]
    dq_ref, own_out = rest[back + 6 : back + 8]
    before_out = rest[back + 8 : 2 * back + 8]
    total_ref = rest[-1]
    total_ref[...] = jnp.zeros_like(total_ref)
    for head in range(heads):
        cols = slice(head * HDIM, (head + 1) * HDIM)
        value_cols = slice((heads + head) * HDIM, (heads + head + 1) * HDIM)
        for step in range(pair_rows // TILE):
            rows = slice(step * TILE, (step + 1) * TILE)
            first = max(back * pair_rows - WINDOW + step * TILE, 0)
            last = back * pair_rows + (step + 1) * TILE
            keys = window_keys(before, own_ref, cols, pair_rows, step)
            values = window_keys(before, own_ref, value_cols, pair_rows, step)
            query, grad = q_ref[rows, cols], grad_ref[rows, cols]
            peak = jnp.concatenate([log_ref[rows, cols]] * ((last - first) // HDIM), axis=1)
            probs, _ = probabilities(
                query, keys, place_ref[:, first:last], low_ref[rows, :], high_ref[rows, :], peak
            )
            grad_probs = dot_last(grad, values)
            inner = jnp.sum(probs * grad_probs, axis=1, keepdims=True)
            grad_scores = (probs * (grad_probs - inner)).astype(BF16)
            grad_query = dot(grad_scores, keys) * HDIM ** (-0.5)
            dq_ref[rows, cols] = turn(grad_query, cos_ref[rows, :], -sin_ref[rows, :]).astype(BF16)
            total_ref[first:last, cols] += dot_first(grad_scores, query) * HDIM ** (-0.5)
            total_ref[first:last, value_cols] += dot_first(probs.astype(BF16), grad)
    own_out[...] = total_ref[back * pair_rows :, :]
    for step in range(back):
        before_out[step][...] = total_ref[step * pair_rows : (step + 1) * pair_rows, :].astype(BF16)


def attend_back(query, grad, logs, before, own, places, low, high, cosine, sine):
    rows, columns = query.shape
    back = len(before)
    return call(
        functools.partial(attend_back_kernel, back, rows, columns // HDIM),
        (),
        [pl.BlockSpec(memory_space=pltpu.VMEM)] * (9 + back),
        [pl.BlockSpec(memory_space=pltpu.VMEM)] * (2 + back),
        [shaped(rows, columns, BF16), shaped(rows, 2 * columns, F32)]
        + [shaped(rows, 2 * columns, BF16)] * back,
        48,
        10 * rows * columns * (WINDOW + TILE),
        scratch=[pltpu.VMEM(((back + 1) * rows, 2 * columns), F32)],
        name="attend_back",
    )(query, grad, logs, *before, own, places, low, high, cosine, sine)


def collect_kernel(heads, back, quads, core_ref, dq_ref, own_ref, cos_ref, sin_ref, x_ref, *rest):
    arrived, wa_refs, wb_refs = rest[:back], rest[back : back + quads], rest[back + quads : back + 2 * quads]
    kept_ref, other_ref, gain_ref, bias_ref, *outs = rest[back + 2 * quads :]
    x_all, grad_all = outs[-2:]
    columns = heads * HDIM
    step = pl.program_id(0)
    total = own_ref[...]
    for ref in arrived:
        total = total + ref[...].astype(F32)
    cosine, sine = cos_ref[...], -sin_ref[...]
    heads_out = [dq_ref[...]]
    for head in range(2 * heads):
        part = total[:, head * HDIM : (head + 1) * HDIM]
        if head < heads:
            part = turn(part, cosine, sine)
        heads_out.append(part.astype(BF16))
    grads = jnp.concatenate(heads_out, axis=1)
    tile = turned(step, core_ref[0], pl.num_programs(0))
    rows = pl.ds(pl.multiple_of(tile * TILE, TILE), TILE)
    x_all[rows, :] = x_ref[...]
    grad_all[rows, :] = grads

    @pl.when(step == 0)
    def _():
        gain_ref[...] = jnp.zeros_like(gain_ref)
        bias_ref[...] = jnp.zeros_like(bias_ref)

    bias_ref[...] += jnp.sum(grads.astype(F32), axis=0, keepdims=True)
    cut = 3 * columns // 2
    block = x_ref.shape[1] // quads
    for key in range(quads):
        cols = slice(key * block, (key + 1) * block)
        part = dot_last(grads[:, :cut], wa_refs[key][...]) + dot_last(grads[:, cut:], wb_refs[key][...])
        kept_ref[:, cols] = part.astype(BF16)
        other_ref[:, cols] = part.astype(BF16)
        gain_ref[:, cols] += jnp.sum(part * x_ref[:, cols].astype(F32), axis=0, keepdims=True)

    @pl.when(step == pl.num_programs(0) - 1)
    def _():
        for key in range(quads):
            weight = dot_first(x_all[:, key * block : (key + 1) * block], grad_all[...]).astype(BF16)
            for part, up in enumerate((True, False)):
                half, index = (int(v) for v in place_of(key, quads, up))
                quarter = quads // 4
                number = 2 if half else index // quarter
                first = (index if half else index % quarter) * block
                outs[part * 3 + number][first : first + block, :] = weight[
                    :, part * cut : (part + 1) * cut
                ]


def collect(core, grad_query, own, cosine, sine, x, arrived, wa, wb):
    rows, columns = grad_query.shape
    width = x.shape[1]
    tiles = rows // TILE
    quads, (block, cut) = len(wa), wa[0].shape
    quarter = width // 4
    fixed = lambda *_: (0, 0)
    halves = halves_specs(width, tiles)
    shapes = [shaped(quarter, cut, BF16), shaped(quarter, cut, BF16), shaped(2 * quarter, cut, BF16)]
    outs = call(
        functools.partial(collect_kernel, columns // HDIM, len(arrived), quads),
        (tiles,),
        [turned_spec(columns, tiles), turned_spec(2 * columns, tiles)]
        + [turned_spec(HDIM, tiles)] * 2
        + [turned_spec(width, tiles)]
        + [turned_spec(2 * columns, tiles)] * len(arrived)
        + [whole((block, cut))] * (2 * quads),
        halves[0]
        + [pl.BlockSpec((1, width), fixed)]
        + [pl.BlockSpec((1, 3 * columns), fixed)]
        + [pl.BlockSpec(shape.shape, fixed) for shape in shapes] * 2,
        halves[1] + [shaped(1, width, F32), shaped(1, 3 * columns, F32)] + shapes * 2,
        60,
        8 * rows * width * cut,
        scratch=[pltpu.VMEM((rows, width), BF16), pltpu.VMEM((rows, 3 * columns), BF16)],
        name="collect",
        scalars=1,
    )(core[None], grad_query, own, cosine, sine, x, *arrived, *wa, *wb)
    return outs[:4], (outs[4:6], outs[6:7]), (outs[7:9], outs[9:])


def expert_kernel(routed, quads, core_ref, x_ref, wd_ref, cot_ref, scale_ref, *rest):
    if routed:
        wg_refs, wu_refs, rest = rest[:quads], rest[quads : 2 * quads], rest[2 * quads :]
        part_in, grad_in, dot_in, lane_ref = rest[:4]
        rest = rest[4:]
    else:
        wgu_refs, rest = rest[:quads], rest[quads:]
    x = x_ref[...]
    hidden, width = wd_ref.shape
    if routed:
        gate_pre = sum_pieces(x, wg_refs)
        up_pre = sum_pieces(x, wu_refs)
    else:
        pre = sum_pieces(x, wgu_refs)
        gate_pre, up_pre = pre[:, :hidden], pre[:, hidden:]
    sigma = jax.nn.sigmoid(gate_pre)
    swish = gate_pre * sigma
    active = (swish * up_pre).astype(BF16)
    rest[0][...] = active
    cot = cot_ref[...].astype(F32)
    scale = scale_ref[...]
    grad_result = (scale * cot).astype(BF16)
    rest[1][...] = grad_result
    grad_active = dot_last(grad_result, wd_ref[...])
    grad_up = grad_active * swish
    grad_gate = grad_active * up_pre * (sigma * (1.0 + gate_pre * (1.0 - sigma)))
    result = dot(active, wd_ref[...])
    if routed:
        result = result.astype(BF16).astype(F32)
    inner = jnp.sum(cot * result, axis=1, keepdims=True)
    part = scale * result
    block = width // quads
    if not routed:
        part_ref, grad_ref, inner_ref, both_ref = rest[2:]
        both = jnp.concatenate([grad_gate, grad_up], axis=1).astype(BF16)
        both_ref[...] = both
        part_ref[...] = part.astype(BF16)
        for key in range(quads):
            grad = dot_last(both, wgu_refs[key][...])
            grad_ref[:, key * block : (key + 1) * block] = grad.astype(BF16)
        inner_ref[...] = inner
        return
    part_refs, grad_refs, gate_ref, up_ref = rest[2:4], rest[4:6], rest[6], rest[7]
    grad_gate, grad_up = grad_gate.astype(BF16), grad_up.astype(BF16)
    gate_ref[...] = grad_gate
    up_ref[...] = grad_up
    part = (part + part_in[...].astype(F32)).astype(BF16)
    for ref in part_refs:
        ref[...] = part
    for key in range(quads):
        cols = slice(key * block, (key + 1) * block)
        grad = dot_last(grad_gate, wg_refs[key][...]) + dot_last(grad_up, wu_refs[key][...])
        grad = (grad.astype(BF16).astype(F32) + grad_in[:, cols].astype(F32)).astype(BF16)
        for ref in grad_refs:
            ref[:, cols] = grad
    lane = lane_ref[...]
    extra = jnp.zeros((x.shape[0], LANES), F32)
    for slot, value in enumerate((inner, dot_in[...])):
        high = value.astype(BF16).astype(F32)
        extra = extra + jnp.where(lane == 2 * slot, high, 0.0)
        extra = extra + jnp.where(lane == 2 * slot + 1, value - high, 0.0)
    for ref in grad_refs:
        ref[:, width:] = extra.astype(BF16)


def expert(core, x, pieces, wd, hidden, cot, scale, routed=()):
    rows, width = x.shape
    tiles = rows // TILE
    quads = len(pieces) // 2 if routed else len(pieces)
    spec = lambda columns: turned_spec(columns, tiles)
    ins = [spec(width), whole((hidden, width)), spec(width), spec(1)]
    ins += [whole(piece.shape) for piece in pieces]
    outs = [spec(hidden), spec(width)]
    shapes = [shaped(rows, hidden, BF16), shaped(rows, width, BF16)]
    if routed:
        ins += [spec(width), spec(width), spec(1), whole((1, LANES))]
        for columns in (width, width + LANES):
            specs, halves = halves_specs(columns, tiles)
            outs, shapes = outs + specs, shapes + halves
        outs += [spec(hidden), spec(hidden)]
        shapes += [shaped(rows, hidden, BF16)] * 2
    else:
        outs += [spec(width), spec(width), spec(1), spec(2 * hidden)]
        shapes += [shaped(rows, width, BF16)] * 2
        shapes += [shaped(rows, 1, F32), shaped(rows, 2 * hidden, BF16)]
    return call(
        functools.partial(expert_kernel, bool(routed), quads),
        (tiles,),
        ins,
        outs,
        shapes,
        60,
        12 * rows * width * hidden,
        name="expert" if routed else "shared",
        scalars=1,
    )(core[None], x, wd, cot, scale, *pieces, *routed)


def reversed_bits(value, count):
    return sum((((value >> k) & 1) << (count - 1 - k) for k in range(count)), 0 * value)


def places(step, quads, up):
    if up:
        return step & 1, reversed_bits(step >> 1, quads.bit_length() - 2)
    half = quads // 2
    return jnp.where(step < half, 0, 1), jnp.where(step < half, step, step - half)


def stack_specs(quads, up, rows, columns, merged):
    quarter = quads // 4

    def spec(half, part):
        def index(step, *_):
            if up:
                return places(step, quads, up)[1] % quarter, 0
            first = half * 2 * quarter + part * quarter
            return jnp.clip(step - first, 0, quarter - 1), 0

        return pl.BlockSpec((rows, columns), index)

    def joined(step, *_):
        if up:
            return places(step, quads, up)[1], 0
        return jnp.clip(step - 2 * quarter, 0, 2 * quarter - 1), 0

    specs = [spec(0, 0), spec(0, 1)]
    shapes = [shaped(quarter * rows, columns, BF16)] * 2
    if merged:
        specs.append(pl.BlockSpec((rows, columns), joined))
        shapes.append(shaped(2 * quarter * rows, columns, BF16))
    else:
        specs += [spec(1, 0), spec(1, 1)]
        shapes += [shaped(quarter * rows, columns, BF16)] * 2
    return specs, shapes


def store_stack(step, quads, up, merged, outs, value):
    half, index = places(step, quads, up)
    part = index // (quads // 4)
    for number, out in enumerate(outs):
        wanted = (half == number // 2) & ((part == number % 2) | (merged and number == 2))

        @pl.when(wanted)
        def _():
            out[...] = value


def row_grads_kernel(quads, cuts, x_ref, grad_ref, *outs):
    step = pl.program_id(0)
    total = dot_first(x_ref[...], grad_ref[...]).astype(BF16)
    first = 0
    for low, high, up, merged in cuts:
        count = 3 if merged else 4
        store_stack(step, quads, up, merged, outs[first : first + count], total[:, low:high])
        first += count


def row_grads(rows, grads, quads, cuts):
    count, width = rows.shape
    columns = grads.shape[1]
    block = width // quads
    specs, shapes = [], []
    for low, high, up, merged in cuts:
        more = stack_specs(quads, up, block, high - low, merged)
        specs, shapes = specs + more[0], shapes + more[1]
    outs = call(
        functools.partial(row_grads_kernel, quads, cuts),
        (quads,),
        [pl.BlockSpec((count, block), lambda i: (0, i)), whole((count, columns))],
        specs,
        shapes,
        48,
        2 * count * width * columns,
        name="row_grads",
    )(rows, grads)
    found = []
    for _, _, _, merged in cuts:
        size = 3 if merged else 4
        found.append((outs[:2], outs[2:size]))
        outs = outs[size:]
    return found


def column_grads_kernel(quads, up, quad_ref, act_ref, grad_ref, *outs):
    total = dot_first(act_ref[...], grad_ref[...]).astype(BF16)
    store_stack(pl.program_id(0), quads, up, True, outs, total)


def column_grads(acts, grads, quad, quads, up):
    count, hidden = acts.shape
    width = grads.shape[1]
    block = width // quads
    specs, shapes = stack_specs(quads, up, hidden, block, True)
    outs = pl.pallas_call(
        functools.partial(column_grads_kernel, quads, up),
        grid_spec=pltpu.PrefetchScalarGridSpec(
            num_scalar_prefetch=1,
            grid=(quads,),
            in_specs=[
                pl.BlockSpec((count, hidden), lambda i, own: (0, 0)),
                pl.BlockSpec((count, block), lambda i, own: (0, own[0] ^ i)),
            ],
            out_specs=specs,
        ),
        out_shape=shapes,
        compiler_params=pltpu.CompilerParams(vmem_limit_bytes=48 * MIB),
        cost_estimate=pl.CostEstimate(
            flops=2 * count * hidden * width,
            bytes_accessed=2 * (count * (hidden + width) + hidden * width),
            transcendentals=0,
        ),
        name="column_grads",
    )(quad[None], acts, grads)
    return outs[:2], outs[2:]


def down_grads_kernel(quads, quad_ref, act_ref, grad_ref, *rest):
    outs, total_ref = rest[:-1], rest[-1]
    step = pl.program_id(0)
    total_ref[...] = dot_first(act_ref[...], grad_ref[...])
    size = total_ref.shape[0] // quads
    quarter = quads // 4
    for part, up in enumerate((True, False)):

        @pl.when(step == part)
        def _():
            for key in range(quads):
                first = pl.multiple_of((quad_ref[0] ^ key) * size, 8)
                half, index = (int(v) for v in place_of(key, quads, up))
                number = 2 if half else index // quarter
                row = (index if half else index % quarter) * size
                outs[part * 3 + number][row : row + size, :] = total_ref[
                    pl.ds(first, size), :
                ].astype(BF16)


def place_of(key, quads, up):
    count = quads.bit_length() - 1
    spot = reversed_bits(key, count) if up else key
    return spot // (quads // 2), spot % (quads // 2)


def down_grads(acts, grads, quad, quads):
    count, hidden = acts.shape
    cut = grads.shape[1] // 2
    rows = hidden // 4
    shapes = [shaped(rows, cut, BF16), shaped(rows, cut, BF16), shaped(2 * rows, cut, BF16)] * 2
    outs = pl.pallas_call(
        functools.partial(down_grads_kernel, quads),
        grid_spec=pltpu.PrefetchScalarGridSpec(
            num_scalar_prefetch=1,
            grid=(2,),
            in_specs=[
                pl.BlockSpec((count, hidden), lambda i, own: (0, 0)),
                pl.BlockSpec((count, cut), lambda i, own: (0, i)),
            ],
            out_specs=[pl.BlockSpec(shape.shape, lambda i, own: (0, 0)) for shape in shapes],
            scratch_shapes=[pltpu.VMEM((hidden, cut), F32)],
        ),
        out_shape=shapes,
        compiler_params=pltpu.CompilerParams(vmem_limit_bytes=48 * MIB),
        cost_estimate=pl.CostEstimate(
            flops=4 * count * hidden * cut,
            bytes_accessed=2 * (count * (hidden + 2 * cut) + 2 * hidden * cut),
            transcendentals=0,
        ),
        name="down_grads",
    )(quad[None], acts, grads)
    return (outs[:2], outs[2:3]), (outs[3:5], outs[5:])


def local(
    residual_in,
    attention_gain,
    query_weight,
    query_bias,
    key_weight,
    key_bias,
    value_weight,
    value_bias,
    output_weight,
    feedforward_gain,
    router_weight,
    shared_logit_weight,
    shared_gate_weight,
    shared_up_weight,
    shared_down_weight,
    expert_gate,
    expert_up,
    expert_down,
    cotangent,
    expert_index,
    token_live,
    document_lengths,
):
    ep_count = lax.axis_size("ep")
    grp_count = lax.axis_size("grp")
    quads = grp_count // 2
    rows_dev, width = residual_in.shape
    group_rows = rows_dev * ep_count
    pair_rows = 2 * group_rows
    seq_len = group_rows * grp_count // SEQS
    expert_count = expert_gate.shape[0] * ep_count
    ffe = expert_gate.shape[2]
    ffs_half = shared_gate_weight.shape[1] // 2
    grp = lax.axis_index("grp")
    ep = lax.axis_index("ep")
    core = grp % 2
    quad = grp // 2
    back = -(-WINDOW // pair_rows)
    heads = query_weight.shape[1] // HDIM // 2
    head_width = heads * HDIM
    up_order = quad_bits()
    down_order = up_order[::-1]

    block = width // quads
    cut = len(up_order) // 2
    up_one, up_two = up_order[:cut], up_order[cut:]
    down_one, down_two = down_order[: len(down_order) - cut], down_order[len(down_order) - cut :]
    ep_masks = [1 << b for b in range(ep_count.bit_length() - 1)]
    quad_masks = [2 * bit for bit in up_order]
    seq_groups = grp_count // SEQS
    experts = jnp.arange(expert_count, dtype=jnp.int32)
    ed_cut = width // 2

    def shifted(values, steps):
        route = [
            (i, i + 2 * steps)
            for i in range(grp_count)
            if 0 <= i + 2 * steps < grp_count and i // seq_groups == (i + 2 * steps) // seq_groups
        ]
        return lax.ppermute(values, "grp", route)

    def gathered(values):
        return lax.all_gather(values, "ep", axis=0, tiled=True)

    def scattered(values):
        return lax.psum_scatter(values, "ep", scatter_dimension=0, tiled=True)

    def core_sum(kept, other):
        return add_rows(kept, across(other, 1))

    def finished(kept, arrived, axis):
        mine, other = finish(core[None], kept, arrived, axis)
        return mine, across(other, 1)

    hidden_in = residual_in.astype(F32)
    grad_out = cotangent.astype(F32)
    gain_one = attention_gain.astype(F32)
    gain_two = feedforward_gain.astype(F32)
    router_all = jnp.concatenate([router_weight, shared_logit_weight[:, None]], axis=1)
    router_flipped = flip_columns(router_all.T, quad).T
    scale_one = norm_scale(hidden_in)
    unit_one = hidden_in * scale_one
    normed_one = (unit_one * gain_one).astype(BF16)
    group_one = gathered(flip_columns(normed_one, quad))

    qk_keep, qk_other = zip(
        *[split_core(weight, core, 1) for weight in (query_weight, key_weight, value_weight)]
    )
    qkv_keep, qkv_other = jnp.concatenate(qk_keep, 1), jnp.concatenate(qk_other, 1)
    qkv_block = merge_core(qkv_keep, across(qkv_other, 1), core, 0)
    qkv_cut = qkv_block.shape[1] // 2
    qkv_a = {0: qkv_block[:, :qkv_cut]}
    qkv_b = {0: qkv_block[:, qkv_cut:]}
    (
        qkv_a, qkv_b, output_weight, shared_gate_weight, shared_up_weight, shared_down_weight,
        expert_gate, expert_up, expert_down,
    ) = together(
        qkv_a, qkv_b, output_weight, shared_gate_weight, shared_up_weight, shared_down_weight,
        expert_gate, expert_up, expert_down,
    )
    qkv_a_one, qkv_a_two = gather_quads(qkv_a, up_one), gather_quads(qkv_a, up_two)
    qkv_b_one, qkv_b_two = gather_quads(qkv_b, down_one), gather_quads(qkv_b, down_two)

    o_keep, o_other = split_core(output_weight, core, 0)
    sg_keep, sg_other = split_core(shared_gate_weight, core, 1)
    su_keep, su_other = split_core(shared_up_weight, core, 1)
    gu_keep = jnp.concatenate([sg_keep, su_keep], axis=1)
    gu_other = jnp.concatenate([sg_other, su_other], axis=1)
    gu_block = merge_core(gu_keep, across(gu_other, 1), core, 0)
    sd_keep, sd_other = split_core(shared_down_weight, core, 0)
    sd_keep = jnp.concatenate([sd_keep, o_keep], axis=0)
    sd_other = jnp.concatenate([sd_other, o_other], axis=0)
    sd_block = merge_core(sd_keep, across(sd_other, 1), core, 1)

    def expert_block(weight):
        keep, other = split_core(weight, core, 0)
        return merge_core(keep[0], across(other[0], 1), core, 0)

    eg_block, eu_block, ed_block = [
        expert_block(weight) for weight in (expert_gate, expert_up, expert_down)
    ]
    eda_block, edb_block = ed_block[:, :ed_cut], ed_block[:, ed_cut:]

    (
        qkv_a_one, qkv_a_two, qkv_b_one, qkv_b_two, gu_block, sd_block, eg_block, eu_block,
        eda_block, edb_block,
    ) = together(
        qkv_a_one, qkv_a_two, qkv_b_one, qkv_b_two, gu_block, sd_block, eg_block, eu_block,
        eda_block, edb_block,
    )
    qkv_a_rest = gather_rest(qkv_a_one, up_two)
    qkv_b_rest = gather_rest(qkv_b_one, down_two)
    sd_one, sd_two = gather_quads({0: sd_block}, down_one), gather_quads({0: sd_block}, down_two)
    chosen = (
        (expert_index[:, :, None] == experts[None, None, :]) & (token_live[:, None, None] > 0)
    ).any(axis=1)
    cot_packed = jnp.concatenate(
        [cotangent, jnp.pad(chosen.astype(BF16), ((0, 0), (0, LANES - expert_count)))], axis=1
    )
    chosen = chosen.astype(F32)
    bias = jnp.concatenate(
        [split_core(b, core, 0)[0] for b in (query_bias, key_bias, value_bias)]
    ).astype(F32)[None, :]
    key_place = (quad - back) * pair_rows + jnp.arange((back + 1) * pair_rows, dtype=jnp.int32)
    query_place = key_place[back * pair_rows :]
    _, position = doc_layout(document_lengths, seq_len, query_place)
    low = jnp.maximum(query_place - position, query_place - WINDOW + 1)[:, None]
    high, key_place = query_place[:, None], key_place[None, :]
    cosine, sine = rope_tables(position)
    (
        group_one, qkv_a, qkv_b, sd_one, sd_two, gu_block, eg_block, eu_block, eda_block,
         edb_block, cot_packed, bias, cosine, sine, low, high,
    ) = together(
        group_one, qkv_a_one | qkv_a_two | qkv_a_rest, qkv_b_one | qkv_b_two | qkv_b_rest,
        sd_one, sd_two, gu_block, eg_block, eu_block, eda_block, edb_block, cot_packed, bias,
        cosine, sine, low, high,
    )

    rows_one = merge_core(group_one, across(group_one, 1), core, 0)
    gu_two = gather_quads({0: gu_block}, up_two)
    sd_rest = gather_rest(sd_one, down_two)
    cot_group = gathered(cot_packed)
    qkv_a, qkv_b = listed(qkv_a), listed(qkv_b)
    query, key_value = project(rows_one, qkv_a, qkv_b, bias, cosine, sine, heads)

    query, key_value, sd_rest = together(query, key_value, sd_rest)
    before = [shifted(key_value, step) for step in range(back, 0, -1)]
    down_full = place_quads(sd_one | sd_two | sd_rest, quad, 1)
    query, before, gu_two, edb_block, down_full = together(
        query, before, gu_two, edb_block, down_full
    )
    edb_one, edb_two = gather_quads({0: edb_block}, down_one), gather_quads({0: edb_block}, down_two)
    attended, log_total = attend(query, before, key_value, key_place, low, high)
    output_rows = down_full[ffs_half:]
    kept, other = split_core(attended, core, 0)
    other = dot(other, output_rows).astype(BF16)
    kept, other, cot_group, edb_one, edb_two = together(kept, other, cot_group, edb_one, edb_two)
    branch = add_rows(dot(kept, output_rows).astype(BF16), across(other, 1))
    branch, gu_block, eu_block, eda_block, cot_group = together(
        branch, gu_block, eu_block, eda_block, cot_group
    )
    branch_sum = scattered(branch)
    cot_other = across(cot_group, 1)
    gu_one = gather_quads({0: gu_block}, up_one)
    eda_one, eda_two = gather_quads({0: eda_block}, up_one), gather_quads({0: eda_block}, up_two)
    eu_one = gather_quads({0: eu_block}, down_one)
    ed_full = jnp.zeros((eda_block.shape[0] * quads, width), BF16)
    ed_full = place_quads(edb_one | edb_two, quad, 0, ed_full, ed_cut)
    branch_sum, cot_other, gu_one, eda_one, eda_two, eu_one, eg_block, edb_one, ed_full = (
        together(
            branch_sum, cot_other, gu_one, eda_one, eda_two, eu_one, eg_block, edb_one, ed_full,
        )
    )

    eg_one = gather_quads({0: eg_block}, up_one)
    edb_rest = gather_rest(edb_one, down_two)
    gu_rest, eda_rest = gather_rest(gu_one, up_two), gather_rest(eda_one, up_two)
    mixed = hidden_in + branch_sum.astype(F32)
    scale_two = norm_scale(mixed)
    unit_two = mixed * scale_two
    normed_two = (unit_two * gain_two).astype(BF16)
    group_two = gathered(flip_columns(normed_two, quad))
    cot_rows = merge_core(cot_group, cot_other, core, 0)
    ed_full = place_quads(eda_one | eda_two, quad, 0, ed_full)
    (
        group_two, eg_one, edb_rest, gu_rest, eda_rest, eu_block, eg_block, eu_one, cot_rows,
        ed_full,
    ) = together(
        group_two, eg_one, edb_rest, gu_rest, eda_rest, eu_block, eg_block, eu_one, cot_rows,
        ed_full,
    )
    eu_two, eg_two = gather_quads({0: eu_block}, down_two), gather_quads({0: eg_block}, up_two)
    eu_rest, eg_rest = gather_rest(eu_one, down_two), gather_rest(eg_one, up_two)
    rows_two = merge_core(group_two, across(group_two, 1), core, 0)
    gu_pieces = listed(gu_one | gu_two | gu_rest)

    def router(rows, weight):
        logits = dot(rows, weight)
        return jax.nn.softmax(logits[:, :expert_count], axis=-1), jax.nn.sigmoid(
            logits[:, expert_count:]
        )

    chosen_rows = cot_rows[:, width : width + expert_count].astype(F32)
    probs_rows, shared_scale_rows = router(rows_two, router_flipped)
    router_probs, shared_scale = router(normed_two, router_all)
    mine = (experts == ep * 2 + core).astype(F32)[None, :]
    gate = jnp.sum(probs_rows * chosen_rows * mine, axis=1, keepdims=True)

    shared_active, grad_shared_out, part, grad_part, shared_dot, grad_gu = expert(
        core, rows_two, gu_pieces, down_full, ffs_half, cot_rows, shared_scale_rows
    )
    gu_cut = 2 * ffs_half * 3 // 4 // LANES * LANES
    (gua_grad, gua_out), (gub_grad, gub_out) = row_grads(
        rows_two, grad_gu, quads, [(0, gu_cut, True, True), (gu_cut, 2 * ffs_half, False, True)]
    )
    sd_grad, sd_out = column_grads(shared_active, grad_shared_out, quad, quads, False)
    gua_grad, eda_rest, edb_rest, ed_full = together(gua_grad, eda_rest, edb_rest, ed_full)
    ed_full = place_quads(eda_rest, quad, 0, ed_full)
    ed_full = place_quads(edb_rest, quad, 0, ed_full, ed_cut)
    (
        grad_part, part, eu_two, eg_two, eu_rest, eg_rest, ed_full, gua_grad, gua_out, gub_grad,
        gub_out, sd_grad, sd_out, gate,
    ) = together(
        grad_part, part, eu_two, eg_two, eu_rest, eg_rest, ed_full, gua_grad, gua_out, gub_grad,
        gub_out, sd_grad, sd_out, gate,
    )
    eg_pieces, eu_pieces = eg_one | eg_two | eg_rest, eu_one | eu_two | eu_rest

    def sent(blocks, bit):
        return [across(part, 2 * bit) for part in blocks]

    gua_sent, gub_sent = sent(gua_out, up_order[0]), sent(gub_out, down_order[0])
    sd_sent = sent(sd_out, down_order[0])

    lanes = jnp.arange(LANES, dtype=jnp.int32)
    lanes = jnp.where(lanes % expert_count == ep * 2 + core, lanes // expert_count, -1)[None, :]
    active, grad_result, *sums, grad_gate_pre, grad_up_pre = expert(
        core,
        rows_two,
        listed(eg_pieces) + listed(eu_pieces),
        ed_full,
        ffe,
        cot_rows,
        gate,
        (part, grad_part, shared_dot, lanes),
    )
    sums, gua_sent, gub_sent, sd_sent, gua_grad, gub_grad, sd_grad = together(
        sums, gua_sent, gub_sent, sd_sent, gua_grad, gub_grad, sd_grad
    )
    forward_part, packed = sums[:2], core_sum(*sums[2:])
    (
        packed, gua_grad, gub_grad, sd_grad, active, grad_result, grad_gate_pre, grad_up_pre,
    ) = together(
        packed, gua_grad, gub_grad, sd_grad, active, grad_result, grad_gate_pre, grad_up_pre,
    )
    spread = scattered(packed)
    (eda_grad, eda_out), (edb_grad, edb_out) = down_grads(active, grad_result, quad, quads)
    eda_out, edb_out, gua_grad, gub_grad, sd_grad, grad_gate_pre, grad_up_pre = together(
        eda_out, edb_out, gua_grad, gub_grad, sd_grad, grad_gate_pre, grad_up_pre
    )
    eda_sent, edb_sent = sent(eda_out, up_order[0]), sent(edb_out, down_order[0])
    gua_grad = first_sum(gua_grad, gua_sent)
    gub_grad = first_sum(gub_grad, gub_sent)
    sd_grad = first_sum(sd_grad, sd_sent)
    gua_sent, gub_sent = across(gua_grad[1], 2 * up_order[1]), across(gub_grad[1], 2 * down_order[1])
    sd_sent = across(sd_grad[1], 2 * down_order[1])
    ((eg_grad, eg_out),) = row_grads(rows_two, grad_gate_pre, quads, [(0, ffe, True, False)])
    ((eu_grad, eu_out),) = row_grads(rows_two, grad_up_pre, quads, [(0, ffe, False, False)])
    spread, eg_grad, eg_out = together(spread, eg_grad, eg_out)

    grad_normed_two = flip_columns(spread[:, :width], quad).astype(F32)
    side = spread[:, width : width + 4 * expert_count].astype(F32).reshape(rows_dev, 4, expert_count)
    grad_gate_own = side[:, 0] + side[:, 1]
    shared_dot_own = jnp.sum(side[:, 2] + side[:, 3], axis=1, keepdims=True)
    grad_logit = shared_dot_own * shared_scale * (1.0 - shared_scale)
    grad_probs = grad_gate_own * chosen
    grad_logits = router_probs * (
        grad_probs - jnp.sum(router_probs * grad_probs, axis=-1, keepdims=True)
    )
    grad_router = jnp.concatenate([grad_logits, grad_logit], axis=1)
    router_grad = dot_first(normed_two.astype(F32), grad_router)
    grad_normed_two = grad_normed_two + dot_last(grad_router, router_all.astype(F32))
    grad_norm_part, ff_gain_grad = norm_backward(grad_normed_two, unit_two, scale_two, gain_two)
    grad_mixed = grad_out + grad_norm_part
    (
        branch_low, eda_grad, eda_sent, edb_grad, edb_sent, gua_grad, gua_sent, gub_grad, gub_sent,
        sd_grad, sd_sent, eg_out, eu_grad, eu_out, forward_part,
    ) = together(
        grad_mixed.astype(BF16), eda_grad, eda_sent, edb_grad, edb_sent, gua_grad, gua_sent, gub_grad,
        gub_sent, sd_grad, sd_sent, eg_out, eu_grad, eu_out, forward_part,
    )
    group_branch = gathered(branch_low)
    eg_sent = sent(eg_out[:1], up_order[0])
    eu_sent = sent(eu_out[:1], down_order[0])
    forward_part = core_sum(*forward_part)
    eda_grad = first_sum(eda_grad, eda_sent)
    edb_grad = first_sum(edb_grad, edb_sent)
    eda_sent, edb_sent = across(eda_grad[1], 2 * up_order[1]), across(edb_grad[1], 2 * down_order[1])

    (
        group_branch, forward_part, eg_grad, eg_out, eg_sent, eu_grad, eu_out, eu_sent, eda_grad,
        eda_sent, edb_grad, edb_sent,
    ) = together(
        group_branch, forward_part, eg_grad, eg_out, eg_sent, eu_grad, eu_out, eu_sent, eda_grad,
        eda_sent, edb_grad, edb_sent,
    )
    grad_branch = merge_core(group_branch, across(group_branch, 1), core, 0)
    eg_sent = eg_sent + sent(eg_out[1:], up_order[0])
    eu_sent = eu_sent + sent(eu_out[1:], down_order[0])

    layer_sum = scattered(forward_part)
    grad_attended = dot_last(grad_branch, down_full[ffs_half:]).astype(BF16)
    grad_query, grad_own, *grad_before = attend_back(
        query, grad_attended, log_total, before, key_value, key_place, low, high, cosine, sine
    )
    (
        grad_query, grad_before, grad_branch, eg_grad, eu_grad, gua_grad, gua_sent, gub_grad,
        gub_sent, sd_grad, sd_sent,
    ) = together(
        grad_query, grad_before, grad_branch, eg_grad, eu_grad, gua_grad, gua_sent, gub_grad,
        gub_sent, sd_grad, sd_sent,
    )
    arrived = [shifted(sent, step - back) for step, sent in enumerate(grad_before)]
    cut = eg_grad[1].shape[0] // 2
    eg_grad = [
        add_low(eg_grad[0], eg_sent[0]),
        add_low(eg_grad[1][:cut], eg_sent[1][:cut]),
        add_low(eg_grad[1][cut:], eg_sent[1][cut:]),
    ]
    eu_grad = [
        add_low(eu_grad[0], eu_sent[0]),
        add_low(eu_grad[1][:cut], eu_sent[1][:cut]),
        add_low(eu_grad[1][cut:], eu_sent[1][cut:]),
    ]
    eg_rest = across(eg_grad[1], 2 * up_order[1])
    arrived, eg_grad, eu_grad, grad_branch = together(arrived, eg_grad, eu_grad, grad_branch)
    eu_rest = across(eu_grad[1], 2 * down_order[1])
    (*partial, att_gain_part, bias_part), (qkv_a_grad, qkv_a_out), (qkv_b_grad, qkv_b_out) = collect(
        core, grad_query, grad_own, cosine, sine, rows_one, arrived, qkv_a, qkv_b
    )
    partial, qkv_a_out, qkv_b_out, eg_grad, eg_rest, eu_grad, eu_rest = together(
        partial, qkv_a_out, qkv_b_out, eg_grad, eg_rest, eu_grad, eu_rest
    )
    eg_last, eu_last = across(eg_grad[2], 2 * up_order[1]), across(eu_grad[2], 2 * down_order[1])
    qkv_a_sent, qkv_b_sent = sent(qkv_a_out, up_order[0]), sent(qkv_b_out, down_order[0])
    partial_sum = core_sum(*partial)

    (
        partial_sum, att_gain_part, bias_part, grad_branch, qkv_a_grad, qkv_b_grad, eda_grad,
        eda_sent, edb_grad, edb_sent,
    ) = together(
        partial_sum, att_gain_part, bias_part, grad_branch, qkv_a_grad, qkv_b_grad, eda_grad,
        eda_sent, edb_grad, edb_sent,
    )
    grad_normed_one = scattered(partial_sum)
    o_grad, o_out = column_grads(attended, grad_branch, quad, quads, False)
    att_gain_part = flip_columns(att_gain_part[0], quad) / gain_one
    late = jnp.concatenate([att_gain_part, ff_gain_grad, router_grad.T.reshape(-1)])
    late = sum_everywhere(late, [], ep_masks[:1])
    (
        late, qkv_a_sent, qkv_b_sent, o_out, eg_last, eu_last, eda_sent, edb_sent, gua_sent,
        gub_sent, sd_sent,
    ) = together(
        late, qkv_a_sent, qkv_b_sent, o_out, eg_last, eu_last, eda_sent, edb_sent, gua_sent,
        gub_sent, sd_sent,
    )
    eg_rest = jnp.concatenate([eg_rest, eg_last], axis=0)
    eu_rest = jnp.concatenate([eu_rest, eu_last], axis=0)
    late = sum_everywhere(late, [], ep_masks[1:])
    bias_part = bias_part.reshape(3, head_width)
    bias_part = jnp.concatenate(
        [jnp.where(core == 0, bias_part, 0.0), jnp.where(core == 0, 0.0, bias_part)], axis=1
    )
    late = sum_everywhere(jnp.concatenate([late, bias_part.reshape(-1)]), [1], [])
    qkv_a_grad = first_sum(qkv_a_grad, qkv_a_sent)
    qkv_b_grad = first_sum(qkv_b_grad, qkv_b_sent)
    qkv_a_rest = across(qkv_a_grad[1], 2 * up_order[1])
    qkv_b_rest = across(qkv_b_grad[1], 2 * down_order[1])
    o_grad = first_sum(o_grad, sent(o_out, down_order[0]))
    o_rest = across(o_grad[1], 2 * down_order[1])
    late = sum_everywhere(late, quad_masks, [])
    eg_grad = merge(core, *finished(*rest_parts(eg_grad[0], eg_rest, up_order), 0), None)
    eda_mine, eda_arrived = finished(*rest_parts(eda_grad[0], eda_sent, up_order), 0)
    edb_mine, edb_arrived = finished(*rest_parts(edb_grad[0], edb_sent, down_order), 0)
    ed_grad = jnp.concatenate(
        [merge(core, eda_mine, eda_arrived, None), merge(core, edb_mine, edb_arrived, None)], axis=2
    )
    gua_mine, gua_arrived = finished(*rest_parts(gua_grad[0], gua_sent, up_order), 0)
    gub_mine, gub_arrived = finished(*rest_parts(gub_grad[0], gub_sent, down_order), 0)
    sd_mine, sd_arrived = finished(*rest_parts(sd_grad[0], sd_sent, down_order), 1)
    gu_mine = jnp.concatenate([gua_mine, gub_mine], axis=1)
    gu_arrived = jnp.concatenate([gua_arrived, gub_arrived], axis=1)
    sg_grad, su_grad = [
        merge_core(
            gu_mine[:, part * ffs_half : (part + 1) * ffs_half],
            gu_arrived[:, part * ffs_half : (part + 1) * ffs_half],
            core,
            1,
        ).astype(F32)
        for part in range(2)
    ]
    sd_grad = merge(core, sd_mine, sd_arrived, 0)
    layer_out = (mixed + layer_sum.astype(F32)).astype(BF16)
    qkv_a_mine, qkv_a_arrived = finished(*rest_parts(qkv_a_grad[0], qkv_a_rest, up_order), 0)
    qkv_b_mine, qkv_b_arrived = finished(*rest_parts(qkv_b_grad[0], qkv_b_rest, down_order), 0)
    o_mine, o_arrived = finished(*rest_parts(o_grad[0], o_rest, down_order), 1)
    (
        grad_normed_one, qkv_a_mine, qkv_a_arrived, qkv_b_mine, qkv_b_arrived, o_mine, o_arrived,
        late, eu_rest, eg_grad, ed_grad, layer_out, sg_grad, su_grad, sd_grad,
    ) = together(
        grad_normed_one, qkv_a_mine, qkv_a_arrived, qkv_b_mine, qkv_b_arrived, o_mine, o_arrived,
        late, eu_rest, eg_grad, ed_grad, layer_out, sg_grad, su_grad, sd_grad,
    )
    eu_grad = merge(core, *finished(*rest_parts(eu_grad[0], eu_rest, down_order), 0), None)
    qkv_mine = jnp.concatenate([qkv_a_mine, qkv_b_mine], axis=1)
    qkv_arrived = jnp.concatenate([qkv_a_arrived, qkv_b_arrived], axis=1)
    q_grad, k_grad, v_grad = [merge(core, qkv_mine, qkv_arrived, 1, part, 3) for part in range(3)]
    o_grad = merge(core, o_mine, o_arrived, 0)
    att_gain_grad, ff_gain_grad = late[:width], late[width : 2 * width]
    router_grad = late[2 * width : (expert_count + 3) * width].reshape(expert_count + 1, width)
    bias_mine = late[(expert_count + 3) * width :].reshape(3, 2 * head_width)
    grad_norm_one, _ = norm_backward(
        flip_columns(grad_normed_one, quad).astype(F32), unit_one, scale_one, gain_one
    )
    input_grad = grad_mixed + grad_norm_one
    return (
        layer_out,
        input_grad,
        att_gain_grad,
        q_grad,
        bias_mine[0],
        k_grad,
        bias_mine[1],
        v_grad,
        bias_mine[2],
        o_grad,
        ff_gain_grad,
        router_grad[:expert_count].T,
        router_grad[expert_count],
        sg_grad,
        su_grad,
        sd_grad,
        eg_grad,
        eu_grad,
        ed_grad,
    )


def solution(mesh):
    tokens = P(("grp", "ep"), None)
    rows, columns, experts = P("grp", "ep"), P("ep", "grp"), P("ep", "grp", None)
    in_specs = (
        tokens, P(), rows, P("ep"), rows, P("ep"), rows, P("ep"), columns, P(), P(), P(),
        rows, rows, columns, experts, experts, experts, tokens, tokens, P(("grp", "ep")), P(),
    )
    out_specs = (
        tokens, tokens, P(), rows, P("ep"), rows, P("ep"), rows, P("ep"), columns, P(), P(), P(),
        rows, rows, columns, experts, experts, experts,
    )
    return jax.shard_map(local, mesh=mesh, in_specs=in_specs, out_specs=out_specs, check_vma=False)
```

```python
import functools

import jax
import jax.numpy as jnp
from jax import lax
from jax.experimental import pallas as pl
from jax.experimental.pallas import tpu as pltpu
from jax.sharding import PartitionSpec as P

HDIM = 128
SEQS = 2
DOCS = 4
WINDOW = 1024
EPS = 1e-06
ROPE_BASE = 1000000.0
MASKED = -1e30
F32 = jnp.float32
BF16 = jnp.bfloat16
TILE = 256
LANES = 128
MIB = 1 << 20


def dot(left, right):
    return jnp.dot(left, right, preferred_element_type=F32)


def dot_last(left, right):
    return lax.dot_general(left, right, (((1,), (1,)), ((), ())), preferred_element_type=F32)


def dot_first(left, right):
    return lax.dot_general(left, right, (((0,), (0,)), ((), ())), preferred_element_type=F32)


def across(block, mask):
    count = lax.axis_size("grp")
    return lax.ppermute(block, "grp", [(i, i ^ mask) for i in range(count)])


def quad_bits():
    return [1 << b for b in range((lax.axis_size("grp") // 2).bit_length() - 1)]


def flip_columns(values, quad):
    quads = lax.axis_size("grp") // 2
    axis = values.ndim - 1
    block = values.shape[axis] // quads
    return jnp.concatenate(
        [
            lax.dynamic_slice_in_dim(values, (quad ^ key) * block, block, axis)
            for key in range(quads)
        ],
        axis=axis,
    )


def gather_quads(pieces, order):
    pieces = dict(pieces)
    for bit in order:
        for key, piece in list(pieces.items()):
            pieces[key | bit] = across(piece, 2 * bit)
    return pieces


def add_low(left, right):
    return (left.astype(F32) + right.astype(F32)).astype(BF16)


def first_sum(parts, arrived):
    half = parts[0].shape[0]
    if len(arrived) == 1:
        arrived = (arrived[0][:half], arrived[0][half:])
    return add_low(parts[0], arrived[0]), add_low(parts[1], arrived[1])


def rest_parts(kept, arrived, order):
    for bit in order[2:]:
        stack = add_rows(kept, arrived)
        half = stack.shape[0] // 2
        kept, arrived = stack[:half], across(stack[half:], 2 * bit)
    return kept, arrived


def together(*values):
    return lax.optimization_barrier(values)


def sum_everywhere(values, masks_grp, masks_ep):
    for mask in masks_grp:
        values = values + across(values, mask)
    count = lax.axis_size("ep")
    for mask in masks_ep:
        values = values + lax.ppermute(values, "ep", [(i, i ^ mask) for i in range(count)])
    return values


def gather_rest(pieces, order):
    found = {}
    for key, piece in pieces.items():
        if key:
            found.update({key | k: v for k, v in gather_quads({0: piece}, order).items()})
    return found


def listed(pieces):
    return [pieces[key] for key in sorted(pieces)]


def place_quads(pieces, quad, axis, whole=None, other=0):
    size = pieces[0].shape[axis] if whole is None else whole.shape[axis] // (lax.axis_size("grp") // 2)
    if whole is None:
        shape = list(pieces[0].shape)
        shape[axis] = size * len(pieces)
        whole = jnp.zeros(shape, pieces[0].dtype)
    for key in sorted(pieces):
        start = [other, other]
        start[axis] = (quad ^ key) * size
        whole = lax.dynamic_update_slice(whole, pieces[key], start)
    return whole


def take_quads(whole, quad, quads, axis):
    size = whole.shape[axis] // quads
    return {
        key: lax.dynamic_slice_in_dim(whole, (quad ^ key) * size, size, axis)
        for key in range(quads)
    }


def merge_core(kept, arrived, core, axis):
    first = jnp.where(core == 0, kept, arrived)
    second = jnp.where(core == 0, arrived, kept)
    return jnp.concatenate([first, second], axis=axis)


def split_core(values, core, axis):
    half = values.shape[axis] // 2
    first = lax.slice_in_dim(values, 0, half, axis=axis)
    second = lax.slice_in_dim(values, half, 2 * half, axis=axis)
    return jnp.where(core == 0, first, second), jnp.where(core == 0, second, first)


def norm_scale(values):
    return lax.rsqrt(jnp.mean(values * values, axis=-1, keepdims=True) + EPS)


def norm_backward(grad_normed, unit, scale, gain):
    grad_unit = grad_normed * gain
    inner = jnp.mean(grad_unit * unit, axis=-1, keepdims=True)
    return scale * (grad_unit - unit * inner), jnp.sum(grad_normed * unit, axis=0)


def doc_layout(document_lengths, seq_len, index):
    valid = index >= 0
    safe = jnp.maximum(index, 0)
    seq_of = safe // seq_len
    place = safe % seq_len
    seq_count = document_lengths.shape[0]
    picker = (seq_of[:, None] == jnp.arange(seq_count, dtype=jnp.int32)[None, :]).astype(jnp.int32)
    lengths = jnp.sum(picker[:, :, None] * document_lengths[None, :, :], axis=1)
    ends = jnp.cumsum(lengths, axis=1)
    doc = jnp.sum((ends <= place[:, None]).astype(jnp.int32), axis=1)
    earlier = jnp.arange(DOCS, dtype=jnp.int32)[None, :] < doc[:, None]
    before = jnp.sum(jnp.where(earlier, lengths, 0), axis=1)
    return jnp.where(valid, seq_of * DOCS + doc, -1), place - before


def rope_tables(position):
    half = HDIM // 2
    freq = ROPE_BASE ** (-(jnp.arange(half, dtype=F32) * 2.0 / HDIM))
    angle = position.astype(F32)[:, None] * freq[None, :]
    cosine, sine = jnp.cos(angle), jnp.sin(angle)
    return jnp.concatenate([cosine, cosine], axis=1), jnp.concatenate([-sine, sine], axis=1)


def turn(values, cosine, sine):
    return values * cosine + pltpu.roll(values, HDIM // 2, 1) * sine


def call(kernel, grid, ins, outs, shapes, limit, flops, scratch=(), name=None, scalars=0):
    moved = 0
    for shape in shapes:
        moved += shape.size * shape.dtype.itemsize

    def run(*args):
        total = moved + sum(a.size * a.dtype.itemsize for a in args)
        if flops == 0:
            total = 0
        return pl.pallas_call(
            kernel,
            grid_spec=pltpu.PrefetchScalarGridSpec(
                num_scalar_prefetch=scalars,
                grid=grid,
                in_specs=ins,
                out_specs=outs,
                scratch_shapes=scratch,
            ),
            out_shape=shapes,
            compiler_params=pltpu.CompilerParams(vmem_limit_bytes=limit * MIB),
            cost_estimate=pl.CostEstimate(
                flops=flops, bytes_accessed=total, transcendentals=0
            ),
            name=name,
        )(*args)

    return run


def whole(shape):
    return pl.BlockSpec(shape, lambda *_: (0,) * len(shape), pipeline_mode=pl.Buffered(1))


def rows_spec(columns, tile=TILE):
    return pl.BlockSpec((tile, columns), lambda i, *_: (i, 0))


def turned(step, core, count):
    return (step + (count // 2) * core) % count


def turned_spec(columns, count):
    return pl.BlockSpec((TILE, columns), lambda i, core: (turned(i, core[0], count), 0))


def halves_specs(columns, count):
    half = count // 2
    specs = [
        pl.BlockSpec((TILE, columns), lambda i, core: (jnp.minimum(i, half), 0)),
        pl.BlockSpec((TILE, columns), lambda i, core: (jnp.maximum(i - half, 0), 0)),
    ]
    return specs, [shaped((half + 1) * TILE, columns, BF16), shaped(half * TILE, columns, BF16)]


def add_kernel(left_ref, right_ref, out_ref):
    out_ref[...] = (left_ref[...].astype(F32) + right_ref[...].astype(F32)).astype(BF16)


def add_rows(left, right):
    rows, columns = right.shape
    tile = rows // 4 if rows % 64 == 0 else rows
    return call(
        add_kernel,
        (rows // tile,),
        [rows_spec(columns, tile)] * 2,
        [rows_spec(columns, tile)],
        [shaped(rows, columns, BF16)],
        16,
        0,
        name="add_rows",
    )(left, right)[0]


def join_kernel(core_ref, own_ref, other_ref, out_ref):
    own = pl.program_id(0) // (pl.num_programs(0) // 2) == core_ref[0]

    @pl.when(own)
    def _():
        out_ref[...] = own_ref[...]

    @pl.when(~own)
    def _():
        out_ref[...] = other_ref[...]


def join_rows(core, own, other):
    rows, columns = own.shape
    tile = rows // 4

    def spec(mine):
        def index(i, core):
            place = i - 4 * jnp.where(mine, core[0], 1 - core[0])
            return jnp.clip(place, 0, 3), 0

        return pl.BlockSpec((tile, columns), index)

    return call(
        join_kernel,
        (8,),
        [spec(True), spec(False)],
        [pl.BlockSpec((tile, columns), lambda i, core: (i, 0))],
        [shaped(2 * rows, columns, BF16)],
        24,
        0,
        name="join_rows",
        scalars=1,
    )(core[None], own, other)[0]


def finish_kernel(core_ref, kept_ref, arrived_ref, mine_ref, other_ref):
    total = (kept_ref[...].astype(F32) + arrived_ref[...].astype(F32)).astype(BF16)

    @pl.when(pl.program_id(0) == 0)
    def _():
        other_ref[...] = total

    @pl.when(pl.program_id(0) == 1)
    def _():
        mine_ref[...] = total


def finish(core, kept, arrived, axis):
    rows, columns = kept.shape
    size = (rows // 2, columns) if axis == 0 else (rows, columns // 2)
    if size[0] % 16 or (axis == 1 and size[1] % LANES):
        return split_core(add_low(kept, arrived), core[0], axis)

    def index(i, core):
        half = jnp.where(i == 0, 1 - core[0], core[0])
        return (half, 0) if axis == 0 else (0, half)

    return call(
        finish_kernel,
        (2,),
        [pl.BlockSpec(size, index)] * 2,
        [pl.BlockSpec(size, lambda i, core: (0, 0))] * 2,
        [shaped(*size, BF16)] * 2,
        24,
        0,
        name="finish",
        scalars=1,
    )(core, kept, arrived)


def merge_kernel(core_ref, mine_ref, arrived_ref, out_ref):
    own = pl.program_id(0) == core_ref[0]

    @pl.when(own)
    def _():
        out_ref[...] = mine_ref[...].astype(F32).reshape(out_ref.shape)

    @pl.when(~own)
    def _():
        out_ref[...] = arrived_ref[...].astype(F32).reshape(out_ref.shape)


def merge(core, mine, arrived, axis, part=0, parts=1):
    rows, columns = mine.shape
    columns = columns // parts
    if axis is None:
        shape, size, index = (2, rows, columns), (1, rows, columns), lambda i, core: (i, 0, 0)
    elif axis == 0:
        shape, size, index = (2 * rows, columns), (rows, columns), lambda i, core: (i, 0)
    else:
        shape, size, index = (rows, 2 * columns), (rows, columns), lambda i, core: (0, i)
    return call(
        merge_kernel,
        (2,),
        [pl.BlockSpec((rows, columns), lambda i, core: (0, part))] * 2,
        [pl.BlockSpec(size, index)],
        [jax.ShapeDtypeStruct(shape, F32)],
        24,
        0,
        name="merge",
        scalars=1,
    )(core[None], mine, arrived)[0]


def shaped(rows, columns, dtype):
    return jax.ShapeDtypeStruct((rows, columns), dtype)


def sum_pieces(x, refs):
    block = x.shape[1] // len(refs)
    total = dot(x[:, :block], refs[0][...])
    for key in range(1, len(refs)):
        total = total + dot(x[:, key * block : (key + 1) * block], refs[key][...])
    return total


def project_kernel(heads, quads, x_ref, bias_ref, cos_ref, sin_ref, *rest):
    wa_refs, wb_refs, (q_ref, kv_ref) = rest[:quads], rest[quads : 2 * quads], rest[2 * quads :]
    x = x_ref[...]
    lin = jnp.concatenate([sum_pieces(x, wa_refs), sum_pieces(x, wb_refs)], axis=1) + bias_ref[...]
    cosine, sine = cos_ref[...], sin_ref[...]
    for head in range(3 * heads):
        part = lin[:, head * HDIM : (head + 1) * HDIM]
        if head < 2 * heads:
            part = turn(part, cosine, sine)
        if head < heads:
            q_ref[:, head * HDIM : (head + 1) * HDIM] = part.astype(BF16)
        else:
            kv_ref[:, (head - heads) * HDIM : (head - heads + 1) * HDIM] = part.astype(BF16)


def project(x, wa, wb, bias, cosine, sine, heads):
    rows, width = x.shape
    quads, (block, cut) = len(wa), wa[0].shape
    return call(
        functools.partial(project_kernel, heads, quads),
        (rows // TILE,),
        [rows_spec(width), whole((1, 2 * cut))]
        + [rows_spec(HDIM)] * 2
        + [whole((block, cut))] * (2 * quads),
        [rows_spec(heads * HDIM), rows_spec(2 * heads * HDIM)],
        [shaped(rows, heads * HDIM, BF16), shaped(rows, 2 * heads * HDIM, BF16)],
        32,
        4 * rows * width * cut,
        name="project",
    )(x, bias, cosine, sine, *wa, *wb)


def window_keys(before_refs, own_ref, place, pair_rows, step):
    parts = []
    start = step * TILE
    reach = -WINDOW + start
    for back, ref in enumerate(before_refs):
        first = -(len(before_refs) - back) * pair_rows
        low = max(reach - first, 0)
        if low < pair_rows:
            parts.append(ref[low:, place])
    parts.append(own_ref[max(reach, 0) : start + TILE, place])
    return jnp.concatenate(parts, axis=0) if len(parts) > 1 else parts[0]


def probabilities(query, keys, key_place, low, high, peak):
    scores = dot_last(query, keys) * HDIM ** (-0.5)
    scores = jnp.where((key_place >= low) & (key_place <= high), scores, MASKED)
    if peak is None:
        top = jnp.max(scores, axis=1, keepdims=True)
        weights = jnp.exp(scores - top)
        total = jnp.sum(weights, axis=1, keepdims=True)
        return weights / total, top + jnp.log(total)
    return jnp.exp(scores - peak), peak


def attend_kernel(back, pair_rows, heads, q_ref, *rest):
    before, (own_ref, place_ref, low_ref, high_ref, out_ref, log_ref) = rest[:back], rest[back:]
    for head in range(heads):
        cols = slice(head * HDIM, (head + 1) * HDIM)
        value_cols = slice((heads + head) * HDIM, (heads + head + 1) * HDIM)
        for step in range(pair_rows // TILE):
            rows = slice(step * TILE, (step + 1) * TILE)
            first = back * pair_rows - WINDOW + step * TILE
            places = place_ref[:, max(first, 0) : back * pair_rows + (step + 1) * TILE]
            keys = window_keys(before, own_ref, cols, pair_rows, step)
            values = window_keys(before, own_ref, value_cols, pair_rows, step)
            probs, logs = probabilities(
                q_ref[rows, cols], keys, places, low_ref[rows, :], high_ref[rows, :], None
            )
            out_ref[rows, cols] = dot(probs.astype(BF16), values).astype(BF16)
            log_ref[rows, cols] = jnp.broadcast_to(logs, (TILE, HDIM))


def attend(query, before, own, places, low, high):
    rows, columns = query.shape
    heads = columns // HDIM
    back = len(before)
    return call(
        functools.partial(attend_kernel, back, rows, heads),
        (),
        [pl.BlockSpec(memory_space=pltpu.VMEM)] * (5 + back),
        [pl.BlockSpec(memory_space=pltpu.VMEM)] * 2,
        [shaped(rows, columns, BF16), shaped(rows, columns, F32)],
        40,
        4 * rows * columns * (WINDOW + TILE),
        name="attend",
    )(query, *before, own, places, low, high)


def attend_back_kernel(back, pair_rows, heads, q_ref, grad_ref, log_ref, *rest):
    before = rest[:back]
    own_ref, place_ref, low_ref, high_ref, cos_ref, sin_ref = rest[back : back + 6]
    dq_ref, own_out = rest[back + 6 : back + 8]
    before_out = rest[back + 8 : 2 * back + 8]
    total_ref = rest[-1]
    total_ref[...] = jnp.zeros_like(total_ref)
    for head in range(heads):
        cols = slice(head * HDIM, (head + 1) * HDIM)
        value_cols = slice((heads + head) * HDIM, (heads + head + 1) * HDIM)
        for step in range(pair_rows // TILE):
            rows = slice(step * TILE, (step + 1) * TILE)
            first = max(back * pair_rows - WINDOW + step * TILE, 0)
            last = back * pair_rows + (step + 1) * TILE
            keys = window_keys(before, own_ref, cols, pair_rows, step)
            values = window_keys(before, own_ref, value_cols, pair_rows, step)
            query, grad = q_ref[rows, cols], grad_ref[rows, cols]
            peak = jnp.concatenate([log_ref[rows, cols]] * ((last - first) // HDIM), axis=1)
            probs, _ = probabilities(
                query, keys, place_ref[:, first:last], low_ref[rows, :], high_ref[rows, :], peak
            )
            grad_probs = dot_last(grad, values)
            inner = jnp.sum(probs * grad_probs, axis=1, keepdims=True)
            grad_scores = (probs * (grad_probs - inner)).astype(BF16)
            grad_query = dot(grad_scores, keys) * HDIM ** (-0.5)
            dq_ref[rows, cols] = turn(grad_query, cos_ref[rows, :], -sin_ref[rows, :]).astype(BF16)
            total_ref[first:last, cols] += dot_first(grad_scores, query) * HDIM ** (-0.5)
            total_ref[first:last, value_cols] += dot_first(probs.astype(BF16), grad)
    own_out[...] = total_ref[back * pair_rows :, :]
    for step in range(back):
        before_out[step][...] = total_ref[step * pair_rows : (step + 1) * pair_rows, :].astype(BF16)


def attend_back(query, grad, logs, before, own, places, low, high, cosine, sine):
    rows, columns = query.shape
    back = len(before)
    return call(
        functools.partial(attend_back_kernel, back, rows, columns // HDIM),
        (),
        [pl.BlockSpec(memory_space=pltpu.VMEM)] * (9 + back),
        [pl.BlockSpec(memory_space=pltpu.VMEM)] * (2 + back),
        [shaped(rows, columns, BF16), shaped(rows, 2 * columns, F32)]
        + [shaped(rows, 2 * columns, BF16)] * back,
        48,
        10 * rows * columns * (WINDOW + TILE),
        scratch=[pltpu.VMEM(((back + 1) * rows, 2 * columns), F32)],
        name="attend_back",
    )(query, grad, logs, *before, own, places, low, high, cosine, sine)


def collect_kernel(heads, back, quads, core_ref, dq_ref, own_ref, cos_ref, sin_ref, x_ref, *rest):
    arrived, wa_refs, wb_refs = rest[:back], rest[back : back + quads], rest[back + quads : back + 2 * quads]
    kept_ref, other_ref, gain_ref, bias_ref, *outs = rest[back + 2 * quads :]
    x_all, grad_all = outs[-2:]
    columns = heads * HDIM
    step = pl.program_id(0)
    total = own_ref[...]
    for ref in arrived:
        total = total + ref[...].astype(F32)
    cosine, sine = cos_ref[...], -sin_ref[...]
    heads_out = [dq_ref[...]]
    for head in range(2 * heads):
        part = total[:, head * HDIM : (head + 1) * HDIM]
        if head < heads:
            part = turn(part, cosine, sine)
        heads_out.append(part.astype(BF16))
    grads = jnp.concatenate(heads_out, axis=1)
    tile = turned(step, core_ref[0], pl.num_programs(0))
    rows = pl.ds(pl.multiple_of(tile * TILE, TILE), TILE)
    x_all[rows, :] = x_ref[...]
    grad_all[rows, :] = grads

    @pl.when(step == 0)
    def _():
        gain_ref[...] = jnp.zeros_like(gain_ref)
        bias_ref[...] = jnp.zeros_like(bias_ref)

    bias_ref[...] += jnp.sum(grads.astype(F32), axis=0, keepdims=True)
    cut = 3 * columns // 2
    block = x_ref.shape[1] // quads
    for key in range(quads):
        cols = slice(key * block, (key + 1) * block)
        part = dot_last(grads[:, :cut], wa_refs[key][...]) + dot_last(grads[:, cut:], wb_refs[key][...])
        kept_ref[:, cols] = part.astype(BF16)
        other_ref[:, cols] = part.astype(BF16)
        gain_ref[:, cols] += jnp.sum(part * x_ref[:, cols].astype(F32), axis=0, keepdims=True)

    @pl.when(step == pl.num_programs(0) - 1)
    def _():
        for key in range(quads):
            weight = dot_first(x_all[:, key * block : (key + 1) * block], grad_all[...]).astype(BF16)
            for part, up in enumerate((True, False)):
                half, index = (int(v) for v in place_of(key, quads, up))
                quarter = quads // 4
                number = 2 if half else index // quarter
                first = (index if half else index % quarter) * block
                outs[part * 3 + number][first : first + block, :] = weight[
                    :, part * cut : (part + 1) * cut
                ]


def collect(core, grad_query, own, cosine, sine, x, arrived, wa, wb):
    rows, columns = grad_query.shape
    width = x.shape[1]
    tiles = rows // TILE
    quads, (block, cut) = len(wa), wa[0].shape
    quarter = width // 4
    fixed = lambda *_: (0, 0)
    halves = halves_specs(width, tiles)
    shapes = [shaped(quarter, cut, BF16), shaped(quarter, cut, BF16), shaped(2 * quarter, cut, BF16)]
    outs = call(
        functools.partial(collect_kernel, columns // HDIM, len(arrived), quads),
        (tiles,),
        [turned_spec(columns, tiles), turned_spec(2 * columns, tiles)]
        + [turned_spec(HDIM, tiles)] * 2
        + [turned_spec(width, tiles)]
        + [turned_spec(2 * columns, tiles)] * len(arrived)
        + [whole((block, cut))] * (2 * quads),
        halves[0]
        + [pl.BlockSpec((1, width), fixed)]
        + [pl.BlockSpec((1, 3 * columns), fixed)]
        + [pl.BlockSpec(shape.shape, fixed) for shape in shapes] * 2,
        halves[1] + [shaped(1, width, F32), shaped(1, 3 * columns, F32)] + shapes * 2,
        60,
        8 * rows * width * cut,
        scratch=[pltpu.VMEM((rows, width), BF16), pltpu.VMEM((rows, 3 * columns), BF16)],
        name="collect",
        scalars=1,
    )(core[None], grad_query, own, cosine, sine, x, *arrived, *wa, *wb)
    return outs[:4], (outs[4:6], outs[6:7]), (outs[7:9], outs[9:])


def expert_kernel(routed, quads, core_ref, x_ref, wd_ref, cot_ref, scale_ref, *rest):
    if routed:
        wg_refs, wu_refs, rest = rest[:quads], rest[quads : 2 * quads], rest[2 * quads :]
        part_in, grad_in, dot_in, lane_ref = rest[:4]
        rest = rest[4:]
    else:
        wgu_refs, rest = rest[:quads], rest[quads:]
    x = x_ref[...]
    hidden, width = wd_ref.shape
    if routed:
        gate_pre = sum_pieces(x, wg_refs)
        up_pre = sum_pieces(x, wu_refs)
    else:
        pre = sum_pieces(x, wgu_refs)
        gate_pre, up_pre = pre[:, :hidden], pre[:, hidden:]
    sigma = jax.nn.sigmoid(gate_pre)
    swish = gate_pre * sigma
    active = (swish * up_pre).astype(BF16)
    rest[0][...] = active
    cot = cot_ref[...].astype(F32)
    scale = scale_ref[...]
    grad_result = (scale * cot).astype(BF16)
    rest[1][...] = grad_result
    grad_active = dot_last(grad_result, wd_ref[...])
    grad_up = grad_active * swish
    grad_gate = grad_active * up_pre * (sigma * (1.0 + gate_pre * (1.0 - sigma)))
    result = dot(active, wd_ref[...])
    if routed:
        result = result.astype(BF16).astype(F32)
    inner = jnp.sum(cot * result, axis=1, keepdims=True)
    part = scale * result
    block = width // quads
    if not routed:
        part_ref, grad_ref, inner_ref, both_ref = rest[2:]
        both = jnp.concatenate([grad_gate, grad_up], axis=1).astype(BF16)
        both_ref[...] = both
        part_ref[...] = part.astype(BF16)
        for key in range(quads):
            grad = dot_last(both, wgu_refs[key][...])
            grad_ref[:, key * block : (key + 1) * block] = grad.astype(BF16)
        inner_ref[...] = inner
        return
    part_refs, grad_refs, gate_ref, up_ref = rest[2:4], rest[4:6], rest[6], rest[7]
    grad_gate, grad_up = grad_gate.astype(BF16), grad_up.astype(BF16)
    gate_ref[...] = grad_gate
    up_ref[...] = grad_up
    part = (part + part_in[...].astype(F32)).astype(BF16)
    for ref in part_refs:
        ref[...] = part
    for key in range(quads):
        cols = slice(key * block, (key + 1) * block)
        grad = dot_last(grad_gate, wg_refs[key][...]) + dot_last(grad_up, wu_refs[key][...])
        grad = (grad.astype(BF16).astype(F32) + grad_in[:, cols].astype(F32)).astype(BF16)
        for ref in grad_refs:
            ref[:, cols] = grad
    lane = lane_ref[...]
    extra = jnp.zeros((x.shape[0], LANES), F32)
    for slot, value in enumerate((inner, dot_in[...])):
        high = value.astype(BF16).astype(F32)
        extra = extra + jnp.where(lane == 2 * slot, high, 0.0)
        extra = extra + jnp.where(lane == 2 * slot + 1, value - high, 0.0)
    for ref in grad_refs:
        ref[:, width:] = extra.astype(BF16)


def expert(core, x, pieces, wd, hidden, cot, scale, routed=()):
    rows, width = x.shape
    tiles = rows // TILE
    quads = len(pieces) // 2 if routed else len(pieces)
    spec = lambda columns: turned_spec(columns, tiles)
    ins = [spec(width), whole((hidden, width)), spec(width), spec(1)]
    ins += [whole(piece.shape) for piece in pieces]
    outs = [spec(hidden), spec(width)]
    shapes = [shaped(rows, hidden, BF16), shaped(rows, width, BF16)]
    if routed:
        ins += [spec(width), spec(width), spec(1), whole((1, LANES))]
        for columns in (width, width + LANES):
            specs, halves = halves_specs(columns, tiles)
            outs, shapes = outs + specs, shapes + halves
        outs += [spec(hidden), spec(hidden)]
        shapes += [shaped(rows, hidden, BF16)] * 2
    else:
        outs += [spec(width), spec(width), spec(1), spec(2 * hidden)]
        shapes += [shaped(rows, width, BF16)] * 2
        shapes += [shaped(rows, 1, F32), shaped(rows, 2 * hidden, BF16)]
    return call(
        functools.partial(expert_kernel, bool(routed), quads),
        (tiles,),
        ins,
        outs,
        shapes,
        60,
        12 * rows * width * hidden,
        name="expert" if routed else "shared",
        scalars=1,
    )(core[None], x, wd, cot, scale, *pieces, *routed)


def reversed_bits(value, count):
    return sum((((value >> k) & 1) << (count - 1 - k) for k in range(count)), 0 * value)


def places(step, quads, up):
    if up:
        return step & 1, reversed_bits(step >> 1, quads.bit_length() - 2)
    half = quads // 2
    return jnp.where(step < half, 0, 1), jnp.where(step < half, step, step - half)


def stack_specs(quads, up, rows, columns, merged):
    quarter = quads // 4

    def spec(half, part):
        def index(step, *_):
            if up:
                return places(step, quads, up)[1] % quarter, 0
            first = half * 2 * quarter + part * quarter
            return jnp.clip(step - first, 0, quarter - 1), 0

        return pl.BlockSpec((rows, columns), index)

    def joined(step, *_):
        if up:
            return places(step, quads, up)[1], 0
        return jnp.clip(step - 2 * quarter, 0, 2 * quarter - 1), 0

    specs = [spec(0, 0), spec(0, 1)]
    shapes = [shaped(quarter * rows, columns, BF16)] * 2
    if merged:
        specs.append(pl.BlockSpec((rows, columns), joined))
        shapes.append(shaped(2 * quarter * rows, columns, BF16))
    else:
        specs += [spec(1, 0), spec(1, 1)]
        shapes += [shaped(quarter * rows, columns, BF16)] * 2
    return specs, shapes


def store_stack(step, quads, up, merged, outs, value):
    half, index = places(step, quads, up)
    part = index // (quads // 4)
    for number, out in enumerate(outs):
        wanted = (half == number // 2) & ((part == number % 2) | (merged and number == 2))

        @pl.when(wanted)
        def _():
            out[...] = value


def row_grads_kernel(quads, cuts, x_ref, grad_ref, *outs):
    step = pl.program_id(0)
    total = dot_first(x_ref[...], grad_ref[...]).astype(BF16)
    first = 0
    for low, high, up, merged in cuts:
        count = 3 if merged else 4
        store_stack(step, quads, up, merged, outs[first : first + count], total[:, low:high])
        first += count


def row_grads(rows, grads, quads, cuts):
    count, width = rows.shape
    columns = grads.shape[1]
    block = width // quads
    specs, shapes = [], []
    for low, high, up, merged in cuts:
        more = stack_specs(quads, up, block, high - low, merged)
        specs, shapes = specs + more[0], shapes + more[1]
    outs = call(
        functools.partial(row_grads_kernel, quads, cuts),
        (quads,),
        [pl.BlockSpec((count, block), lambda i: (0, i)), whole((count, columns))],
        specs,
        shapes,
        48,
        2 * count * width * columns,
        name="row_grads",
    )(rows, grads)
    found = []
    for _, _, _, merged in cuts:
        size = 3 if merged else 4
        found.append((outs[:2], outs[2:size]))
        outs = outs[size:]
    return found


def column_grads_kernel(quads, up, quad_ref, act_ref, grad_ref, *outs):
    total = dot_first(act_ref[...], grad_ref[...]).astype(BF16)
    store_stack(pl.program_id(0), quads, up, True, outs, total)


def column_grads(acts, grads, quad, quads, up):
    count, hidden = acts.shape
    width = grads.shape[1]
    block = width // quads
    specs, shapes = stack_specs(quads, up, hidden, block, True)
    outs = pl.pallas_call(
        functools.partial(column_grads_kernel, quads, up),
        grid_spec=pltpu.PrefetchScalarGridSpec(
            num_scalar_prefetch=1,
            grid=(quads,),
            in_specs=[
                pl.BlockSpec((count, hidden), lambda i, own: (0, 0)),
                pl.BlockSpec((count, block), lambda i, own: (0, own[0] ^ i)),
            ],
            out_specs=specs,
        ),
        out_shape=shapes,
        compiler_params=pltpu.CompilerParams(vmem_limit_bytes=48 * MIB),
        cost_estimate=pl.CostEstimate(
            flops=2 * count * hidden * width,
            bytes_accessed=2 * (count * (hidden + width) + hidden * width),
            transcendentals=0,
        ),
        name="column_grads",
    )(quad[None], acts, grads)
    return outs[:2], outs[2:]


def down_grads_kernel(quads, quad_ref, act_ref, grad_ref, *rest):
    outs, total_ref = rest[:-1], rest[-1]
    step = pl.program_id(0)
    total_ref[...] = dot_first(act_ref[...], grad_ref[...])
    size = total_ref.shape[0] // quads
    quarter = quads // 4
    for part, up in enumerate((True, False)):

        @pl.when(step == part)
        def _():
            for key in range(quads):
                first = pl.multiple_of((quad_ref[0] ^ key) * size, 8)
                half, index = (int(v) for v in place_of(key, quads, up))
                number = 2 if half else index // quarter
                row = (index if half else index % quarter) * size
                outs[part * 3 + number][row : row + size, :] = total_ref[
                    pl.ds(first, size), :
                ].astype(BF16)


def place_of(key, quads, up):
    count = quads.bit_length() - 1
    spot = reversed_bits(key, count) if up else key
    return spot // (quads // 2), spot % (quads // 2)


def down_grads(acts, grads, quad, quads):
    count, hidden = acts.shape
    cut = grads.shape[1] // 2
    rows = hidden // 4
    shapes = [shaped(rows, cut, BF16), shaped(rows, cut, BF16), shaped(2 * rows, cut, BF16)] * 2
    outs = pl.pallas_call(
        functools.partial(down_grads_kernel, quads),
        grid_spec=pltpu.PrefetchScalarGridSpec(
            num_scalar_prefetch=1,
            grid=(2,),
            in_specs=[
                pl.BlockSpec((count, hidden), lambda i, own: (0, 0)),
                pl.BlockSpec((count, cut), lambda i, own: (0, i)),
            ],
            out_specs=[pl.BlockSpec(shape.shape, lambda i, own: (0, 0)) for shape in shapes],
            scratch_shapes=[pltpu.VMEM((hidden, cut), F32)],
        ),
        out_shape=shapes,
        compiler_params=pltpu.CompilerParams(vmem_limit_bytes=48 * MIB),
        cost_estimate=pl.CostEstimate(
            flops=4 * count * hidden * cut,
            bytes_accessed=2 * (count * (hidden + 2 * cut) + 2 * hidden * cut),
            transcendentals=0,
        ),
        name="down_grads",
    )(quad[None], acts, grads)
    return (outs[:2], outs[2:3]), (outs[3:5], outs[5:])


def local(
    residual_in,
    attention_gain,
    query_weight,
    query_bias,
    key_weight,
    key_bias,
    value_weight,
    value_bias,
    output_weight,
    feedforward_gain,
    router_weight,
    shared_logit_weight,
    shared_gate_weight,
    shared_up_weight,
    shared_down_weight,
    expert_gate,
    expert_up,
    expert_down,
    cotangent,
    expert_index,
    token_live,
    document_lengths,
):
    ep_count = lax.axis_size("ep")
    grp_count = lax.axis_size("grp")
    quads = grp_count // 2
    rows_dev, width = residual_in.shape
    group_rows = rows_dev * ep_count
    pair_rows = 2 * group_rows
    seq_len = group_rows * grp_count // SEQS
    expert_count = expert_gate.shape[0] * ep_count
    ffe = expert_gate.shape[2]
    ffs_half = shared_gate_weight.shape[1] // 2
    grp = lax.axis_index("grp")
    ep = lax.axis_index("ep")
    core = grp % 2
    quad = grp // 2
    back = -(-WINDOW // pair_rows)
    heads = query_weight.shape[1] // HDIM // 2
    head_width = heads * HDIM
    up_order = quad_bits()
    down_order = up_order[::-1]

    block = width // quads
    cut = len(up_order) // 2
    up_one, up_two = up_order[:cut], up_order[cut:]
    down_one, down_two = down_order[: len(down_order) - cut], down_order[len(down_order) - cut :]
    ep_masks = [1 << b for b in range(ep_count.bit_length() - 1)]
    quad_masks = [2 * bit for bit in up_order]
    seq_groups = grp_count // SEQS
    experts = jnp.arange(expert_count, dtype=jnp.int32)
    ed_cut = width // 2

    def shifted(values, steps):
        route = [
            (i, i + 2 * steps)
            for i in range(grp_count)
            if 0 <= i + 2 * steps < grp_count and i // seq_groups == (i + 2 * steps) // seq_groups
        ]
        return lax.ppermute(values, "grp", route)

    def gathered(values):
        return lax.all_gather(values, "ep", axis=0, tiled=True)

    def scattered(values):
        return lax.psum_scatter(values, "ep", scatter_dimension=0, tiled=True)

    def core_sum(kept, other):
        return add_rows(kept, across(other, 1))

    def finished(kept, arrived, axis):
        mine, other = finish(core[None], kept, arrived, axis)
        return mine, across(other, 1)

    hidden_in = residual_in.astype(F32)
    grad_out = cotangent.astype(F32)
    gain_one = attention_gain.astype(F32)
    gain_two = feedforward_gain.astype(F32)
    router_all = jnp.concatenate([router_weight, shared_logit_weight[:, None]], axis=1)
    router_flipped = flip_columns(router_all.T, quad).T
    scale_one = norm_scale(hidden_in)
    unit_one = hidden_in * scale_one
    normed_one = (unit_one * gain_one).astype(BF16)
    group_one = gathered(flip_columns(normed_one, quad))

    qk_keep, qk_other = zip(
        *[split_core(weight, core, 1) for weight in (query_weight, key_weight, value_weight)]
    )
    qkv_keep, qkv_other = jnp.concatenate(qk_keep, 1), jnp.concatenate(qk_other, 1)
    qkv_block = merge_core(qkv_keep, across(qkv_other, 1), core, 0)
    qkv_cut = qkv_block.shape[1] // 2
    qkv_a = {0: qkv_block[:, :qkv_cut]}
    qkv_b = {0: qkv_block[:, qkv_cut:]}
    (
        qkv_a, qkv_b, output_weight, shared_gate_weight, shared_up_weight, shared_down_weight,
        expert_gate, expert_up, expert_down,
    ) = together(
        qkv_a, qkv_b, output_weight, shared_gate_weight, shared_up_weight, shared_down_weight,
        expert_gate, expert_up, expert_down,
    )
    qkv_a_one, qkv_a_two = gather_quads(qkv_a, up_one), gather_quads(qkv_a, up_two)
    qkv_b_one, qkv_b_two = gather_quads(qkv_b, down_one), gather_quads(qkv_b, down_two)

    o_keep, o_other = split_core(output_weight, core, 0)
    sg_keep, sg_other = split_core(shared_gate_weight, core, 1)
    su_keep, su_other = split_core(shared_up_weight, core, 1)
    gu_keep = jnp.concatenate([sg_keep, su_keep], axis=1)
    gu_other = jnp.concatenate([sg_other, su_other], axis=1)
    gu_block = merge_core(gu_keep, across(gu_other, 1), core, 0)
    sd_keep, sd_other = split_core(shared_down_weight, core, 0)
    sd_keep = jnp.concatenate([sd_keep, o_keep], axis=0)
    sd_other = jnp.concatenate([sd_other, o_other], axis=0)
    sd_block = merge_core(sd_keep, across(sd_other, 1), core, 1)

    def expert_block(weight):
        keep, other = split_core(weight, core, 0)
        return merge_core(keep[0], across(other[0], 1), core, 0)

    eg_block, eu_block, ed_block = [
        expert_block(weight) for weight in (expert_gate, expert_up, expert_down)
    ]
    eda_block, edb_block = ed_block[:, :ed_cut], ed_block[:, ed_cut:]

    (
        qkv_a_one, qkv_a_two, qkv_b_one, qkv_b_two, gu_block, sd_block, eg_block, eu_block,
        eda_block, edb_block,
    ) = together(
        qkv_a_one, qkv_a_two, qkv_b_one, qkv_b_two, gu_block, sd_block, eg_block, eu_block,
        eda_block, edb_block,
    )
    qkv_a_rest = gather_rest(qkv_a_one, up_two)
    qkv_b_rest = gather_rest(qkv_b_one, down_two)
    sd_one, sd_two = gather_quads({0: sd_block}, down_one), gather_quads({0: sd_block}, down_two)
    chosen = (
        (expert_index[:, :, None] == experts[None, None, :]) & (token_live[:, None, None] > 0)
    ).any(axis=1)
    cot_packed = jnp.concatenate(
        [cotangent, jnp.pad(chosen.astype(BF16), ((0, 0), (0, LANES - expert_count)))], axis=1
    )
    chosen = chosen.astype(F32)
    bias = jnp.concatenate(
        [split_core(b, core, 0)[0] for b in (query_bias, key_bias, value_bias)]
    ).astype(F32)[None, :]
    key_place = (quad - back) * pair_rows + jnp.arange((back + 1) * pair_rows, dtype=jnp.int32)
    query_place = key_place[back * pair_rows :]
    _, position = doc_layout(document_lengths, seq_len, query_place)
    low = jnp.maximum(query_place - position, query_place - WINDOW + 1)[:, None]
    high, key_place = query_place[:, None], key_place[None, :]
    cosine, sine = rope_tables(position)
    (
        group_one, qkv_a, qkv_b, sd_one, sd_two, gu_block, eg_block, eu_block, eda_block,
         edb_block, cot_packed, bias, cosine, sine, low, high,
    ) = together(
        group_one, qkv_a_one | qkv_a_two | qkv_a_rest, qkv_b_one | qkv_b_two | qkv_b_rest,
        sd_one, sd_two, gu_block, eg_block, eu_block, eda_block, edb_block, cot_packed, bias,
        cosine, sine, low, high,
    )

    rows_one = join_rows(core, group_one, across(group_one, 1))
    gu_two = gather_quads({0: gu_block}, up_two)
    sd_rest = gather_rest(sd_one, down_two)
    cot_group = gathered(cot_packed)
    qkv_a, qkv_b = listed(qkv_a), listed(qkv_b)
    query, key_value = project(rows_one, qkv_a, qkv_b, bias, cosine, sine, heads)

    before = [shifted(key_value, step) for step in range(back, 0, -1)]
    down_full = place_quads(sd_one | sd_two | sd_rest, quad, 1)
    query, before, gu_two, edb_block, down_full = together(
        query, before, gu_two, edb_block, down_full
    )
    edb_one, edb_two = gather_quads({0: edb_block}, down_one), gather_quads({0: edb_block}, down_two)
    attended, log_total = attend(query, before, key_value, key_place, low, high)
    output_rows = down_full[ffs_half:]
    kept, other = split_core(attended, core, 0)
    other = dot(other, output_rows).astype(BF16)
    kept, other, cot_group, edb_one, edb_two = together(kept, other, cot_group, edb_one, edb_two)
    branch = add_rows(dot(kept, output_rows).astype(BF16), across(other, 1))
    branch, gu_block, eu_block, eda_block, cot_group = together(
        branch, gu_block, eu_block, eda_block, cot_group
    )
    branch_sum = scattered(branch)
    cot_other = across(cot_group, 1)
    gu_one = gather_quads({0: gu_block}, up_one)
    eda_one, eda_two = gather_quads({0: eda_block}, up_one), gather_quads({0: eda_block}, up_two)
    eu_one = gather_quads({0: eu_block}, down_one)
    ed_full = jnp.zeros((eda_block.shape[0] * quads, width), BF16)
    ed_full = place_quads(edb_one | edb_two, quad, 0, ed_full, ed_cut)
    branch_sum, cot_other, gu_one, eda_one, eda_two, eu_one, eg_block, edb_one, ed_full = (
        together(
            branch_sum, cot_other, gu_one, eda_one, eda_two, eu_one, eg_block, edb_one, ed_full,
        )
    )

    eg_one = gather_quads({0: eg_block}, up_one)
    edb_rest = gather_rest(edb_one, down_two)
    gu_rest, eda_rest = gather_rest(gu_one, up_two), gather_rest(eda_one, up_two)
    mixed = hidden_in + branch_sum.astype(F32)
    scale_two = norm_scale(mixed)
    unit_two = mixed * scale_two
    normed_two = (unit_two * gain_two).astype(BF16)
    group_two = gathered(flip_columns(normed_two, quad))
    cot_rows = join_rows(core, cot_group, cot_other)
    ed_full = place_quads(eda_one | eda_two, quad, 0, ed_full)
    (
        group_two, eg_one, edb_rest, gu_rest, eda_rest, eu_block, eg_block, eu_one, cot_rows,
        ed_full,
    ) = together(
        group_two, eg_one, edb_rest, gu_rest, eda_rest, eu_block, eg_block, eu_one, cot_rows,
        ed_full,
    )
    eu_two, eg_two = gather_quads({0: eu_block}, down_two), gather_quads({0: eg_block}, up_two)
    eu_rest, eg_rest = gather_rest(eu_one, down_two), gather_rest(eg_one, up_two)
    rows_two = join_rows(core, group_two, across(group_two, 1))
    gu_pieces = listed(gu_one | gu_two | gu_rest)

    def router(rows, weight):
        logits = dot(rows, weight)
        return jax.nn.softmax(logits[:, :expert_count], axis=-1), jax.nn.sigmoid(
            logits[:, expert_count:]
        )

    chosen_rows = cot_rows[:, width : width + expert_count].astype(F32)
    probs_rows, shared_scale_rows = router(rows_two, router_flipped)
    router_probs, shared_scale = router(normed_two, router_all)
    mine = (experts == ep * 2 + core).astype(F32)[None, :]
    gate = jnp.sum(probs_rows * chosen_rows * mine, axis=1, keepdims=True)

    shared_active, grad_shared_out, part, grad_part, shared_dot, grad_gu = expert(
        core, rows_two, gu_pieces, down_full, ffs_half, cot_rows, shared_scale_rows
    )
    gu_cut = 2 * ffs_half * 3 // 4 // LANES * LANES
    (gua_grad, gua_out), (gub_grad, gub_out) = row_grads(
        rows_two, grad_gu, quads, [(0, gu_cut, True, True), (gu_cut, 2 * ffs_half, False, True)]
    )
    sd_grad, sd_out = column_grads(shared_active, grad_shared_out, quad, quads, False)
    gua_grad, eda_rest, edb_rest, ed_full = together(gua_grad, eda_rest, edb_rest, ed_full)
    ed_full = place_quads(eda_rest, quad, 0, ed_full)
    ed_full = place_quads(edb_rest, quad, 0, ed_full, ed_cut)
    (
        grad_part, part, eu_two, eg_two, eu_rest, eg_rest, ed_full, gua_grad, gua_out, gub_grad,
        gub_out, sd_grad, sd_out, gate,
    ) = together(
        grad_part, part, eu_two, eg_two, eu_rest, eg_rest, ed_full, gua_grad, gua_out, gub_grad,
        gub_out, sd_grad, sd_out, gate,
    )
    eg_pieces, eu_pieces = eg_one | eg_two | eg_rest, eu_one | eu_two | eu_rest

    def sent(blocks, bit):
        return [across(part, 2 * bit) for part in blocks]

    gua_sent, gub_sent = sent(gua_out, up_order[0]), sent(gub_out, down_order[0])
    sd_sent = sent(sd_out, down_order[0])

    lanes = jnp.arange(LANES, dtype=jnp.int32)
    lanes = jnp.where(lanes % expert_count == ep * 2 + core, lanes // expert_count, -1)[None, :]
    active, grad_result, *sums, grad_gate_pre, grad_up_pre = expert(
        core,
        rows_two,
        listed(eg_pieces) + listed(eu_pieces),
        ed_full,
        ffe,
        cot_rows,
        gate,
        (part, grad_part, shared_dot, lanes),
    )
    sums, gua_sent, gub_sent, sd_sent, gua_grad, gub_grad, sd_grad = together(
        sums, gua_sent, gub_sent, sd_sent, gua_grad, gub_grad, sd_grad
    )
    forward_part, packed = sums[:2], core_sum(*sums[2:])
    gua_grad = first_sum(gua_grad, gua_sent)
    gub_grad = first_sum(gub_grad, gub_sent)
    sd_grad = first_sum(sd_grad, sd_sent)
    (
        packed, gua_grad, gub_grad, sd_grad, active, grad_result, grad_gate_pre, grad_up_pre,
    ) = together(
        packed, gua_grad, gub_grad, sd_grad, active, grad_result, grad_gate_pre, grad_up_pre,
    )
    spread = scattered(packed)
    gua_sent, gub_sent = across(gua_grad[1], 2 * up_order[1]), across(gub_grad[1], 2 * down_order[1])
    sd_sent = across(sd_grad[1], 2 * down_order[1])
    (eda_grad, eda_out), (edb_grad, edb_out) = down_grads(active, grad_result, quad, quads)
    eda_out, edb_out, grad_gate_pre, grad_up_pre, gua_sent, gub_sent, sd_sent = together(
        eda_out, edb_out, grad_gate_pre, grad_up_pre, gua_sent, gub_sent, sd_sent
    )
    eda_sent, edb_sent = sent(eda_out, up_order[0]), sent(edb_out, down_order[0])
    ((eg_grad, eg_out),) = row_grads(rows_two, grad_gate_pre, quads, [(0, ffe, True, False)])
    ((eu_grad, eu_out),) = row_grads(rows_two, grad_up_pre, quads, [(0, ffe, False, False)])
    spread, eg_grad, eg_out = together(spread, eg_grad, eg_out)

    grad_normed_two = flip_columns(spread[:, :width], quad).astype(F32)
    side = spread[:, width : width + 4 * expert_count].astype(F32).reshape(rows_dev, 4, expert_count)
    grad_gate_own = side[:, 0] + side[:, 1]
    shared_dot_own = jnp.sum(side[:, 2] + side[:, 3], axis=1, keepdims=True)
    grad_logit = shared_dot_own * shared_scale * (1.0 - shared_scale)
    grad_probs = grad_gate_own * chosen
    grad_logits = router_probs * (
        grad_probs - jnp.sum(router_probs * grad_probs, axis=-1, keepdims=True)
    )
    grad_router = jnp.concatenate([grad_logits, grad_logit], axis=1)
    router_grad = dot_first(normed_two.astype(F32), grad_router)
    grad_normed_two = grad_normed_two + dot_last(grad_router, router_all.astype(F32))
    grad_norm_part, ff_gain_grad = norm_backward(grad_normed_two, unit_two, scale_two, gain_two)
    grad_mixed = grad_out + grad_norm_part
    (
        branch_low, eda_grad, eda_sent, edb_grad, edb_sent, gua_grad, gua_sent, gub_grad, gub_sent,
        sd_grad, sd_sent, eg_out, eu_grad, eu_out, forward_part,
    ) = together(
        grad_mixed.astype(BF16), eda_grad, eda_sent, edb_grad, edb_sent, gua_grad, gua_sent, gub_grad,
        gub_sent, sd_grad, sd_sent, eg_out, eu_grad, eu_out, forward_part,
    )
    group_branch = gathered(branch_low)
    eg_sent = sent(eg_out[:1], up_order[0])
    eu_sent = sent(eu_out[:1], down_order[0])
    forward_part = core_sum(*forward_part)
    forward_part, gua_grad, gua_sent, gub_grad, gub_sent, sd_grad, sd_sent = together(
        forward_part, gua_grad, gua_sent, gub_grad, gub_sent, sd_grad, sd_sent
    )
    eda_grad = first_sum(eda_grad, eda_sent)
    edb_grad = first_sum(edb_grad, edb_sent)
    eda_sent, edb_sent = across(eda_grad[1], 2 * up_order[1]), across(edb_grad[1], 2 * down_order[1])

    gua_mine, gua_arrived = finished(*rest_parts(gua_grad[0], gua_sent, up_order), 0)
    gub_mine, gub_arrived = finished(*rest_parts(gub_grad[0], gub_sent, down_order), 0)
    sd_mine, sd_arrived = finished(*rest_parts(sd_grad[0], sd_sent, down_order), 1)
    gu_mine = jnp.concatenate([gua_mine, gub_mine], axis=1)
    gu_arrived = jnp.concatenate([gua_arrived, gub_arrived], axis=1)
    sg_grad, su_grad = [
        merge_core(
            gu_mine[:, part * ffs_half : (part + 1) * ffs_half],
            gu_arrived[:, part * ffs_half : (part + 1) * ffs_half],
            core,
            1,
        ).astype(F32)
        for part in range(2)
    ]
    sd_grad = merge(core, sd_mine, sd_arrived, 0)
    (
        group_branch, forward_part, sg_grad, su_grad, sd_grad, eg_grad, eg_out, eg_sent, eu_grad, eu_out, eu_sent, eda_grad,
        eda_sent, edb_grad, edb_sent,
    ) = together(
        group_branch, forward_part, sg_grad, su_grad, sd_grad, eg_grad, eg_out, eg_sent, eu_grad, eu_out, eu_sent, eda_grad,
        eda_sent, edb_grad, edb_sent,
    )
    grad_branch = join_rows(core, group_branch, across(group_branch, 1))
    eg_sent = eg_sent + sent(eg_out[1:], up_order[0])
    eu_sent = eu_sent + sent(eu_out[1:], down_order[0])

    layer_sum = scattered(forward_part)
    grad_attended = dot_last(grad_branch, down_full[ffs_half:]).astype(BF16)
    grad_query, grad_own, *grad_before = attend_back(
        query, grad_attended, log_total, before, key_value, key_place, low, high, cosine, sine
    )
    (
        grad_query, grad_before, grad_branch, eg_grad, eu_grad,
    ) = together(
        grad_query, grad_before, grad_branch, eg_grad, eu_grad,
    )
    arrived = [shifted(sent, step - back) for step, sent in enumerate(grad_before)]
    cut = eg_grad[1].shape[0] // 2
    eg_grad = [
        add_low(eg_grad[0], eg_sent[0]),
        add_low(eg_grad[1][:cut], eg_sent[1][:cut]),
        add_low(eg_grad[1][cut:], eg_sent[1][cut:]),
    ]
    eu_grad = [
        add_low(eu_grad[0], eu_sent[0]),
        add_low(eu_grad[1][:cut], eu_sent[1][:cut]),
        add_low(eu_grad[1][cut:], eu_sent[1][cut:]),
    ]
    eg_rest = across(eg_grad[1], 2 * up_order[1])
    arrived, eg_grad, eu_grad, grad_branch = together(arrived, eg_grad, eu_grad, grad_branch)
    eu_rest = across(eu_grad[1], 2 * down_order[1])
    (*partial, att_gain_part, bias_part), (qkv_a_grad, qkv_a_out), (qkv_b_grad, qkv_b_out) = collect(
        core, grad_query, grad_own, cosine, sine, rows_one, arrived, qkv_a, qkv_b
    )
    partial, qkv_a_out, qkv_b_out, eg_grad, eg_rest, eu_grad, eu_rest = together(
        partial, qkv_a_out, qkv_b_out, eg_grad, eg_rest, eu_grad, eu_rest
    )
    eg_last, eu_last = across(eg_grad[2], 2 * up_order[1]), across(eu_grad[2], 2 * down_order[1])
    qkv_a_sent, qkv_b_sent = sent(qkv_a_out, up_order[0]), sent(qkv_b_out, down_order[0])
    partial_sum = core_sum(*partial)

    (
        partial_sum, att_gain_part, bias_part, grad_branch, qkv_a_grad, qkv_b_grad, eda_grad,
        eda_sent, edb_grad, edb_sent,
    ) = together(
        partial_sum, att_gain_part, bias_part, grad_branch, qkv_a_grad, qkv_b_grad, eda_grad,
        eda_sent, edb_grad, edb_sent,
    )
    grad_normed_one = scattered(partial_sum)
    o_grad, o_out = column_grads(attended, grad_branch, quad, quads, False)
    att_gain_part = flip_columns(att_gain_part[0], quad) / gain_one
    late = jnp.concatenate([att_gain_part, ff_gain_grad, router_grad.T.reshape(-1)])
    late = sum_everywhere(late, [], ep_masks)
    o_sent = sent(o_out, down_order[0])
    (
        late, qkv_a_sent, qkv_b_sent, eg_last, eu_last, eda_sent, edb_sent,
    ) = together(
        late, qkv_a_sent, qkv_b_sent, eg_last, eu_last, eda_sent, edb_sent,
    )
    eg_rest = jnp.concatenate([eg_rest, eg_last], axis=0)
    eu_rest = jnp.concatenate([eu_rest, eu_last], axis=0)
    bias_part = bias_part.reshape(3, head_width)
    bias_part = jnp.concatenate(
        [jnp.where(core == 0, bias_part, 0.0), jnp.where(core == 0, 0.0, bias_part)], axis=1
    )
    late = sum_everywhere(jnp.concatenate([late, bias_part.reshape(-1)]), [1], [])
    qkv_a_grad = first_sum(qkv_a_grad, qkv_a_sent)
    qkv_b_grad = first_sum(qkv_b_grad, qkv_b_sent)
    qkv_a_rest = across(qkv_a_grad[1], 2 * up_order[1])
    qkv_b_rest = across(qkv_b_grad[1], 2 * down_order[1])
    o_grad = first_sum(o_grad, o_sent)
    o_rest = across(o_grad[1], 2 * down_order[1])
    late = sum_everywhere(late, quad_masks, [])
    eg_grad = merge(core, *finished(*rest_parts(eg_grad[0], eg_rest, up_order), 0), None)
    eu_grad = merge(core, *finished(*rest_parts(eu_grad[0], eu_rest, down_order), 0), None)
    eda_mine, eda_arrived = finished(*rest_parts(eda_grad[0], eda_sent, up_order), 0)
    edb_mine, edb_arrived = finished(*rest_parts(edb_grad[0], edb_sent, down_order), 0)
    ed_grad = jnp.concatenate(
        [merge(core, eda_mine, eda_arrived, None), merge(core, edb_mine, edb_arrived, None)], axis=2
    )
    layer_out = (mixed + layer_sum.astype(F32)).astype(BF16)
    qkv_a_mine, qkv_a_arrived = finished(*rest_parts(qkv_a_grad[0], qkv_a_rest, up_order), 0)
    qkv_b_mine, qkv_b_arrived = finished(*rest_parts(qkv_b_grad[0], qkv_b_rest, down_order), 0)
    o_mine, o_arrived = finished(*rest_parts(o_grad[0], o_rest, down_order), 1)
    (
        grad_normed_one, qkv_a_mine, qkv_a_arrived, qkv_b_mine, qkv_b_arrived, o_mine, o_arrived,
        late, eu_grad, eg_grad, ed_grad, layer_out,
    ) = together(
        grad_normed_one, qkv_a_mine, qkv_a_arrived, qkv_b_mine, qkv_b_arrived, o_mine, o_arrived,
        late, eu_grad, eg_grad, ed_grad, layer_out,
    )
    qkv_mine = jnp.concatenate([qkv_a_mine, qkv_b_mine], axis=1)
    qkv_arrived = jnp.concatenate([qkv_a_arrived, qkv_b_arrived], axis=1)
    q_grad, k_grad, v_grad = [merge(core, qkv_mine, qkv_arrived, 1, part, 3) for part in range(3)]
    o_grad = merge(core, o_mine, o_arrived, 0)
    att_gain_grad, ff_gain_grad = late[:width], late[width : 2 * width]
    router_grad = late[2 * width : (expert_count + 3) * width].reshape(expert_count + 1, width)
    bias_mine = late[(expert_count + 3) * width :].reshape(3, 2 * head_width)
    grad_norm_one, _ = norm_backward(
        flip_columns(grad_normed_one, quad).astype(F32), unit_one, scale_one, gain_one
    )
    input_grad = grad_mixed + grad_norm_one
    return (
        layer_out,
        input_grad,
        att_gain_grad,
        q_grad,
        bias_mine[0],
        k_grad,
        bias_mine[1],
        v_grad,
        bias_mine[2],
        o_grad,
        ff_gain_grad,
        router_grad[:expert_count].T,
        router_grad[expert_count],
        sg_grad,
        su_grad,
        sd_grad,
        eg_grad,
        eu_grad,
        ed_grad,
    )


def solution(mesh):
    tokens = P(("grp", "ep"), None)
    rows, columns, experts = P("grp", "ep"), P("ep", "grp"), P("ep", "grp", None)
    in_specs = (
        tokens, P(), rows, P("ep"), rows, P("ep"), rows, P("ep"), columns, P(), P(), P(),
        rows, rows, columns, experts, experts, experts, tokens, tokens, P(("grp", "ep")), P(),
    )
    out_specs = (
        tokens, tokens, P(), rows, P("ep"), rows, P("ep"), rows, P("ep"), columns, P(), P(), P(),
        rows, rows, columns, experts, experts, experts,
    )
    return jax.shard_map(local, mesh=mesh, in_specs=in_specs, out_specs=out_specs, check_vma=False)
```

```python
import functools

import jax
import jax.numpy as jnp
from jax import lax
from jax.experimental import pallas as pl
from jax.experimental.pallas import tpu as pltpu
from jax.sharding import PartitionSpec as P

HDIM = 128
SEQS = 2
DOCS = 4
WINDOW = 1024
EPS = 1e-06
ROPE_BASE = 1000000.0
MASKED = -1e30
F32 = jnp.float32
BF16 = jnp.bfloat16
TILE = 256
LANES = 128
MIB = 1 << 20


def dot(left, right):
    return jnp.dot(left, right, preferred_element_type=F32)


def dot_last(left, right):
    return lax.dot_general(left, right, (((1,), (1,)), ((), ())), preferred_element_type=F32)


def dot_first(left, right):
    return lax.dot_general(left, right, (((0,), (0,)), ((), ())), preferred_element_type=F32)


def across(block, mask):
    count = lax.axis_size("grp")
    return lax.ppermute(block, "grp", [(i, i ^ mask) for i in range(count)])


def quad_bits():
    return [1 << b for b in range((lax.axis_size("grp") // 2).bit_length() - 1)]


def flip_columns(values, quad):
    quads = lax.axis_size("grp") // 2
    axis = values.ndim - 1
    block = values.shape[axis] // quads
    return jnp.concatenate(
        [
            lax.dynamic_slice_in_dim(values, (quad ^ key) * block, block, axis)
            for key in range(quads)
        ],
        axis=axis,
    )


def gather_quads(pieces, order):
    pieces = dict(pieces)
    for bit in order:
        for key, piece in list(pieces.items()):
            pieces[key | bit] = across(piece, 2 * bit)
    return pieces


def add_low(left, right):
    return (left.astype(F32) + right.astype(F32)).astype(BF16)


def first_sum(parts, arrived):
    half = parts[0].shape[0]
    if len(arrived) == 1:
        arrived = (arrived[0][:half], arrived[0][half:])
    return add_low(parts[0], arrived[0]), add_low(parts[1], arrived[1])


def rest_parts(kept, arrived, order):
    for bit in order[2:]:
        stack = add_rows(kept, arrived)
        half = stack.shape[0] // 2
        kept, arrived = stack[:half], across(stack[half:], 2 * bit)
    return kept, arrived


def together(*values):
    return lax.optimization_barrier(values)


def sum_everywhere(values, masks_grp, masks_ep):
    for mask in masks_grp:
        values = values + across(values, mask)
    count = lax.axis_size("ep")
    for mask in masks_ep:
        values = values + lax.ppermute(values, "ep", [(i, i ^ mask) for i in range(count)])
    return values


def gather_rest(pieces, order):
    found = {}
    for key, piece in pieces.items():
        if key:
            found.update({key | k: v for k, v in gather_quads({0: piece}, order).items()})
    return found


def listed(pieces):
    return [pieces[key] for key in sorted(pieces)]


def place_quads(pieces, quad, axis, whole=None, other=0):
    size = pieces[0].shape[axis] if whole is None else whole.shape[axis] // (lax.axis_size("grp") // 2)
    if whole is None:
        shape = list(pieces[0].shape)
        shape[axis] = size * len(pieces)
        whole = jnp.zeros(shape, pieces[0].dtype)
    for key in sorted(pieces):
        start = [other, other]
        start[axis] = (quad ^ key) * size
        whole = lax.dynamic_update_slice(whole, pieces[key], start)
    return whole


def take_quads(whole, quad, quads, axis):
    size = whole.shape[axis] // quads
    return {
        key: lax.dynamic_slice_in_dim(whole, (quad ^ key) * size, size, axis)
        for key in range(quads)
    }


def merge_core(kept, arrived, core, axis):
    first = jnp.where(core == 0, kept, arrived)
    second = jnp.where(core == 0, arrived, kept)
    return jnp.concatenate([first, second], axis=axis)


def split_core(values, core, axis):
    half = values.shape[axis] // 2
    first = lax.slice_in_dim(values, 0, half, axis=axis)
    second = lax.slice_in_dim(values, half, 2 * half, axis=axis)
    return jnp.where(core == 0, first, second), jnp.where(core == 0, second, first)


def norm_scale(values):
    return lax.rsqrt(jnp.mean(values * values, axis=-1, keepdims=True) + EPS)


def norm_backward(grad_normed, unit, scale, gain):
    grad_unit = grad_normed * gain
    inner = jnp.mean(grad_unit * unit, axis=-1, keepdims=True)
    return scale * (grad_unit - unit * inner), jnp.sum(grad_normed * unit, axis=0)


def doc_layout(document_lengths, seq_len, index):
    valid = index >= 0
    safe = jnp.maximum(index, 0)
    seq_of = safe // seq_len
    place = safe % seq_len
    seq_count = document_lengths.shape[0]
    picker = (seq_of[:, None] == jnp.arange(seq_count, dtype=jnp.int32)[None, :]).astype(jnp.int32)
    lengths = jnp.sum(picker[:, :, None] * document_lengths[None, :, :], axis=1)
    ends = jnp.cumsum(lengths, axis=1)
    doc = jnp.sum((ends <= place[:, None]).astype(jnp.int32), axis=1)
    earlier = jnp.arange(DOCS, dtype=jnp.int32)[None, :] < doc[:, None]
    before = jnp.sum(jnp.where(earlier, lengths, 0), axis=1)
    return jnp.where(valid, seq_of * DOCS + doc, -1), place - before


def rope_tables(position):
    half = HDIM // 2
    freq = ROPE_BASE ** (-(jnp.arange(half, dtype=F32) * 2.0 / HDIM))
    angle = position.astype(F32)[:, None] * freq[None, :]
    cosine, sine = jnp.cos(angle), jnp.sin(angle)
    return jnp.concatenate([cosine, cosine], axis=1), jnp.concatenate([-sine, sine], axis=1)


def turn(values, cosine, sine):
    return values * cosine + pltpu.roll(values, HDIM // 2, 1) * sine


def call(kernel, grid, ins, outs, shapes, limit, flops, scratch=(), name=None, scalars=0):
    moved = 0
    for shape in shapes:
        moved += shape.size * shape.dtype.itemsize

    def run(*args):
        total = moved + sum(a.size * a.dtype.itemsize for a in args)
        if flops == 0:
            total = 0
        return pl.pallas_call(
            kernel,
            grid_spec=pltpu.PrefetchScalarGridSpec(
                num_scalar_prefetch=scalars,
                grid=grid,
                in_specs=ins,
                out_specs=outs,
                scratch_shapes=scratch,
            ),
            out_shape=shapes,
            compiler_params=pltpu.CompilerParams(vmem_limit_bytes=limit * MIB),
            cost_estimate=pl.CostEstimate(
                flops=flops, bytes_accessed=total, transcendentals=0
            ),
            name=name,
        )(*args)

    return run


def whole(shape):
    return pl.BlockSpec(shape, lambda *_: (0,) * len(shape), pipeline_mode=pl.Buffered(1))


def rows_spec(columns, tile=TILE):
    return pl.BlockSpec((tile, columns), lambda i, *_: (i, 0))


def turned(step, core, count):
    return (step + (count // 2) * core) % count


def turned_spec(columns, count):
    return pl.BlockSpec((TILE, columns), lambda i, core: (turned(i, core[0], count), 0))


def halves_specs(columns, count):
    half = count // 2
    specs = [
        pl.BlockSpec((TILE, columns), lambda i, core: (jnp.minimum(i, half), 0)),
        pl.BlockSpec((TILE, columns), lambda i, core: (jnp.maximum(i - half, 0), 0)),
    ]
    return specs, [shaped((half + 1) * TILE, columns, BF16), shaped(half * TILE, columns, BF16)]


def add_kernel(left_ref, right_ref, out_ref):
    out_ref[...] = (left_ref[...].astype(F32) + right_ref[...].astype(F32)).astype(BF16)


def add_rows(left, right):
    rows, columns = right.shape
    tile = rows // 4 if rows % 64 == 0 else rows
    return call(
        add_kernel,
        (rows // tile,),
        [rows_spec(columns, tile)] * 2,
        [rows_spec(columns, tile)],
        [shaped(rows, columns, BF16)],
        16,
        0,
        name="add_rows",
    )(left, right)[0]


def join_kernel(core_ref, own_ref, other_ref, out_ref):
    own = pl.program_id(0) // (pl.num_programs(0) // 2) == core_ref[0]

    @pl.when(own)
    def _():
        out_ref[...] = own_ref[...]

    @pl.when(~own)
    def _():
        out_ref[...] = other_ref[...]


def join_rows(core, own, other):
    rows, columns = own.shape
    tile = rows // 4

    def spec(mine):
        def index(i, core):
            place = i - 4 * jnp.where(mine, core[0], 1 - core[0])
            return jnp.clip(place, 0, 3), 0

        return pl.BlockSpec((tile, columns), index)

    return call(
        join_kernel,
        (8,),
        [spec(True), spec(False)],
        [pl.BlockSpec((tile, columns), lambda i, core: (i, 0))],
        [shaped(2 * rows, columns, BF16)],
        24,
        0,
        name="join_rows",
        scalars=1,
    )(core[None], own, other)[0]


def finish_kernel(core_ref, kept_ref, arrived_ref, mine_ref, other_ref):
    total = (kept_ref[...].astype(F32) + arrived_ref[...].astype(F32)).astype(BF16)

    @pl.when(pl.program_id(0) == 0)
    def _():
        other_ref[...] = total

    @pl.when(pl.program_id(0) == 1)
    def _():
        mine_ref[...] = total


def finish(core, kept, arrived, axis):
    rows, columns = kept.shape
    size = (rows // 2, columns) if axis == 0 else (rows, columns // 2)
    if size[0] % 16 or (axis == 1 and size[1] % LANES):
        return split_core(add_low(kept, arrived), core[0], axis)

    def index(i, core):
        half = jnp.where(i == 0, 1 - core[0], core[0])
        return (half, 0) if axis == 0 else (0, half)

    return call(
        finish_kernel,
        (2,),
        [pl.BlockSpec(size, index)] * 2,
        [pl.BlockSpec(size, lambda i, core: (0, 0))] * 2,
        [shaped(*size, BF16)] * 2,
        24,
        0,
        name="finish",
        scalars=1,
    )(core, kept, arrived)


def merge_kernel(core_ref, mine_ref, arrived_ref, out_ref):
    own = pl.program_id(0) == core_ref[0]

    @pl.when(own)
    def _():
        out_ref[...] = mine_ref[...].astype(F32).reshape(out_ref.shape)

    @pl.when(~own)
    def _():
        out_ref[...] = arrived_ref[...].astype(F32).reshape(out_ref.shape)


def merge(core, mine, arrived, axis, part=0, parts=1):
    rows, columns = mine.shape
    columns = columns // parts
    if axis is None:
        shape, size, index = (2, rows, columns), (1, rows, columns), lambda i, core: (i, 0, 0)
    elif axis == 0:
        shape, size, index = (2 * rows, columns), (rows, columns), lambda i, core: (i, 0)
    else:
        shape, size, index = (rows, 2 * columns), (rows, columns), lambda i, core: (0, i)
    return call(
        merge_kernel,
        (2,),
        [pl.BlockSpec((rows, columns), lambda i, core: (0, part))] * 2,
        [pl.BlockSpec(size, index)],
        [jax.ShapeDtypeStruct(shape, F32)],
        24,
        0,
        name="merge",
        scalars=1,
    )(core[None], mine, arrived)[0]


def shaped(rows, columns, dtype):
    return jax.ShapeDtypeStruct((rows, columns), dtype)


def sum_pieces(x, refs):
    block = x.shape[1] // len(refs)
    total = dot(x[:, :block], refs[0][...])
    for key in range(1, len(refs)):
        total = total + dot(x[:, key * block : (key + 1) * block], refs[key][...])
    return total


def project_kernel(heads, quads, x_ref, bias_ref, cos_ref, sin_ref, *rest):
    wa_refs, wb_refs, (q_ref, kv_ref) = rest[:quads], rest[quads : 2 * quads], rest[2 * quads :]
    x = x_ref[...]
    lin = jnp.concatenate([sum_pieces(x, wa_refs), sum_pieces(x, wb_refs)], axis=1) + bias_ref[...]
    cosine, sine = cos_ref[...], sin_ref[...]
    for head in range(3 * heads):
        part = lin[:, head * HDIM : (head + 1) * HDIM]
        if head < 2 * heads:
            part = turn(part, cosine, sine)
        if head < heads:
            q_ref[:, head * HDIM : (head + 1) * HDIM] = part.astype(BF16)
        else:
            kv_ref[:, (head - heads) * HDIM : (head - heads + 1) * HDIM] = part.astype(BF16)


def project(x, wa, wb, bias, cosine, sine, heads):
    rows, width = x.shape
    quads, (block, cut) = len(wa), wa[0].shape
    return call(
        functools.partial(project_kernel, heads, quads),
        (rows // TILE,),
        [rows_spec(width), whole((1, 2 * cut))]
        + [rows_spec(HDIM)] * 2
        + [whole((block, cut))] * (2 * quads),
        [rows_spec(heads * HDIM), rows_spec(2 * heads * HDIM)],
        [shaped(rows, heads * HDIM, BF16), shaped(rows, 2 * heads * HDIM, BF16)],
        32,
        4 * rows * width * cut,
        name="project",
    )(x, bias, cosine, sine, *wa, *wb)


def window_keys(before_refs, own_ref, place, pair_rows, step):
    parts = []
    start = step * TILE
    reach = -WINDOW + start
    for back, ref in enumerate(before_refs):
        first = -(len(before_refs) - back) * pair_rows
        low = max(reach - first, 0)
        if low < pair_rows:
            parts.append(ref[low:, place])
    parts.append(own_ref[max(reach, 0) : start + TILE, place])
    return jnp.concatenate(parts, axis=0) if len(parts) > 1 else parts[0]


def probabilities(query, keys, key_place, low, high, peak):
    scores = dot_last(query, keys) * HDIM ** (-0.5)
    scores = jnp.where((key_place >= low) & (key_place <= high), scores, MASKED)
    if peak is None:
        top = jnp.max(scores, axis=1, keepdims=True)
        weights = jnp.exp(scores - top)
        total = jnp.sum(weights, axis=1, keepdims=True)
        return weights / total, top + jnp.log(total)
    return jnp.exp(scores - peak), peak


def attend_kernel(back, pair_rows, heads, q_ref, *rest):
    before, (own_ref, place_ref, low_ref, high_ref, out_ref, log_ref) = rest[:back], rest[back:]
    for head in range(heads):
        cols = slice(head * HDIM, (head + 1) * HDIM)
        value_cols = slice((heads + head) * HDIM, (heads + head + 1) * HDIM)
        for step in range(pair_rows // TILE):
            rows = slice(step * TILE, (step + 1) * TILE)
            first = back * pair_rows - WINDOW + step * TILE
            places = place_ref[:, max(first, 0) : back * pair_rows + (step + 1) * TILE]
            keys = window_keys(before, own_ref, cols, pair_rows, step)
            values = window_keys(before, own_ref, value_cols, pair_rows, step)
            probs, logs = probabilities(
                q_ref[rows, cols], keys, places, low_ref[rows, :], high_ref[rows, :], None
            )
            out_ref[rows, cols] = dot(probs.astype(BF16), values).astype(BF16)
            log_ref[rows, cols] = jnp.broadcast_to(logs, (TILE, HDIM))


def attend(query, before, own, places, low, high):
    rows, columns = query.shape
    heads = columns // HDIM
    back = len(before)
    return call(
        functools.partial(attend_kernel, back, rows, heads),
        (),
        [pl.BlockSpec(memory_space=pltpu.VMEM)] * (5 + back),
        [pl.BlockSpec(memory_space=pltpu.VMEM)] * 2,
        [shaped(rows, columns, BF16), shaped(rows, columns, F32)],
        40,
        4 * rows * columns * (WINDOW + TILE),
        name="attend",
    )(query, *before, own, places, low, high)


def attend_back_kernel(
    back, pair_rows, heads, core_ref, q_ref, mine_ref, other_ref, weight_ref, log_ref, *rest
):
    before = rest[:back]
    own_ref, place_ref, low_ref, high_ref, cos_ref, sin_ref = rest[back : back + 6]
    dq_ref, own_out = rest[back + 6 : back + 8]
    before_out = rest[back + 8 : 2 * back + 8]
    total_ref, grad_ref = rest[-2:]
    half = pair_rows // 2
    for ref, place in ((mine_ref, core_ref[0]), (other_ref, 1 - core_ref[0])):
        rows = pl.ds(pl.multiple_of(place * half, half), half)
        grad_ref[rows, :] = dot_last(ref[...], weight_ref[...]).astype(BF16)
    total_ref[...] = jnp.zeros_like(total_ref)
    for head in range(heads):
        cols = slice(head * HDIM, (head + 1) * HDIM)
        value_cols = slice((heads + head) * HDIM, (heads + head + 1) * HDIM)
        for step in range(pair_rows // TILE):
            rows = slice(step * TILE, (step + 1) * TILE)
            first = max(back * pair_rows - WINDOW + step * TILE, 0)
            last = back * pair_rows + (step + 1) * TILE
            keys = window_keys(before, own_ref, cols, pair_rows, step)
            values = window_keys(before, own_ref, value_cols, pair_rows, step)
            query, grad = q_ref[rows, cols], grad_ref[rows, cols]
            peak = jnp.concatenate([log_ref[rows, cols]] * ((last - first) // HDIM), axis=1)
            probs, _ = probabilities(
                query, keys, place_ref[:, first:last], low_ref[rows, :], high_ref[rows, :], peak
            )
            grad_probs = dot_last(grad, values)
            inner = jnp.sum(probs * grad_probs, axis=1, keepdims=True)
            grad_scores = (probs * (grad_probs - inner)).astype(BF16)
            grad_query = dot(grad_scores, keys) * HDIM ** (-0.5)
            dq_ref[rows, cols] = turn(grad_query, cos_ref[rows, :], -sin_ref[rows, :]).astype(BF16)
            total_ref[first:last, cols] += dot_first(grad_scores, query) * HDIM ** (-0.5)
            total_ref[first:last, value_cols] += dot_first(probs.astype(BF16), grad)
    own_out[...] = total_ref[back * pair_rows :, :]
    for step in range(back):
        before_out[step][...] = total_ref[step * pair_rows : (step + 1) * pair_rows, :].astype(BF16)


def attend_back(
    core, query, mine, other, weight, logs, before, own, places, low, high, cosine, sine
):
    rows, columns = query.shape
    back = len(before)
    vmem = pl.BlockSpec(memory_space=pltpu.VMEM)
    return call(
        functools.partial(attend_back_kernel, back, rows, columns // HDIM),
        (),
        [vmem] * (11 + back),
        [vmem] * (2 + back),
        [shaped(rows, columns, BF16), shaped(rows, 2 * columns, F32)]
        + [shaped(rows, 2 * columns, BF16)] * back,
        56,
        10 * rows * columns * (WINDOW + TILE),
        scratch=[
            pltpu.VMEM(((back + 1) * rows, 2 * columns), F32),
            pltpu.VMEM((rows, columns), BF16),
        ],
        name="attend_back",
        scalars=1,
    )(
        core[None], query, mine, other, weight, logs, *before, own, places, low, high, cosine, sine
    )


def collect_kernel(heads, back, quads, core_ref, dq_ref, own_ref, cos_ref, sin_ref, x_ref, *rest):
    arrived, wa_refs, wb_refs = rest[:back], rest[back : back + quads], rest[back + quads : back + 2 * quads]
    kept_ref, other_ref, gain_ref, bias_ref, *outs = rest[back + 2 * quads :]
    x_all, grad_all = outs[-2:]
    columns = heads * HDIM
    step = pl.program_id(0)
    total = own_ref[...]
    for ref in arrived:
        total = total + ref[...].astype(F32)
    cosine, sine = cos_ref[...], -sin_ref[...]
    heads_out = [dq_ref[...]]
    for head in range(2 * heads):
        part = total[:, head * HDIM : (head + 1) * HDIM]
        if head < heads:
            part = turn(part, cosine, sine)
        heads_out.append(part.astype(BF16))
    grads = jnp.concatenate(heads_out, axis=1)
    tile = turned(step, core_ref[0], pl.num_programs(0))
    rows = pl.ds(pl.multiple_of(tile * TILE, TILE), TILE)
    x_all[rows, :] = x_ref[...]
    grad_all[rows, :] = grads

    @pl.when(step == 0)
    def _():
        gain_ref[...] = jnp.zeros_like(gain_ref)
        bias_ref[...] = jnp.zeros_like(bias_ref)

    bias_ref[...] += jnp.sum(grads.astype(F32), axis=0, keepdims=True)
    cut = 3 * columns // 2
    block = x_ref.shape[1] // quads
    for key in range(quads):
        cols = slice(key * block, (key + 1) * block)
        part = dot_last(grads[:, :cut], wa_refs[key][...]) + dot_last(grads[:, cut:], wb_refs[key][...])
        kept_ref[:, cols] = part.astype(BF16)
        other_ref[:, cols] = part.astype(BF16)
        gain_ref[:, cols] += jnp.sum(part * x_ref[:, cols].astype(F32), axis=0, keepdims=True)

    @pl.when(step == pl.num_programs(0) - 1)
    def _():
        for key in range(quads):
            weight = dot_first(x_all[:, key * block : (key + 1) * block], grad_all[...]).astype(BF16)
            for part, up in enumerate((True, False)):
                half, index = (int(v) for v in place_of(key, quads, up))
                quarter = quads // 4
                number = 2 if half else index // quarter
                first = (index if half else index % quarter) * block
                outs[part * 3 + number][first : first + block, :] = weight[
                    :, part * cut : (part + 1) * cut
                ]


def collect(core, grad_query, own, cosine, sine, x, arrived, wa, wb):
    rows, columns = grad_query.shape
    width = x.shape[1]
    tiles = rows // TILE
    quads, (block, cut) = len(wa), wa[0].shape
    quarter = width // 4
    fixed = lambda *_: (0, 0)
    halves = halves_specs(width, tiles)
    shapes = [shaped(quarter, cut, BF16), shaped(quarter, cut, BF16), shaped(2 * quarter, cut, BF16)]
    outs = call(
        functools.partial(collect_kernel, columns // HDIM, len(arrived), quads),
        (tiles,),
        [turned_spec(columns, tiles), turned_spec(2 * columns, tiles)]
        + [turned_spec(HDIM, tiles)] * 2
        + [turned_spec(width, tiles)]
        + [turned_spec(2 * columns, tiles)] * len(arrived)
        + [whole((block, cut))] * (2 * quads),
        halves[0]
        + [pl.BlockSpec((1, width), fixed)]
        + [pl.BlockSpec((1, 3 * columns), fixed)]
        + [pl.BlockSpec(shape.shape, fixed) for shape in shapes] * 2,
        halves[1] + [shaped(1, width, F32), shaped(1, 3 * columns, F32)] + shapes * 2,
        60,
        8 * rows * width * cut,
        scratch=[pltpu.VMEM((rows, width), BF16), pltpu.VMEM((rows, 3 * columns), BF16)],
        name="collect",
        scalars=1,
    )(core[None], grad_query, own, cosine, sine, x, *arrived, *wa, *wb)
    return outs[:4], (outs[4:6], outs[6:7]), (outs[7:9], outs[9:])


def expert_kernel(routed, quads, core_ref, x_ref, wd_ref, cot_ref, scale_ref, *rest):
    if routed:
        wg_refs, wu_refs, rest = rest[:quads], rest[quads : 2 * quads], rest[2 * quads :]
        part_in, grad_in, dot_in, lane_ref = rest[:4]
        rest = rest[4:]
    else:
        wgu_refs, rest = rest[:quads], rest[quads:]
    x = x_ref[...]
    hidden, width = wd_ref.shape
    if routed:
        gate_pre = sum_pieces(x, wg_refs)
        up_pre = sum_pieces(x, wu_refs)
    else:
        pre = sum_pieces(x, wgu_refs)
        gate_pre, up_pre = pre[:, :hidden], pre[:, hidden:]
    sigma = jax.nn.sigmoid(gate_pre)
    swish = gate_pre * sigma
    active = (swish * up_pre).astype(BF16)
    rest[0][...] = active
    cot = cot_ref[...].astype(F32)
    scale = scale_ref[...]
    grad_result = (scale * cot).astype(BF16)
    rest[1][...] = grad_result
    grad_active = dot_last(grad_result, wd_ref[...])
    grad_up = grad_active * swish
    grad_gate = grad_active * up_pre * (sigma * (1.0 + gate_pre * (1.0 - sigma)))
    result = dot(active, wd_ref[...])
    if routed:
        result = result.astype(BF16).astype(F32)
    inner = jnp.sum(cot * result, axis=1, keepdims=True)
    part = scale * result
    block = width // quads
    if not routed:
        part_ref, grad_ref, inner_ref, both_ref = rest[2:]
        both = jnp.concatenate([grad_gate, grad_up], axis=1).astype(BF16)
        both_ref[...] = both
        part_ref[...] = part.astype(BF16)
        for key in range(quads):
            grad = dot_last(both, wgu_refs[key][...])
            grad_ref[:, key * block : (key + 1) * block] = grad.astype(BF16)
        inner_ref[...] = inner
        return
    part_refs, grad_refs, gate_ref, up_ref = rest[2:4], rest[4:6], rest[6], rest[7]
    grad_gate, grad_up = grad_gate.astype(BF16), grad_up.astype(BF16)
    gate_ref[...] = grad_gate
    up_ref[...] = grad_up
    part = (part + part_in[...].astype(F32)).astype(BF16)
    for ref in part_refs:
        ref[...] = part
    for key in range(quads):
        cols = slice(key * block, (key + 1) * block)
        grad = dot_last(grad_gate, wg_refs[key][...]) + dot_last(grad_up, wu_refs[key][...])
        grad = (grad.astype(BF16).astype(F32) + grad_in[:, cols].astype(F32)).astype(BF16)
        for ref in grad_refs:
            ref[:, cols] = grad
    lane = lane_ref[...]
    extra = jnp.zeros((x.shape[0], LANES), F32)
    for slot, value in enumerate((inner, dot_in[...])):
        high = value.astype(BF16).astype(F32)
        extra = extra + jnp.where(lane == 2 * slot, high, 0.0)
        extra = extra + jnp.where(lane == 2 * slot + 1, value - high, 0.0)
    for ref in grad_refs:
        ref[:, width:] = extra.astype(BF16)


def expert(core, x, pieces, wd, hidden, cot, scale, routed=()):
    rows, width = x.shape
    tiles = rows // TILE
    quads = len(pieces) // 2 if routed else len(pieces)
    spec = lambda columns: turned_spec(columns, tiles)
    ins = [spec(width), whole((hidden, width)), spec(width), spec(1)]
    ins += [whole(piece.shape) for piece in pieces]
    outs = [spec(hidden), spec(width)]
    shapes = [shaped(rows, hidden, BF16), shaped(rows, width, BF16)]
    if routed:
        ins += [spec(width), spec(width), spec(1), whole((1, LANES))]
        for columns in (width, width + LANES):
            specs, halves = halves_specs(columns, tiles)
            outs, shapes = outs + specs, shapes + halves
        outs += [spec(hidden), spec(hidden)]
        shapes += [shaped(rows, hidden, BF16)] * 2
    else:
        outs += [spec(width), spec(width), spec(1), spec(2 * hidden)]
        shapes += [shaped(rows, width, BF16)] * 2
        shapes += [shaped(rows, 1, F32), shaped(rows, 2 * hidden, BF16)]
    return call(
        functools.partial(expert_kernel, bool(routed), quads),
        (tiles,),
        ins,
        outs,
        shapes,
        60,
        12 * rows * width * hidden,
        name="expert" if routed else "shared",
        scalars=1,
    )(core[None], x, wd, cot, scale, *pieces, *routed)


def reversed_bits(value, count):
    return sum((((value >> k) & 1) << (count - 1 - k) for k in range(count)), 0 * value)


def places(step, quads, up):
    if up:
        return step & 1, reversed_bits(step >> 1, quads.bit_length() - 2)
    half = quads // 2
    return jnp.where(step < half, 0, 1), jnp.where(step < half, step, step - half)


def stack_specs(quads, up, rows, columns, merged):
    quarter = quads // 4

    def spec(half, part):
        def index(step, *_):
            if up:
                return places(step, quads, up)[1] % quarter, 0
            first = half * 2 * quarter + part * quarter
            return jnp.clip(step - first, 0, quarter - 1), 0

        return pl.BlockSpec((rows, columns), index)

    def joined(step, *_):
        if up:
            return places(step, quads, up)[1], 0
        return jnp.clip(step - 2 * quarter, 0, 2 * quarter - 1), 0

    specs = [spec(0, 0), spec(0, 1)]
    shapes = [shaped(quarter * rows, columns, BF16)] * 2
    if merged:
        specs.append(pl.BlockSpec((rows, columns), joined))
        shapes.append(shaped(2 * quarter * rows, columns, BF16))
    else:
        specs += [spec(1, 0), spec(1, 1)]
        shapes += [shaped(quarter * rows, columns, BF16)] * 2
    return specs, shapes


def store_stack(step, quads, up, merged, outs, value):
    half, index = places(step, quads, up)
    part = index // (quads // 4)
    for number, out in enumerate(outs):
        wanted = (half == number // 2) & ((part == number % 2) | (merged and number == 2))

        @pl.when(wanted)
        def _():
            out[...] = value


def row_grads_kernel(quads, cuts, x_ref, grad_ref, *outs):
    step = pl.program_id(0)
    total = dot_first(x_ref[...], grad_ref[...]).astype(BF16)
    first = 0
    for low, high, up, merged in cuts:
        count = 3 if merged else 4
        store_stack(step, quads, up, merged, outs[first : first + count], total[:, low:high])
        first += count


def row_grads(rows, grads, quads, cuts):
    count, width = rows.shape
    columns = grads.shape[1]
    block = width // quads
    specs, shapes = [], []
    for low, high, up, merged in cuts:
        more = stack_specs(quads, up, block, high - low, merged)
        specs, shapes = specs + more[0], shapes + more[1]
    outs = call(
        functools.partial(row_grads_kernel, quads, cuts),
        (quads,),
        [pl.BlockSpec((count, block), lambda i: (0, i)), whole((count, columns))],
        specs,
        shapes,
        48,
        2 * count * width * columns,
        name="row_grads",
    )(rows, grads)
    found = []
    for _, _, _, merged in cuts:
        size = 3 if merged else 4
        found.append((outs[:2], outs[2:size]))
        outs = outs[size:]
    return found


def column_grads_kernel(quads, up, quad_ref, act_ref, grad_ref, *outs):
    total = dot_first(act_ref[...], grad_ref[...]).astype(BF16)
    store_stack(pl.program_id(0), quads, up, True, outs, total)


def column_grads(acts, grads, quad, quads, up):
    count, hidden = acts.shape
    width = grads.shape[1]
    block = width // quads
    specs, shapes = stack_specs(quads, up, hidden, block, True)
    outs = pl.pallas_call(
        functools.partial(column_grads_kernel, quads, up),
        grid_spec=pltpu.PrefetchScalarGridSpec(
            num_scalar_prefetch=1,
            grid=(quads,),
            in_specs=[
                pl.BlockSpec((count, hidden), lambda i, own: (0, 0)),
                pl.BlockSpec((count, block), lambda i, own: (0, own[0] ^ i)),
            ],
            out_specs=specs,
        ),
        out_shape=shapes,
        compiler_params=pltpu.CompilerParams(vmem_limit_bytes=48 * MIB),
        cost_estimate=pl.CostEstimate(
            flops=2 * count * hidden * width,
            bytes_accessed=2 * (count * (hidden + width) + hidden * width),
            transcendentals=0,
        ),
        name="column_grads",
    )(quad[None], acts, grads)
    return outs[:2], outs[2:]


def down_grads_kernel(quads, quad_ref, act_ref, grad_ref, *rest):
    outs, total_ref = rest[:-1], rest[-1]
    step = pl.program_id(0)
    total_ref[...] = dot_first(act_ref[...], grad_ref[...])
    size = total_ref.shape[0] // quads
    quarter = quads // 4
    for part, up in enumerate((True, False)):

        @pl.when(step == part)
        def _():
            for key in range(quads):
                first = pl.multiple_of((quad_ref[0] ^ key) * size, 8)
                half, index = (int(v) for v in place_of(key, quads, up))
                number = 2 if half else index // quarter
                row = (index if half else index % quarter) * size
                outs[part * 3 + number][row : row + size, :] = total_ref[
                    pl.ds(first, size), :
                ].astype(BF16)


def place_of(key, quads, up):
    count = quads.bit_length() - 1
    spot = reversed_bits(key, count) if up else key
    return spot // (quads // 2), spot % (quads // 2)


def down_grads(acts, grads, quad, quads):
    count, hidden = acts.shape
    cut = grads.shape[1] // 2
    rows = hidden // 4
    shapes = [shaped(rows, cut, BF16), shaped(rows, cut, BF16), shaped(2 * rows, cut, BF16)] * 2
    outs = pl.pallas_call(
        functools.partial(down_grads_kernel, quads),
        grid_spec=pltpu.PrefetchScalarGridSpec(
            num_scalar_prefetch=1,
            grid=(2,),
            in_specs=[
                pl.BlockSpec((count, hidden), lambda i, own: (0, 0)),
                pl.BlockSpec((count, cut), lambda i, own: (0, i)),
            ],
            out_specs=[pl.BlockSpec(shape.shape, lambda i, own: (0, 0)) for shape in shapes],
            scratch_shapes=[pltpu.VMEM((hidden, cut), F32)],
        ),
        out_shape=shapes,
        compiler_params=pltpu.CompilerParams(vmem_limit_bytes=48 * MIB),
        cost_estimate=pl.CostEstimate(
            flops=4 * count * hidden * cut,
            bytes_accessed=2 * (count * (hidden + 2 * cut) + 2 * hidden * cut),
            transcendentals=0,
        ),
        name="down_grads",
    )(quad[None], acts, grads)
    return (outs[:2], outs[2:3]), (outs[3:5], outs[5:])


def local(
    residual_in,
    attention_gain,
    query_weight,
    query_bias,
    key_weight,
    key_bias,
    value_weight,
    value_bias,
    output_weight,
    feedforward_gain,
    router_weight,
    shared_logit_weight,
    shared_gate_weight,
    shared_up_weight,
    shared_down_weight,
    expert_gate,
    expert_up,
    expert_down,
    cotangent,
    expert_index,
    token_live,
    document_lengths,
):
    ep_count = lax.axis_size("ep")
    grp_count = lax.axis_size("grp")
    quads = grp_count // 2
    rows_dev, width = residual_in.shape
    group_rows = rows_dev * ep_count
    pair_rows = 2 * group_rows
    seq_len = group_rows * grp_count // SEQS
    expert_count = expert_gate.shape[0] * ep_count
    ffe = expert_gate.shape[2]
    ffs_half = shared_gate_weight.shape[1] // 2
    grp = lax.axis_index("grp")
    ep = lax.axis_index("ep")
    core = grp % 2
    quad = grp // 2
    back = -(-WINDOW // pair_rows)
    heads = query_weight.shape[1] // HDIM // 2
    head_width = heads * HDIM
    up_order = quad_bits()
    down_order = up_order[::-1]

    block = width // quads
    cut = len(up_order) // 2
    up_one, up_two = up_order[:cut], up_order[cut:]
    down_one, down_two = down_order[: len(down_order) - cut], down_order[len(down_order) - cut :]
    ep_masks = [1 << b for b in range(ep_count.bit_length() - 1)]
    quad_masks = [2 * bit for bit in up_order]
    seq_groups = grp_count // SEQS
    experts = jnp.arange(expert_count, dtype=jnp.int32)
    ed_cut = width // 2

    def shifted(values, steps):
        route = [
            (i, i + 2 * steps)
            for i in range(grp_count)
            if 0 <= i + 2 * steps < grp_count and i // seq_groups == (i + 2 * steps) // seq_groups
        ]
        return lax.ppermute(values, "grp", route)

    def gathered(values):
        return lax.all_gather(values, "ep", axis=0, tiled=True)

    def scattered(values):
        return lax.psum_scatter(values, "ep", scatter_dimension=0, tiled=True)

    def core_sum(kept, other):
        return add_rows(kept, across(other, 1))

    def finished(kept, arrived, axis):
        mine, other = finish(core[None], kept, arrived, axis)
        return mine, across(other, 1)

    def merged(halves):
        return merge(core, halves[0], across(halves[1], 1), None)

    hidden_in = residual_in.astype(F32)
    grad_out = cotangent.astype(F32)
    gain_one = attention_gain.astype(F32)
    gain_two = feedforward_gain.astype(F32)
    router_all = jnp.concatenate([router_weight, shared_logit_weight[:, None]], axis=1)
    router_flipped = flip_columns(router_all.T, quad).T
    scale_one = norm_scale(hidden_in)
    unit_one = hidden_in * scale_one
    normed_one = (unit_one * gain_one).astype(BF16)
    group_one = gathered(flip_columns(normed_one, quad))

    qk_keep, qk_other = zip(
        *[split_core(weight, core, 1) for weight in (query_weight, key_weight, value_weight)]
    )
    qkv_keep, qkv_other = jnp.concatenate(qk_keep, 1), jnp.concatenate(qk_other, 1)
    qkv_block = merge_core(qkv_keep, across(qkv_other, 1), core, 0)
    qkv_cut = qkv_block.shape[1] // 2
    qkv_a = {0: qkv_block[:, :qkv_cut]}
    qkv_b = {0: qkv_block[:, qkv_cut:]}
    (
        qkv_a, qkv_b, output_weight, shared_gate_weight, shared_up_weight, shared_down_weight,
        expert_gate, expert_up, expert_down,
    ) = together(
        qkv_a, qkv_b, output_weight, shared_gate_weight, shared_up_weight, shared_down_weight,
        expert_gate, expert_up, expert_down,
    )
    qkv_a_one, qkv_a_two = gather_quads(qkv_a, up_one), gather_quads(qkv_a, up_two)
    qkv_b_one, qkv_b_two = gather_quads(qkv_b, down_one), gather_quads(qkv_b, down_two)

    o_keep, o_other = split_core(output_weight, core, 0)
    sg_keep, sg_other = split_core(shared_gate_weight, core, 1)
    su_keep, su_other = split_core(shared_up_weight, core, 1)
    gu_keep = jnp.concatenate([sg_keep, su_keep], axis=1)
    gu_other = jnp.concatenate([sg_other, su_other], axis=1)
    gu_block = merge_core(gu_keep, across(gu_other, 1), core, 0)
    sd_keep, sd_other = split_core(shared_down_weight, core, 0)
    sd_keep = jnp.concatenate([sd_keep, o_keep], axis=0)
    sd_other = jnp.concatenate([sd_other, o_other], axis=0)
    sd_block = merge_core(sd_keep, across(sd_other, 1), core, 1)

    def expert_block(weight):
        keep, other = split_core(weight, core, 0)
        return merge_core(keep[0], across(other[0], 1), core, 0)

    eg_block, eu_block, ed_block = [
        expert_block(weight) for weight in (expert_gate, expert_up, expert_down)
    ]
    eda_block, edb_block = ed_block[:, :ed_cut], ed_block[:, ed_cut:]

    (
        qkv_a_one, qkv_a_two, qkv_b_one, qkv_b_two, gu_block, sd_block, eg_block, eu_block,
        eda_block, edb_block,
    ) = together(
        qkv_a_one, qkv_a_two, qkv_b_one, qkv_b_two, gu_block, sd_block, eg_block, eu_block,
        eda_block, edb_block,
    )
    qkv_a_rest = gather_rest(qkv_a_one, up_two)
    qkv_b_rest = gather_rest(qkv_b_one, down_two)
    sd_one, sd_two = gather_quads({0: sd_block}, down_one), gather_quads({0: sd_block}, down_two)
    chosen = (
        (expert_index[:, :, None] == experts[None, None, :]) & (token_live[:, None, None] > 0)
    ).any(axis=1)
    cot_packed = jnp.concatenate(
        [cotangent, jnp.pad(chosen.astype(BF16), ((0, 0), (0, LANES - expert_count)))], axis=1
    )
    chosen = chosen.astype(F32)
    bias = jnp.concatenate(
        [split_core(b, core, 0)[0] for b in (query_bias, key_bias, value_bias)]
    ).astype(F32)[None, :]
    key_place = (quad - back) * pair_rows + jnp.arange((back + 1) * pair_rows, dtype=jnp.int32)
    query_place = key_place[back * pair_rows :]
    _, position = doc_layout(document_lengths, seq_len, query_place)
    low = jnp.maximum(query_place - position, query_place - WINDOW + 1)[:, None]
    high, key_place = query_place[:, None], key_place[None, :]
    cosine, sine = rope_tables(position)
    (
        group_one, qkv_a, qkv_b, sd_one, sd_two, gu_block, eg_block, eu_block, eda_block,
         edb_block, cot_packed, bias, cosine, sine, low, high,
    ) = together(
        group_one, qkv_a_one | qkv_a_two | qkv_a_rest, qkv_b_one | qkv_b_two | qkv_b_rest,
        sd_one, sd_two, gu_block, eg_block, eu_block, eda_block, edb_block, cot_packed, bias,
        cosine, sine, low, high,
    )

    rows_one = join_rows(core, group_one, across(group_one, 1))
    gu_two = gather_quads({0: gu_block}, up_two)
    sd_rest = gather_rest(sd_one, down_two)
    cot_group = gathered(cot_packed)
    qkv_a, qkv_b = listed(qkv_a), listed(qkv_b)
    query, key_value = project(rows_one, qkv_a, qkv_b, bias, cosine, sine, heads)

    before = [shifted(key_value, step) for step in range(back, 0, -1)]
    down_full = place_quads(sd_one | sd_two | sd_rest, quad, 1)
    output_rows = down_full[ffs_half:]
    query, before, gu_two, edb_block, down_full, output_rows = together(
        query, before, gu_two, edb_block, down_full, output_rows
    )
    edb_one, edb_two = gather_quads({0: edb_block}, down_one), gather_quads({0: edb_block}, down_two)
    attended, log_total = attend(query, before, key_value, key_place, low, high)
    kept, other = split_core(attended, core, 0)
    other = dot(other, output_rows).astype(BF16)
    kept, other, cot_group, edb_one, edb_two = together(kept, other, cot_group, edb_one, edb_two)
    branch = add_rows(dot(kept, output_rows).astype(BF16), across(other, 1))
    branch, gu_block, eu_block, eda_block, cot_group = together(
        branch, gu_block, eu_block, eda_block, cot_group
    )
    branch_sum = scattered(branch)
    cot_other = across(cot_group, 1)
    gu_one = gather_quads({0: gu_block}, up_one)
    eda_one, eda_two = gather_quads({0: eda_block}, up_one), gather_quads({0: eda_block}, up_two)
    eu_one = gather_quads({0: eu_block}, down_one)
    ed_full = jnp.zeros((eda_block.shape[0] * quads, width), BF16)
    ed_full = place_quads(edb_one | edb_two, quad, 0, ed_full, ed_cut)
    branch_sum, cot_other, gu_one, eda_one, eda_two, eu_one, eg_block, edb_one, ed_full = (
        together(
            branch_sum, cot_other, gu_one, eda_one, eda_two, eu_one, eg_block, edb_one, ed_full,
        )
    )

    eg_one = gather_quads({0: eg_block}, up_one)
    edb_rest = gather_rest(edb_one, down_two)
    gu_rest, eda_rest = gather_rest(gu_one, up_two), gather_rest(eda_one, up_two)
    mixed = hidden_in + branch_sum.astype(F32)
    scale_two = norm_scale(mixed)
    unit_two = mixed * scale_two
    normed_two = (unit_two * gain_two).astype(BF16)
    group_two = gathered(flip_columns(normed_two, quad))
    cot_rows = join_rows(core, cot_group, cot_other)
    ed_full = place_quads(eda_one | eda_two, quad, 0, ed_full)
    (
        group_two, eg_one, edb_rest, gu_rest, eda_rest, eu_block, eg_block, eu_one, cot_rows,
        ed_full,
    ) = together(
        group_two, eg_one, edb_rest, gu_rest, eda_rest, eu_block, eg_block, eu_one, cot_rows,
        ed_full,
    )
    eu_two, eg_two = gather_quads({0: eu_block}, down_two), gather_quads({0: eg_block}, up_two)
    eu_rest, eg_rest = gather_rest(eu_one, down_two), gather_rest(eg_one, up_two)
    rows_two = join_rows(core, group_two, across(group_two, 1))
    gu_pieces = listed(gu_one | gu_two | gu_rest)

    def router(rows, weight):
        logits = dot(rows, weight)
        return jax.nn.softmax(logits[:, :expert_count], axis=-1), jax.nn.sigmoid(
            logits[:, expert_count:]
        )

    chosen_rows = cot_rows[:, width : width + expert_count].astype(F32)
    probs_rows, shared_scale_rows = router(rows_two, router_flipped)
    router_probs, shared_scale = router(normed_two, router_all)
    mine = (experts == ep * 2 + core).astype(F32)[None, :]
    gate = jnp.sum(probs_rows * chosen_rows * mine, axis=1, keepdims=True)

    shared_active, grad_shared_out, part, grad_part, shared_dot, grad_gu = expert(
        core, rows_two, gu_pieces, down_full, ffs_half, cot_rows, shared_scale_rows
    )
    gu_cut = 2 * ffs_half * 3 // 4 // LANES * LANES
    (gua_grad, gua_out), (gub_grad, gub_out) = row_grads(
        rows_two, grad_gu, quads, [(0, gu_cut, True, True), (gu_cut, 2 * ffs_half, False, True)]
    )
    sd_grad, sd_out = column_grads(shared_active, grad_shared_out, quad, quads, False)
    gua_grad, eda_rest, edb_rest, ed_full = together(gua_grad, eda_rest, edb_rest, ed_full)
    ed_full = place_quads(eda_rest, quad, 0, ed_full)
    ed_full = place_quads(edb_rest, quad, 0, ed_full, ed_cut)
    (
        grad_part, part, eu_two, eg_two, eu_rest, eg_rest, ed_full, gua_grad, gua_out, gub_grad,
        gub_out, sd_grad, sd_out, gate,
    ) = together(
        grad_part, part, eu_two, eg_two, eu_rest, eg_rest, ed_full, gua_grad, gua_out, gub_grad,
        gub_out, sd_grad, sd_out, gate,
    )
    eg_pieces, eu_pieces = eg_one | eg_two | eg_rest, eu_one | eu_two | eu_rest

    def sent(blocks, bit):
        return [across(part, 2 * bit) for part in blocks]

    gua_sent, gub_sent = sent(gua_out, up_order[0]), sent(gub_out, down_order[0])
    sd_sent = sent(sd_out, down_order[0])

    lanes = jnp.arange(LANES, dtype=jnp.int32)
    lanes = jnp.where(lanes % expert_count == ep * 2 + core, lanes // expert_count, -1)[None, :]
    active, grad_result, *sums, grad_gate_pre, grad_up_pre = expert(
        core,
        rows_two,
        listed(eg_pieces) + listed(eu_pieces),
        ed_full,
        ffe,
        cot_rows,
        gate,
        (part, grad_part, shared_dot, lanes),
    )
    sums, gua_sent, gub_sent, sd_sent, gua_grad, gub_grad, sd_grad = together(
        sums, gua_sent, gub_sent, sd_sent, gua_grad, gub_grad, sd_grad
    )
    forward_part, packed = sums[:2], core_sum(*sums[2:])
    gua_grad = first_sum(gua_grad, gua_sent)
    gub_grad = first_sum(gub_grad, gub_sent)
    sd_grad = first_sum(sd_grad, sd_sent)
    (
        packed, gua_grad, gub_grad, sd_grad, active, grad_result, grad_gate_pre, grad_up_pre,
    ) = together(
        packed, gua_grad, gub_grad, sd_grad, active, grad_result, grad_gate_pre, grad_up_pre,
    )
    spread = scattered(packed)
    gua_sent, gub_sent = across(gua_grad[1], 2 * up_order[1]), across(gub_grad[1], 2 * down_order[1])
    sd_sent = across(sd_grad[1], 2 * down_order[1])
    (eda_grad, eda_out), (edb_grad, edb_out) = down_grads(active, grad_result, quad, quads)
    eda_out, edb_out, grad_gate_pre = together(eda_out, edb_out, grad_gate_pre)
    eda_sent, edb_sent = sent(eda_out, up_order[0]), sent(edb_out, down_order[0])
    ((eg_grad, eg_out),) = row_grads(rows_two, grad_gate_pre, quads, [(0, ffe, True, False)])
    eg_grad, eg_out, grad_up_pre, gua_sent, gub_sent, sd_sent = together(
        eg_grad, eg_out, grad_up_pre, gua_sent, gub_sent, sd_sent
    )
    ((eu_grad, eu_out),) = row_grads(rows_two, grad_up_pre, quads, [(0, ffe, False, False)])
    spread, eg_grad, eg_out = together(spread, eg_grad, eg_out)

    grad_normed_two = flip_columns(spread[:, :width], quad).astype(F32)
    side = spread[:, width : width + 4 * expert_count].astype(F32).reshape(rows_dev, 4, expert_count)
    grad_gate_own = side[:, 0] + side[:, 1]
    shared_dot_own = jnp.sum(side[:, 2] + side[:, 3], axis=1, keepdims=True)
    grad_logit = shared_dot_own * shared_scale * (1.0 - shared_scale)
    grad_probs = grad_gate_own * chosen
    grad_logits = router_probs * (
        grad_probs - jnp.sum(router_probs * grad_probs, axis=-1, keepdims=True)
    )
    grad_router = jnp.concatenate([grad_logits, grad_logit], axis=1)
    router_grad = dot_first(normed_two.astype(F32), grad_router)
    grad_normed_two = grad_normed_two + dot_last(grad_router, router_all.astype(F32))
    grad_norm_part, ff_gain_grad = norm_backward(grad_normed_two, unit_two, scale_two, gain_two)
    grad_mixed = grad_out + grad_norm_part
    (
        branch_low, eda_grad, eda_sent, edb_grad, edb_sent, gua_grad, gua_sent, gub_grad, gub_sent,
        sd_grad, sd_sent, eg_out, eu_grad, eu_out, forward_part,
    ) = together(
        grad_mixed.astype(BF16), eda_grad, eda_sent, edb_grad, edb_sent, gua_grad, gua_sent, gub_grad,
        gub_sent, sd_grad, sd_sent, eg_out, eu_grad, eu_out, forward_part,
    )
    group_branch = gathered(branch_low)
    eg_sent = sent(eg_out[:1], up_order[0])
    eu_sent = sent(eu_out[:1], down_order[0])
    forward_part = core_sum(*forward_part)
    forward_part, gua_grad, gua_sent, gub_grad, gub_sent, sd_grad, sd_sent = together(
        forward_part, gua_grad, gua_sent, gub_grad, gub_sent, sd_grad, sd_sent
    )
    eda_grad = first_sum(eda_grad, eda_sent)
    edb_grad = first_sum(edb_grad, edb_sent)
    eda_sent, edb_sent = across(eda_grad[1], 2 * up_order[1]), across(edb_grad[1], 2 * down_order[1])

    gua_mine, gua_arrived = finished(*rest_parts(gua_grad[0], gua_sent, up_order), 0)
    gub_mine, gub_arrived = finished(*rest_parts(gub_grad[0], gub_sent, down_order), 0)
    sd_mine, sd_arrived = finished(*rest_parts(sd_grad[0], sd_sent, down_order), 1)
    gu_mine = jnp.concatenate([gua_mine, gub_mine], axis=1)
    gu_arrived = jnp.concatenate([gua_arrived, gub_arrived], axis=1)
    sg_grad, su_grad = [
        merge_core(
            gu_mine[:, part * ffs_half : (part + 1) * ffs_half],
            gu_arrived[:, part * ffs_half : (part + 1) * ffs_half],
            core,
            1,
        ).astype(F32)
        for part in range(2)
    ]
    sd_grad = merge(core, sd_mine, sd_arrived, 0)
    (
        group_branch, forward_part, sg_grad, su_grad, sd_grad, eg_grad, eg_out, eg_sent, eu_grad, eu_out, eu_sent, eda_grad,
        eda_sent, edb_grad, edb_sent,
    ) = together(
        group_branch, forward_part, sg_grad, su_grad, sd_grad, eg_grad, eg_out, eg_sent, eu_grad, eu_out, eu_sent, eda_grad,
        eda_sent, edb_grad, edb_sent,
    )
    other_branch = across(group_branch, 1)
    eg_sent = eg_sent + sent(eg_out[1:], up_order[0])
    eu_sent = eu_sent + sent(eu_out[1:], down_order[0])

    layer_sum = scattered(forward_part)
    grad_query, grad_own, *grad_before = attend_back(
        core, query, group_branch, other_branch, output_rows, log_total, before, key_value, key_place,
        low, high, cosine, sine,
    )
    grad_query, grad_before, group_branch, other_branch, eg_grad, eu_grad = together(
        grad_query, grad_before, group_branch, other_branch, eg_grad, eu_grad
    )
    arrived = [shifted(sent, step - back) for step, sent in enumerate(grad_before)]
    cut = eg_grad[1].shape[0] // 2
    eg_grad = [
        add_low(eg_grad[0], eg_sent[0]),
        add_low(eg_grad[1][:cut], eg_sent[1][:cut]),
        add_low(eg_grad[1][cut:], eg_sent[1][cut:]),
    ]
    eu_grad = [
        add_low(eu_grad[0], eu_sent[0]),
        add_low(eu_grad[1][:cut], eu_sent[1][:cut]),
        add_low(eu_grad[1][cut:], eu_sent[1][cut:]),
    ]
    eg_rest = across(eg_grad[1], 2 * up_order[1])
    arrived, eg_grad, eu_grad, group_branch, other_branch = together(
        arrived, eg_grad, eu_grad, group_branch, other_branch
    )
    eu_rest = across(eu_grad[1], 2 * down_order[1])
    (*partial, att_gain_part, bias_part), (qkv_a_grad, qkv_a_out), (qkv_b_grad, qkv_b_out) = collect(
        core, grad_query, grad_own, cosine, sine, rows_one, arrived, qkv_a, qkv_b
    )
    partial, qkv_a_out, qkv_b_out, eg_grad, eg_rest, eu_grad, eu_rest = together(
        partial, qkv_a_out, qkv_b_out, eg_grad, eg_rest, eu_grad, eu_rest
    )
    eg_last, eu_last = across(eg_grad[2], 2 * up_order[1]), across(eu_grad[2], 2 * down_order[1])
    qkv_a_sent, qkv_b_sent = sent(qkv_a_out, up_order[0]), sent(qkv_b_out, down_order[0])
    partial_sum = core_sum(*partial)

    (
        partial_sum, att_gain_part, bias_part, group_branch, other_branch, qkv_a_grad, qkv_b_grad, eda_grad,
        eda_sent, edb_grad, edb_sent,
    ) = together(
        partial_sum, att_gain_part, bias_part, group_branch, other_branch, qkv_a_grad, qkv_b_grad, eda_grad,
        eda_sent, edb_grad, edb_sent,
    )
    grad_normed_one = scattered(partial_sum)
    grad_branch = join_rows(core, group_branch, other_branch)
    o_grad, o_out = column_grads(attended, grad_branch, quad, quads, False)
    att_gain_part = flip_columns(att_gain_part[0], quad) / gain_one
    late = jnp.concatenate([att_gain_part, ff_gain_grad, router_grad.T.reshape(-1)])
    late = sum_everywhere(late, [], ep_masks)
    o_sent = sent(o_out, down_order[0])
    (
        late, qkv_a_sent, qkv_b_sent, eg_last, eu_last, eda_sent, edb_sent,
    ) = together(
        late, qkv_a_sent, qkv_b_sent, eg_last, eu_last, eda_sent, edb_sent,
    )
    bias_part = bias_part.reshape(3, head_width)
    bias_part = jnp.concatenate(
        [jnp.where(core == 0, bias_part, 0.0), jnp.where(core == 0, 0.0, bias_part)], axis=1
    )
    late = sum_everywhere(jnp.concatenate([late, bias_part.reshape(-1)]), [1], [])
    qkv_a_grad = first_sum(qkv_a_grad, qkv_a_sent)
    qkv_b_grad = first_sum(qkv_b_grad, qkv_b_sent)
    o_grad = first_sum(o_grad, o_sent)
    qkv_a_grad, qkv_b_grad, o_grad, eg_last, eu_last, eda_sent, edb_sent = together(
        qkv_a_grad, qkv_b_grad, o_grad, eg_last, eu_last, eda_sent, edb_sent
    )
    eg_rest = jnp.concatenate([eg_rest, eg_last], axis=0)
    eu_rest = jnp.concatenate([eu_rest, eu_last], axis=0)
    qkv_a_rest = across(qkv_a_grad[1], 2 * up_order[1])
    qkv_b_rest = across(qkv_b_grad[1], 2 * down_order[1])
    o_rest = across(o_grad[1], 2 * down_order[1])
    late = sum_everywhere(late, quad_masks, [])
    last = [
        finish(core[None], *rest_parts(kept, arrived, order), 0)
        for kept, arrived, order in (
            (eg_grad[0], eg_rest, up_order),
            (eu_grad[0], eu_rest, down_order),
            (eda_grad[0], eda_sent, up_order),
            (edb_grad[0], edb_sent, down_order),
        )
    ]
    last, qkv_a_rest, qkv_b_rest, o_rest = together(last, qkv_a_rest, qkv_b_rest, o_rest)
    eg_grad, eu_grad, eda_grad, edb_grad = [merged(halves) for halves in last]
    ed_grad = jnp.concatenate([eda_grad, edb_grad], axis=2)
    layer_out = (mixed + layer_sum.astype(F32)).astype(BF16)
    qkv_a_mine, qkv_a_arrived = finished(*rest_parts(qkv_a_grad[0], qkv_a_rest, up_order), 0)
    qkv_b_mine, qkv_b_arrived = finished(*rest_parts(qkv_b_grad[0], qkv_b_rest, down_order), 0)
    o_mine, o_arrived = finished(*rest_parts(o_grad[0], o_rest, down_order), 1)
    (
        grad_normed_one, qkv_a_mine, qkv_a_arrived, qkv_b_mine, qkv_b_arrived, o_mine, o_arrived,
        late, eu_grad, eg_grad, ed_grad, layer_out,
    ) = together(
        grad_normed_one, qkv_a_mine, qkv_a_arrived, qkv_b_mine, qkv_b_arrived, o_mine, o_arrived,
        late, eu_grad, eg_grad, ed_grad, layer_out,
    )
    qkv_mine = jnp.concatenate([qkv_a_mine, qkv_b_mine], axis=1)
    qkv_arrived = jnp.concatenate([qkv_a_arrived, qkv_b_arrived], axis=1)
    q_grad, k_grad, v_grad = [merge(core, qkv_mine, qkv_arrived, 1, part, 3) for part in range(3)]
    o_grad = merge(core, o_mine, o_arrived, 0)
    att_gain_grad, ff_gain_grad = late[:width], late[width : 2 * width]
    router_grad = late[2 * width : (expert_count + 3) * width].reshape(expert_count + 1, width)
    bias_mine = late[(expert_count + 3) * width :].reshape(3, 2 * head_width)
    grad_norm_one, _ = norm_backward(
        flip_columns(grad_normed_one, quad).astype(F32), unit_one, scale_one, gain_one
    )
    input_grad = grad_mixed + grad_norm_one
    return (
        layer_out,
        input_grad,
        att_gain_grad,
        q_grad,
        bias_mine[0],
        k_grad,
        bias_mine[1],
        v_grad,
        bias_mine[2],
        o_grad,
        ff_gain_grad,
        router_grad[:expert_count].T,
        router_grad[expert_count],
        sg_grad,
        su_grad,
        sd_grad,
        eg_grad,
        eu_grad,
        ed_grad,
    )


def solution(mesh):
    tokens = P(("grp", "ep"), None)
    rows, columns, experts = P("grp", "ep"), P("ep", "grp"), P("ep", "grp", None)
    in_specs = (
        tokens, P(), rows, P("ep"), rows, P("ep"), rows, P("ep"), columns, P(), P(), P(),
        rows, rows, columns, experts, experts, experts, tokens, tokens, P(("grp", "ep")), P(),
    )
    out_specs = (
        tokens, tokens, P(), rows, P("ep"), rows, P("ep"), rows, P("ep"), columns, P(), P(), P(),
        rows, rows, columns, experts, experts, experts,
    )
    return jax.shard_map(local, mesh=mesh, in_specs=in_specs, out_specs=out_specs, check_vma=False)
```

```python
import functools

import jax
import jax.numpy as jnp
from jax import lax
from jax.experimental import pallas as pl
from jax.experimental.pallas import tpu as pltpu
from jax.sharding import PartitionSpec as P

HDIM = 128
SEQS = 2
DOCS = 4
WINDOW = 1024
EPS = 1e-06
ROPE_BASE = 1000000.0
MASKED = -1e30
F32 = jnp.float32
BF16 = jnp.bfloat16
TILE = 256
LANES = 128
MIB = 1 << 20


def dot(left, right):
    return jnp.dot(left, right, preferred_element_type=F32)


def dot_last(left, right):
    return lax.dot_general(left, right, (((1,), (1,)), ((), ())), preferred_element_type=F32)


def dot_first(left, right):
    return lax.dot_general(left, right, (((0,), (0,)), ((), ())), preferred_element_type=F32)


def across(block, mask):
    count = lax.axis_size("grp")
    return lax.ppermute(block, "grp", [(i, i ^ mask) for i in range(count)])


def quad_bits():
    return [1 << b for b in range((lax.axis_size("grp") // 2).bit_length() - 1)]


def flip_columns(values, quad):
    quads = lax.axis_size("grp") // 2
    axis = values.ndim - 1
    block = values.shape[axis] // quads
    return jnp.concatenate(
        [
            lax.dynamic_slice_in_dim(values, (quad ^ key) * block, block, axis)
            for key in range(quads)
        ],
        axis=axis,
    )


def gather_quads(pieces, order):
    pieces = dict(pieces)
    for bit in order:
        for key, piece in list(pieces.items()):
            pieces[key | bit] = across(piece, 2 * bit)
    return pieces


def add_low(left, right):
    return (left.astype(F32) + right.astype(F32)).astype(BF16)


def first_sum(parts, arrived):
    half = parts[0].shape[0]
    if len(arrived) == 1:
        arrived = (arrived[0][:half], arrived[0][half:])
    return add_low(parts[0], arrived[0]), add_low(parts[1], arrived[1])


def rest_parts(kept, arrived, order):
    for bit in order[2:]:
        stack = add_rows(kept, arrived)
        half = stack.shape[0] // 2
        kept, arrived = stack[:half], across(stack[half:], 2 * bit)
    return kept, arrived


def together(*values):
    return lax.optimization_barrier(values)


def sum_everywhere(values, masks_grp, masks_ep):
    for mask in masks_grp:
        values = values + across(values, mask)
    count = lax.axis_size("ep")
    for mask in masks_ep:
        values = values + lax.ppermute(values, "ep", [(i, i ^ mask) for i in range(count)])
    return values


def gather_rest(pieces, order):
    found = {}
    for key, piece in pieces.items():
        if key:
            found.update({key | k: v for k, v in gather_quads({0: piece}, order).items()})
    return found


def listed(pieces):
    return [pieces[key] for key in sorted(pieces)]


def place_quads(pieces, quad, axis, whole=None, other=0):
    size = pieces[0].shape[axis] if whole is None else whole.shape[axis] // (lax.axis_size("grp") // 2)
    if whole is None:
        shape = list(pieces[0].shape)
        shape[axis] = size * len(pieces)
        whole = jnp.zeros(shape, pieces[0].dtype)
    for key in sorted(pieces):
        start = [other, other]
        start[axis] = (quad ^ key) * size
        whole = lax.dynamic_update_slice(whole, pieces[key], start)
    return whole


def take_quads(whole, quad, quads, axis):
    size = whole.shape[axis] // quads
    return {
        key: lax.dynamic_slice_in_dim(whole, (quad ^ key) * size, size, axis)
        for key in range(quads)
    }


def merge_core(kept, arrived, core, axis):
    first = jnp.where(core == 0, kept, arrived)
    second = jnp.where(core == 0, arrived, kept)
    return jnp.concatenate([first, second], axis=axis)


def split_core(values, core, axis):
    half = values.shape[axis] // 2
    first = lax.slice_in_dim(values, 0, half, axis=axis)
    second = lax.slice_in_dim(values, half, 2 * half, axis=axis)
    return jnp.where(core == 0, first, second), jnp.where(core == 0, second, first)


def norm_scale(values):
    return lax.rsqrt(jnp.mean(values * values, axis=-1, keepdims=True) + EPS)


def norm_backward(grad_normed, unit, scale, gain):
    grad_unit = grad_normed * gain
    inner = jnp.mean(grad_unit * unit, axis=-1, keepdims=True)
    return scale * (grad_unit - unit * inner), jnp.sum(grad_normed * unit, axis=0)


def doc_layout(document_lengths, seq_len, index):
    valid = index >= 0
    safe = jnp.maximum(index, 0)
    seq_of = safe // seq_len
    place = safe % seq_len
    seq_count = document_lengths.shape[0]
    picker = (seq_of[:, None] == jnp.arange(seq_count, dtype=jnp.int32)[None, :]).astype(jnp.int32)
    lengths = jnp.sum(picker[:, :, None] * document_lengths[None, :, :], axis=1)
    ends = jnp.cumsum(lengths, axis=1)
    doc = jnp.sum((ends <= place[:, None]).astype(jnp.int32), axis=1)
    earlier = jnp.arange(DOCS, dtype=jnp.int32)[None, :] < doc[:, None]
    before = jnp.sum(jnp.where(earlier, lengths, 0), axis=1)
    return jnp.where(valid, seq_of * DOCS + doc, -1), place - before


def rope_tables(position):
    half = HDIM // 2
    freq = ROPE_BASE ** (-(jnp.arange(half, dtype=F32) * 2.0 / HDIM))
    angle = position.astype(F32)[:, None] * freq[None, :]
    cosine, sine = jnp.cos(angle), jnp.sin(angle)
    return jnp.concatenate([cosine, cosine], axis=1), jnp.concatenate([-sine, sine], axis=1)


def turn(values, cosine, sine):
    return values * cosine + pltpu.roll(values, HDIM // 2, 1) * sine


def call(kernel, grid, ins, outs, shapes, limit, flops, scratch=(), name=None, scalars=0):
    moved = 0
    for shape in shapes:
        moved += shape.size * shape.dtype.itemsize

    def run(*args):
        total = moved + sum(a.size * a.dtype.itemsize for a in args)
        if flops == 0:
            total = 0
        return pl.pallas_call(
            kernel,
            grid_spec=pltpu.PrefetchScalarGridSpec(
                num_scalar_prefetch=scalars,
                grid=grid,
                in_specs=ins,
                out_specs=outs,
                scratch_shapes=scratch,
            ),
            out_shape=shapes,
            compiler_params=pltpu.CompilerParams(vmem_limit_bytes=limit * MIB),
            cost_estimate=pl.CostEstimate(
                flops=flops, bytes_accessed=total, transcendentals=0
            ),
            name=name,
        )(*args)

    return run


def whole(shape):
    return pl.BlockSpec(shape, lambda *_: (0,) * len(shape), pipeline_mode=pl.Buffered(1))


def rows_spec(columns, tile=TILE):
    return pl.BlockSpec((tile, columns), lambda i, *_: (i, 0))


def turned(step, core, count):
    return (step + (count // 2) * core) % count


def turned_spec(columns, count):
    return pl.BlockSpec((TILE, columns), lambda i, core: (turned(i, core[0], count), 0))


def halves_specs(columns, count):
    half = count // 2
    specs = [
        pl.BlockSpec((TILE, columns), lambda i, core: (jnp.minimum(i, half), 0)),
        pl.BlockSpec((TILE, columns), lambda i, core: (jnp.maximum(i - half, 0), 0)),
    ]
    return specs, [shaped((half + 1) * TILE, columns, BF16), shaped(half * TILE, columns, BF16)]


def add_kernel(left_ref, right_ref, out_ref):
    out_ref[...] = (left_ref[...].astype(F32) + right_ref[...].astype(F32)).astype(BF16)


def add_rows(left, right):
    rows, columns = right.shape
    tile = rows // 4 if rows % 64 == 0 else rows
    return call(
        add_kernel,
        (rows // tile,),
        [rows_spec(columns, tile)] * 2,
        [rows_spec(columns, tile)],
        [shaped(rows, columns, BF16)],
        16,
        0,
        name="add_rows",
    )(left, right)[0]


def join_kernel(core_ref, own_ref, other_ref, out_ref):
    own = pl.program_id(0) // (pl.num_programs(0) // 2) == core_ref[0]

    @pl.when(own)
    def _():
        out_ref[...] = own_ref[...]

    @pl.when(~own)
    def _():
        out_ref[...] = other_ref[...]


def join_rows(core, own, other):
    rows, columns = own.shape
    tile = rows // 4

    def spec(mine):
        def index(i, core):
            place = i - 4 * jnp.where(mine, core[0], 1 - core[0])
            return jnp.clip(place, 0, 3), 0

        return pl.BlockSpec((tile, columns), index)

    return call(
        join_kernel,
        (8,),
        [spec(True), spec(False)],
        [pl.BlockSpec((tile, columns), lambda i, core: (i, 0))],
        [shaped(2 * rows, columns, BF16)],
        24,
        0,
        name="join_rows",
        scalars=1,
    )(core[None], own, other)[0]


def finish_kernel(core_ref, kept_ref, arrived_ref, mine_ref, other_ref):
    total = (kept_ref[...].astype(F32) + arrived_ref[...].astype(F32)).astype(BF16)

    @pl.when(pl.program_id(0) == 0)
    def _():
        other_ref[...] = total

    @pl.when(pl.program_id(0) == 1)
    def _():
        mine_ref[...] = total


def finish(core, kept, arrived, axis):
    rows, columns = kept.shape
    size = (rows // 2, columns) if axis == 0 else (rows, columns // 2)
    if size[0] % 16 or (axis == 1 and size[1] % LANES):
        return split_core(add_low(kept, arrived), core[0], axis)

    def index(i, core):
        half = jnp.where(i == 0, 1 - core[0], core[0])
        return (half, 0) if axis == 0 else (0, half)

    return call(
        finish_kernel,
        (2,),
        [pl.BlockSpec(size, index)] * 2,
        [pl.BlockSpec(size, lambda i, core: (0, 0))] * 2,
        [shaped(*size, BF16)] * 2,
        24,
        0,
        name="finish",
        scalars=1,
    )(core, kept, arrived)


def merge_kernel(core_ref, mine_ref, arrived_ref, out_ref):
    own = pl.program_id(0) == core_ref[0]

    @pl.when(own)
    def _():
        out_ref[...] = mine_ref[...].astype(F32).reshape(out_ref.shape)

    @pl.when(~own)
    def _():
        out_ref[...] = arrived_ref[...].astype(F32).reshape(out_ref.shape)


def merge(core, mine, arrived, axis, part=0, parts=1):
    rows, columns = mine.shape
    columns = columns // parts
    if axis is None:
        shape, size, index = (2, rows, columns), (1, rows, columns), lambda i, core: (i, 0, 0)
    elif axis == 0:
        shape, size, index = (2 * rows, columns), (rows, columns), lambda i, core: (i, 0)
    else:
        shape, size, index = (rows, 2 * columns), (rows, columns), lambda i, core: (0, i)
    return call(
        merge_kernel,
        (2,),
        [pl.BlockSpec((rows, columns), lambda i, core: (0, part))] * 2,
        [pl.BlockSpec(size, index)],
        [jax.ShapeDtypeStruct(shape, F32)],
        24,
        0,
        name="merge",
        scalars=1,
    )(core[None], mine, arrived)[0]


def shaped(rows, columns, dtype):
    return jax.ShapeDtypeStruct((rows, columns), dtype)


def sum_pieces(x, refs):
    block = x.shape[1] // len(refs)
    total = dot(x[:, :block], refs[0][...])
    for key in range(1, len(refs)):
        total = total + dot(x[:, key * block : (key + 1) * block], refs[key][...])
    return total


def project_kernel(heads, quads, x_ref, bias_ref, cos_ref, sin_ref, *rest):
    wa_refs, wb_refs, (q_ref, kv_ref) = rest[:quads], rest[quads : 2 * quads], rest[2 * quads :]
    x = x_ref[...]
    lin = jnp.concatenate([sum_pieces(x, wa_refs), sum_pieces(x, wb_refs)], axis=1) + bias_ref[...]
    cosine, sine = cos_ref[...], sin_ref[...]
    for head in range(3 * heads):
        part = lin[:, head * HDIM : (head + 1) * HDIM]
        if head < 2 * heads:
            part = turn(part, cosine, sine)
        if head < heads:
            q_ref[:, head * HDIM : (head + 1) * HDIM] = part.astype(BF16)
        else:
            kv_ref[:, (head - heads) * HDIM : (head - heads + 1) * HDIM] = part.astype(BF16)


def project(x, wa, wb, bias, cosine, sine, heads):
    rows, width = x.shape
    quads, (block, cut) = len(wa), wa[0].shape
    return call(
        functools.partial(project_kernel, heads, quads),
        (rows // TILE,),
        [rows_spec(width), whole((1, 2 * cut))]
        + [rows_spec(HDIM)] * 2
        + [whole((block, cut))] * (2 * quads),
        [rows_spec(heads * HDIM), rows_spec(2 * heads * HDIM)],
        [shaped(rows, heads * HDIM, BF16), shaped(rows, 2 * heads * HDIM, BF16)],
        32,
        4 * rows * width * cut,
        name="project",
    )(x, bias, cosine, sine, *wa, *wb)


def window_keys(before_refs, own_ref, place, pair_rows, step):
    parts = []
    start = step * TILE
    reach = -WINDOW + start
    for back, ref in enumerate(before_refs):
        first = -(len(before_refs) - back) * pair_rows
        low = max(reach - first, 0)
        if low < pair_rows:
            parts.append(ref[low:, place])
    parts.append(own_ref[max(reach, 0) : start + TILE, place])
    return jnp.concatenate(parts, axis=0) if len(parts) > 1 else parts[0]


def probabilities(query, keys, key_place, low, high, peak):
    scores = dot_last(query, keys) * HDIM ** (-0.5)
    scores = jnp.where((key_place >= low) & (key_place <= high), scores, MASKED)
    if peak is None:
        top = jnp.max(scores, axis=1, keepdims=True)
        weights = jnp.exp(scores - top)
        total = jnp.sum(weights, axis=1, keepdims=True)
        return weights / total, top + jnp.log(total)
    return jnp.exp(scores - peak), peak


def attend_kernel(back, pair_rows, heads, q_ref, *rest):
    before, (own_ref, place_ref, low_ref, high_ref, out_ref, log_ref) = rest[:back], rest[back:]
    for head in range(heads):
        cols = slice(head * HDIM, (head + 1) * HDIM)
        value_cols = slice((heads + head) * HDIM, (heads + head + 1) * HDIM)
        for step in range(pair_rows // TILE):
            rows = slice(step * TILE, (step + 1) * TILE)
            first = back * pair_rows - WINDOW + step * TILE
            places = place_ref[:, max(first, 0) : back * pair_rows + (step + 1) * TILE]
            keys = window_keys(before, own_ref, cols, pair_rows, step)
            values = window_keys(before, own_ref, value_cols, pair_rows, step)
            probs, logs = probabilities(
                q_ref[rows, cols], keys, places, low_ref[rows, :], high_ref[rows, :], None
            )
            out_ref[rows, cols] = dot(probs.astype(BF16), values).astype(BF16)
            log_ref[rows, cols] = jnp.broadcast_to(logs, (TILE, HDIM))


def attend(query, before, own, places, low, high):
    rows, columns = query.shape
    heads = columns // HDIM
    back = len(before)
    return call(
        functools.partial(attend_kernel, back, rows, heads),
        (),
        [pl.BlockSpec(memory_space=pltpu.VMEM)] * (5 + back),
        [pl.BlockSpec(memory_space=pltpu.VMEM)] * 2,
        [shaped(rows, columns, BF16), shaped(rows, columns, F32)],
        40,
        4 * rows * columns * (WINDOW + TILE),
        name="attend",
    )(query, *before, own, places, low, high)


def attend_back_kernel(
    back, pair_rows, heads, core_ref, q_ref, mine_ref, other_ref, weight_ref, log_ref, *rest
):
    before = rest[:back]
    own_ref, place_ref, low_ref, high_ref, cos_ref, sin_ref = rest[back : back + 6]
    dq_ref, own_out = rest[back + 6 : back + 8]
    before_out = rest[back + 8 : 2 * back + 8]
    total_ref, grad_ref = rest[-2:]
    half = pair_rows // 2
    for ref, place in ((mine_ref, core_ref[0]), (other_ref, 1 - core_ref[0])):
        rows = pl.ds(pl.multiple_of(place * half, half), half)
        grad_ref[rows, :] = dot_last(ref[...], weight_ref[...]).astype(BF16)
    total_ref[...] = jnp.zeros_like(total_ref)
    for head in range(heads):
        cols = slice(head * HDIM, (head + 1) * HDIM)
        value_cols = slice((heads + head) * HDIM, (heads + head + 1) * HDIM)
        for step in range(pair_rows // TILE):
            rows = slice(step * TILE, (step + 1) * TILE)
            first = max(back * pair_rows - WINDOW + step * TILE, 0)
            last = back * pair_rows + (step + 1) * TILE
            keys = window_keys(before, own_ref, cols, pair_rows, step)
            values = window_keys(before, own_ref, value_cols, pair_rows, step)
            query, grad = q_ref[rows, cols], grad_ref[rows, cols]
            peak = jnp.concatenate([log_ref[rows, cols]] * ((last - first) // HDIM), axis=1)
            probs, _ = probabilities(
                query, keys, place_ref[:, first:last], low_ref[rows, :], high_ref[rows, :], peak
            )
            grad_probs = dot_last(grad, values)
            inner = jnp.sum(probs * grad_probs, axis=1, keepdims=True)
            grad_scores = (probs * (grad_probs - inner)).astype(BF16)
            grad_query = dot(grad_scores, keys) * HDIM ** (-0.5)
            dq_ref[rows, cols] = turn(grad_query, cos_ref[rows, :], -sin_ref[rows, :]).astype(BF16)
            total_ref[first:last, cols] += dot_first(grad_scores, query) * HDIM ** (-0.5)
            total_ref[first:last, value_cols] += dot_first(probs.astype(BF16), grad)
    own_out[...] = total_ref[back * pair_rows :, :]
    for step in range(back):
        before_out[step][...] = total_ref[step * pair_rows : (step + 1) * pair_rows, :].astype(BF16)


def attend_back(
    core, query, mine, other, weight, logs, before, own, places, low, high, cosine, sine
):
    rows, columns = query.shape
    back = len(before)
    vmem = pl.BlockSpec(memory_space=pltpu.VMEM)
    return call(
        functools.partial(attend_back_kernel, back, rows, columns // HDIM),
        (),
        [vmem] * (11 + back),
        [vmem] * (2 + back),
        [shaped(rows, columns, BF16), shaped(rows, 2 * columns, F32)]
        + [shaped(rows, 2 * columns, BF16)] * back,
        56,
        10 * rows * columns * (WINDOW + TILE),
        scratch=[
            pltpu.VMEM(((back + 1) * rows, 2 * columns), F32),
            pltpu.VMEM((rows, columns), BF16),
        ],
        name="attend_back",
        scalars=1,
    )(
        core[None], query, mine, other, weight, logs, *before, own, places, low, high, cosine, sine
    )


def collect_kernel(heads, back, quads, core_ref, dq_ref, own_ref, cos_ref, sin_ref, x_ref, *rest):
    arrived, wa_refs, wb_refs = rest[:back], rest[back : back + quads], rest[back + quads : back + 2 * quads]
    kept_ref, other_ref, gain_ref, bias_ref, *outs = rest[back + 2 * quads :]
    x_all, grad_all = outs[-2:]
    columns = heads * HDIM
    step = pl.program_id(0)
    total = own_ref[...]
    for ref in arrived:
        total = total + ref[...].astype(F32)
    cosine, sine = cos_ref[...], -sin_ref[...]
    heads_out = [dq_ref[...]]
    for head in range(2 * heads):
        part = total[:, head * HDIM : (head + 1) * HDIM]
        if head < heads:
            part = turn(part, cosine, sine)
        heads_out.append(part.astype(BF16))
    grads = jnp.concatenate(heads_out, axis=1)
    tile = turned(step, core_ref[0], pl.num_programs(0))
    rows = pl.ds(pl.multiple_of(tile * TILE, TILE), TILE)
    x_all[rows, :] = x_ref[...]
    grad_all[rows, :] = grads

    @pl.when(step == 0)
    def _():
        gain_ref[...] = jnp.zeros_like(gain_ref)
        bias_ref[...] = jnp.zeros_like(bias_ref)

    bias_ref[...] += jnp.sum(grads.astype(F32), axis=0, keepdims=True)
    cut = 3 * columns // 2
    block = x_ref.shape[1] // quads
    for key in range(quads):
        cols = slice(key * block, (key + 1) * block)
        part = dot_last(grads[:, :cut], wa_refs[key][...]) + dot_last(grads[:, cut:], wb_refs[key][...])
        kept_ref[:, cols] = part.astype(BF16)
        other_ref[:, cols] = part.astype(BF16)
        gain_ref[:, cols] += jnp.sum(part * x_ref[:, cols].astype(F32), axis=0, keepdims=True)

    @pl.when(step == pl.num_programs(0) - 1)
    def _():
        for key in range(quads):
            weight = dot_first(x_all[:, key * block : (key + 1) * block], grad_all[...]).astype(BF16)
            for part, up in enumerate((True, False)):
                half, index = (int(v) for v in place_of(key, quads, up))
                quarter = quads // 4
                number = 2 if half else index // quarter
                first = (index if half else index % quarter) * block
                outs[part * 3 + number][first : first + block, :] = weight[
                    :, part * cut : (part + 1) * cut
                ]


def collect(core, grad_query, own, cosine, sine, x, arrived, wa, wb):
    rows, columns = grad_query.shape
    width = x.shape[1]
    tiles = rows // TILE
    quads, (block, cut) = len(wa), wa[0].shape
    quarter = width // 4
    fixed = lambda *_: (0, 0)
    halves = halves_specs(width, tiles)
    shapes = [shaped(quarter, cut, BF16), shaped(quarter, cut, BF16), shaped(2 * quarter, cut, BF16)]
    outs = call(
        functools.partial(collect_kernel, columns // HDIM, len(arrived), quads),
        (tiles,),
        [turned_spec(columns, tiles), turned_spec(2 * columns, tiles)]
        + [turned_spec(HDIM, tiles)] * 2
        + [turned_spec(width, tiles)]
        + [turned_spec(2 * columns, tiles)] * len(arrived)
        + [whole((block, cut))] * (2 * quads),
        halves[0]
        + [pl.BlockSpec((1, width), fixed)]
        + [pl.BlockSpec((1, 3 * columns), fixed)]
        + [pl.BlockSpec(shape.shape, fixed) for shape in shapes] * 2,
        halves[1] + [shaped(1, width, F32), shaped(1, 3 * columns, F32)] + shapes * 2,
        60,
        8 * rows * width * cut,
        scratch=[pltpu.VMEM((rows, width), BF16), pltpu.VMEM((rows, 3 * columns), BF16)],
        name="collect",
        scalars=1,
    )(core[None], grad_query, own, cosine, sine, x, *arrived, *wa, *wb)
    return outs[:4], (outs[4:6], outs[6:7]), (outs[7:9], outs[9:])


def expert_kernel(routed, quads, core_ref, x_ref, wd_ref, cot_ref, scale_ref, *rest):
    if routed:
        wg_refs, wu_refs, rest = rest[:quads], rest[quads : 2 * quads], rest[2 * quads :]
        part_in, grad_in, dot_in, lane_ref = rest[:4]
        rest = rest[4:]
    else:
        wgu_refs, rest = rest[:quads], rest[quads:]
    x = x_ref[...]
    hidden, width = wd_ref.shape
    if routed:
        gate_pre = sum_pieces(x, wg_refs)
        up_pre = sum_pieces(x, wu_refs)
    else:
        pre = sum_pieces(x, wgu_refs)
        gate_pre, up_pre = pre[:, :hidden], pre[:, hidden:]
    sigma = jax.nn.sigmoid(gate_pre)
    swish = gate_pre * sigma
    active = (swish * up_pre).astype(BF16)
    rest[0][...] = active
    cot = cot_ref[...].astype(F32)
    scale = scale_ref[...]
    grad_result = (scale * cot).astype(BF16)
    rest[1][...] = grad_result
    grad_active = dot_last(grad_result, wd_ref[...])
    grad_up = grad_active * swish
    grad_gate = grad_active * up_pre * (sigma * (1.0 + gate_pre * (1.0 - sigma)))
    result = dot(active, wd_ref[...])
    if routed:
        result = result.astype(BF16).astype(F32)
    inner = jnp.sum(cot * result, axis=1, keepdims=True)
    part = scale * result
    block = width // quads
    if not routed:
        part_ref, grad_ref, inner_ref, both_ref = rest[2:]
        both = jnp.concatenate([grad_gate, grad_up], axis=1).astype(BF16)
        both_ref[...] = both
        part_ref[...] = part.astype(BF16)
        for key in range(quads):
            grad = dot_last(both, wgu_refs[key][...])
            grad_ref[:, key * block : (key + 1) * block] = grad.astype(BF16)
        inner_ref[...] = inner
        return
    part_refs, grad_refs, gate_ref, up_ref = rest[2:4], rest[4:6], rest[6], rest[7]
    grad_gate, grad_up = grad_gate.astype(BF16), grad_up.astype(BF16)
    gate_ref[...] = grad_gate
    up_ref[...] = grad_up
    part = (part + part_in[...].astype(F32)).astype(BF16)
    for ref in part_refs:
        ref[...] = part
    for key in range(quads):
        cols = slice(key * block, (key + 1) * block)
        grad = dot_last(grad_gate, wg_refs[key][...]) + dot_last(grad_up, wu_refs[key][...])
        grad = (grad.astype(BF16).astype(F32) + grad_in[:, cols].astype(F32)).astype(BF16)
        for ref in grad_refs:
            ref[:, cols] = grad
    lane = lane_ref[...]
    extra = jnp.zeros((x.shape[0], LANES), F32)
    for slot, value in enumerate((inner, dot_in[...])):
        high = value.astype(BF16).astype(F32)
        extra = extra + jnp.where(lane == 2 * slot, high, 0.0)
        extra = extra + jnp.where(lane == 2 * slot + 1, value - high, 0.0)
    for ref in grad_refs:
        ref[:, width:] = extra.astype(BF16)


def expert(core, x, pieces, wd, hidden, cot, scale, routed=()):
    rows, width = x.shape
    tiles = rows // TILE
    quads = len(pieces) // 2 if routed else len(pieces)
    spec = lambda columns: turned_spec(columns, tiles)
    ins = [spec(width), whole((hidden, width)), spec(width), spec(1)]
    ins += [whole(piece.shape) for piece in pieces]
    outs = [spec(hidden), spec(width)]
    shapes = [shaped(rows, hidden, BF16), shaped(rows, width, BF16)]
    if routed:
        ins += [spec(width), spec(width), spec(1), whole((1, LANES))]
        for columns in (width, width + LANES):
            specs, halves = halves_specs(columns, tiles)
            outs, shapes = outs + specs, shapes + halves
        outs += [spec(hidden), spec(hidden)]
        shapes += [shaped(rows, hidden, BF16)] * 2
    else:
        outs += [spec(width), spec(width), spec(1), spec(2 * hidden)]
        shapes += [shaped(rows, width, BF16)] * 2
        shapes += [shaped(rows, 1, F32), shaped(rows, 2 * hidden, BF16)]
    return call(
        functools.partial(expert_kernel, bool(routed), quads),
        (tiles,),
        ins,
        outs,
        shapes,
        60,
        12 * rows * width * hidden,
        name="expert" if routed else "shared",
        scalars=1,
    )(core[None], x, wd, cot, scale, *pieces, *routed)


def reversed_bits(value, count):
    return sum((((value >> k) & 1) << (count - 1 - k) for k in range(count)), 0 * value)


def places(step, quads, up):
    if up:
        return step & 1, reversed_bits(step >> 1, quads.bit_length() - 2)
    half = quads // 2
    return jnp.where(step < half, 0, 1), jnp.where(step < half, step, step - half)


def stack_specs(quads, up, rows, columns, merged):
    quarter = quads // 4

    def spec(half, part):
        def index(step, *_):
            if up:
                return places(step, quads, up)[1] % quarter, 0
            first = half * 2 * quarter + part * quarter
            return jnp.clip(step - first, 0, quarter - 1), 0

        return pl.BlockSpec((rows, columns), index)

    def joined(step, *_):
        if up:
            return places(step, quads, up)[1], 0
        return jnp.clip(step - 2 * quarter, 0, 2 * quarter - 1), 0

    specs = [spec(0, 0), spec(0, 1)]
    shapes = [shaped(quarter * rows, columns, BF16)] * 2
    if merged:
        specs.append(pl.BlockSpec((rows, columns), joined))
        shapes.append(shaped(2 * quarter * rows, columns, BF16))
    else:
        specs += [spec(1, 0), spec(1, 1)]
        shapes += [shaped(quarter * rows, columns, BF16)] * 2
    return specs, shapes


def store_stack(step, quads, up, merged, outs, value):
    half, index = places(step, quads, up)
    part = index // (quads // 4)
    for number, out in enumerate(outs):
        wanted = (half == number // 2) & ((part == number % 2) | (merged and number == 2))

        @pl.when(wanted)
        def _():
            out[...] = value


def row_grads_kernel(quads, cuts, x_ref, grad_ref, *outs):
    step = pl.program_id(0)
    total = dot_first(x_ref[...], grad_ref[...]).astype(BF16)
    first = 0
    for low, high, up, merged in cuts:
        count = 3 if merged else 4
        store_stack(step, quads, up, merged, outs[first : first + count], total[:, low:high])
        first += count


def row_grads(rows, grads, quads, cuts):
    count, width = rows.shape
    columns = grads.shape[1]
    block = width // quads
    specs, shapes = [], []
    for low, high, up, merged in cuts:
        more = stack_specs(quads, up, block, high - low, merged)
        specs, shapes = specs + more[0], shapes + more[1]
    outs = call(
        functools.partial(row_grads_kernel, quads, cuts),
        (quads,),
        [pl.BlockSpec((count, block), lambda i: (0, i)), whole((count, columns))],
        specs,
        shapes,
        48,
        2 * count * width * columns,
        name="row_grads",
    )(rows, grads)
    found = []
    for _, _, _, merged in cuts:
        size = 3 if merged else 4
        found.append((outs[:2], outs[2:size]))
        outs = outs[size:]
    return found


def column_grads_kernel(quads, up, quad_ref, act_ref, grad_ref, *outs):
    total = dot_first(act_ref[...], grad_ref[...]).astype(BF16)
    store_stack(pl.program_id(0), quads, up, True, outs, total)


def column_grads(acts, grads, quad, quads, up):
    count, hidden = acts.shape
    width = grads.shape[1]
    block = width // quads
    specs, shapes = stack_specs(quads, up, hidden, block, True)
    outs = pl.pallas_call(
        functools.partial(column_grads_kernel, quads, up),
        grid_spec=pltpu.PrefetchScalarGridSpec(
            num_scalar_prefetch=1,
            grid=(quads,),
            in_specs=[
                pl.BlockSpec((count, hidden), lambda i, own: (0, 0)),
                pl.BlockSpec((count, block), lambda i, own: (0, own[0] ^ i)),
            ],
            out_specs=specs,
        ),
        out_shape=shapes,
        compiler_params=pltpu.CompilerParams(vmem_limit_bytes=48 * MIB),
        cost_estimate=pl.CostEstimate(
            flops=2 * count * hidden * width,
            bytes_accessed=2 * (count * (hidden + width) + hidden * width),
            transcendentals=0,
        ),
        name="column_grads",
    )(quad[None], acts, grads)
    return outs[:2], outs[2:]


def down_grads_kernel(quads, quad_ref, act_ref, grad_ref, *rest):
    outs, total_ref = rest[:-1], rest[-1]
    step = pl.program_id(0)
    total_ref[...] = dot_first(act_ref[...], grad_ref[...])
    size = total_ref.shape[0] // quads
    quarter = quads // 4
    for part, up in enumerate((True, False)):

        @pl.when(step == part)
        def _():
            for key in range(quads):
                first = pl.multiple_of((quad_ref[0] ^ key) * size, 8)
                half, index = (int(v) for v in place_of(key, quads, up))
                number = 2 if half else index // quarter
                row = (index if half else index % quarter) * size
                outs[part * 3 + number][row : row + size, :] = total_ref[
                    pl.ds(first, size), :
                ].astype(BF16)


def place_of(key, quads, up):
    count = quads.bit_length() - 1
    spot = reversed_bits(key, count) if up else key
    return spot // (quads // 2), spot % (quads // 2)


def down_grads(acts, grads, quad, quads):
    count, hidden = acts.shape
    cut = grads.shape[1] // 2
    rows = hidden // 4
    shapes = [shaped(rows, cut, BF16), shaped(rows, cut, BF16), shaped(2 * rows, cut, BF16)] * 2
    outs = pl.pallas_call(
        functools.partial(down_grads_kernel, quads),
        grid_spec=pltpu.PrefetchScalarGridSpec(
            num_scalar_prefetch=1,
            grid=(2,),
            in_specs=[
                pl.BlockSpec((count, hidden), lambda i, own: (0, 0)),
                pl.BlockSpec((count, cut), lambda i, own: (0, i)),
            ],
            out_specs=[pl.BlockSpec(shape.shape, lambda i, own: (0, 0)) for shape in shapes],
            scratch_shapes=[pltpu.VMEM((hidden, cut), F32)],
        ),
        out_shape=shapes,
        compiler_params=pltpu.CompilerParams(vmem_limit_bytes=48 * MIB),
        cost_estimate=pl.CostEstimate(
            flops=4 * count * hidden * cut,
            bytes_accessed=2 * (count * (hidden + 2 * cut) + 2 * hidden * cut),
            transcendentals=0,
        ),
        name="down_grads",
    )(quad[None], acts, grads)
    return (outs[:2], outs[2:3]), (outs[3:5], outs[5:])


def local(
    residual_in,
    attention_gain,
    query_weight,
    query_bias,
    key_weight,
    key_bias,
    value_weight,
    value_bias,
    output_weight,
    feedforward_gain,
    router_weight,
    shared_logit_weight,
    shared_gate_weight,
    shared_up_weight,
    shared_down_weight,
    expert_gate,
    expert_up,
    expert_down,
    cotangent,
    expert_index,
    token_live,
    document_lengths,
):
    ep_count = lax.axis_size("ep")
    grp_count = lax.axis_size("grp")
    quads = grp_count // 2
    rows_dev, width = residual_in.shape
    group_rows = rows_dev * ep_count
    pair_rows = 2 * group_rows
    seq_len = group_rows * grp_count // SEQS
    expert_count = expert_gate.shape[0] * ep_count
    ffe = expert_gate.shape[2]
    ffs_half = shared_gate_weight.shape[1] // 2
    grp = lax.axis_index("grp")
    ep = lax.axis_index("ep")
    core = grp % 2
    quad = grp // 2
    back = -(-WINDOW // pair_rows)
    heads = query_weight.shape[1] // HDIM // 2
    head_width = heads * HDIM
    up_order = quad_bits()
    down_order = up_order[::-1]

    block = width // quads
    cut = len(up_order) // 2
    up_one, up_two = up_order[:cut], up_order[cut:]
    down_one, down_two = down_order[: len(down_order) - cut], down_order[len(down_order) - cut :]
    ep_masks = [1 << b for b in range(ep_count.bit_length() - 1)]
    quad_masks = [2 * bit for bit in up_order]
    seq_groups = grp_count // SEQS
    experts = jnp.arange(expert_count, dtype=jnp.int32)
    ed_cut = width // 2

    def shifted(values, steps):
        route = [
            (i, i + 2 * steps)
            for i in range(grp_count)
            if 0 <= i + 2 * steps < grp_count and i // seq_groups == (i + 2 * steps) // seq_groups
        ]
        return lax.ppermute(values, "grp", route)

    def gathered(values):
        return lax.all_gather(values, "ep", axis=0, tiled=True)

    def scattered(values):
        return lax.psum_scatter(values, "ep", scatter_dimension=0, tiled=True)

    def core_sum(kept, other):
        return add_rows(kept, across(other, 1))

    def finished(kept, arrived, axis):
        mine, other = finish(core[None], kept, arrived, axis)
        return mine, across(other, 1)

    def merged(halves):
        return merge(core, halves[0], across(halves[1], 1), None)

    hidden_in = residual_in.astype(F32)
    grad_out = cotangent.astype(F32)
    gain_one = attention_gain.astype(F32)
    gain_two = feedforward_gain.astype(F32)
    router_all = jnp.concatenate([router_weight, shared_logit_weight[:, None]], axis=1)
    router_flipped = flip_columns(router_all.T, quad).T
    scale_one = norm_scale(hidden_in)
    unit_one = hidden_in * scale_one
    normed_one = (unit_one * gain_one).astype(BF16)
    group_one = gathered(flip_columns(normed_one, quad))

    qk_keep, qk_other = zip(
        *[split_core(weight, core, 1) for weight in (query_weight, key_weight, value_weight)]
    )
    qkv_keep, qkv_other = jnp.concatenate(qk_keep, 1), jnp.concatenate(qk_other, 1)
    qkv_block = merge_core(qkv_keep, across(qkv_other, 1), core, 0)
    qkv_cut = qkv_block.shape[1] // 2
    qkv_a = {0: qkv_block[:, :qkv_cut]}
    qkv_b = {0: qkv_block[:, qkv_cut:]}
    (
        qkv_a, qkv_b, output_weight, shared_gate_weight, shared_up_weight, shared_down_weight,
        expert_gate, expert_up, expert_down,
    ) = together(
        qkv_a, qkv_b, output_weight, shared_gate_weight, shared_up_weight, shared_down_weight,
        expert_gate, expert_up, expert_down,
    )
    qkv_a_one, qkv_a_two = gather_quads(qkv_a, up_one), gather_quads(qkv_a, up_two)
    qkv_b_one, qkv_b_two = gather_quads(qkv_b, down_one), gather_quads(qkv_b, down_two)

    o_keep, o_other = split_core(output_weight, core, 0)
    sg_keep, sg_other = split_core(shared_gate_weight, core, 1)
    su_keep, su_other = split_core(shared_up_weight, core, 1)
    gu_keep = jnp.concatenate([sg_keep, su_keep], axis=1)
    gu_other = jnp.concatenate([sg_other, su_other], axis=1)
    gu_block = merge_core(gu_keep, across(gu_other, 1), core, 0)
    sd_keep, sd_other = split_core(shared_down_weight, core, 0)
    sd_keep = jnp.concatenate([sd_keep, o_keep], axis=0)
    sd_other = jnp.concatenate([sd_other, o_other], axis=0)
    sd_block = merge_core(sd_keep, across(sd_other, 1), core, 1)

    def expert_block(weight):
        keep, other = split_core(weight, core, 0)
        return merge_core(keep[0], across(other[0], 1), core, 0)

    eg_block, eu_block, ed_block = [
        expert_block(weight) for weight in (expert_gate, expert_up, expert_down)
    ]
    eda_block, edb_block = ed_block[:, :ed_cut], ed_block[:, ed_cut:]

    (
        qkv_a_one, qkv_a_two, qkv_b_one, qkv_b_two, gu_block, sd_block, eg_block, eu_block,
        eda_block, edb_block,
    ) = together(
        qkv_a_one, qkv_a_two, qkv_b_one, qkv_b_two, gu_block, sd_block, eg_block, eu_block,
        eda_block, edb_block,
    )
    qkv_a_rest = gather_rest(qkv_a_one, up_two)
    qkv_b_rest = gather_rest(qkv_b_one, down_two)
    sd_one, sd_two = gather_quads({0: sd_block}, down_one), gather_quads({0: sd_block}, down_two)
    chosen = (
        (expert_index[:, :, None] == experts[None, None, :]) & (token_live[:, None, None] > 0)
    ).any(axis=1)
    cot_packed = jnp.concatenate(
        [cotangent, jnp.pad(chosen.astype(BF16), ((0, 0), (0, LANES - expert_count)))], axis=1
    )
    chosen = chosen.astype(F32)
    bias = jnp.concatenate(
        [split_core(b, core, 0)[0] for b in (query_bias, key_bias, value_bias)]
    ).astype(F32)[None, :]
    key_place = (quad - back) * pair_rows + jnp.arange((back + 1) * pair_rows, dtype=jnp.int32)
    query_place = key_place[back * pair_rows :]
    _, position = doc_layout(document_lengths, seq_len, query_place)
    low = jnp.maximum(query_place - position, query_place - WINDOW + 1)[:, None]
    high, key_place = query_place[:, None], key_place[None, :]
    cosine, sine = rope_tables(position)
    (
        group_one, qkv_a, qkv_b, sd_one, sd_two, gu_block, eg_block, eu_block, eda_block,
         edb_block, cot_packed, bias, cosine, sine, low, high,
    ) = together(
        group_one, qkv_a_one | qkv_a_two | qkv_a_rest, qkv_b_one | qkv_b_two | qkv_b_rest,
        sd_one, sd_two, gu_block, eg_block, eu_block, eda_block, edb_block, cot_packed, bias,
        cosine, sine, low, high,
    )

    rows_one = join_rows(core, group_one, across(group_one, 1))
    gu_two = gather_quads({0: gu_block}, up_two)
    sd_rest = gather_rest(sd_one, down_two)
    cot_group = gathered(cot_packed)
    qkv_a, qkv_b = listed(qkv_a), listed(qkv_b)
    query, key_value = project(rows_one, qkv_a, qkv_b, bias, cosine, sine, heads)

    before = [shifted(key_value, step) for step in range(back, 0, -1)]
    down_full = place_quads(sd_one | sd_two | sd_rest, quad, 1)
    output_rows = down_full[ffs_half:]
    query, before, gu_two, edb_block, down_full, output_rows = together(
        query, before, gu_two, edb_block, down_full, output_rows
    )
    edb_one, edb_two = gather_quads({0: edb_block}, down_one), gather_quads({0: edb_block}, down_two)
    attended, log_total = attend(query, before, key_value, key_place, low, high)
    kept, other = split_core(attended, core, 0)
    other = dot(other, output_rows).astype(BF16)
    kept, other, cot_group, edb_one, edb_two = together(kept, other, cot_group, edb_one, edb_two)
    branch = add_rows(dot(kept, output_rows).astype(BF16), across(other, 1))
    branch, gu_block, eu_block, eda_block, cot_group = together(
        branch, gu_block, eu_block, eda_block, cot_group
    )
    branch_sum = scattered(branch)
    cot_other = across(cot_group, 1)
    gu_one = gather_quads({0: gu_block}, up_one)
    eda_one, eda_two = gather_quads({0: eda_block}, up_one), gather_quads({0: eda_block}, up_two)
    eu_one = gather_quads({0: eu_block}, down_one)
    ed_full = jnp.zeros((eda_block.shape[0] * quads, width), BF16)
    ed_full = place_quads(edb_one | edb_two, quad, 0, ed_full, ed_cut)
    branch_sum, cot_other, gu_one, eda_one, eda_two, eu_one, eg_block, edb_one, ed_full = (
        together(
            branch_sum, cot_other, gu_one, eda_one, eda_two, eu_one, eg_block, edb_one, ed_full,
        )
    )

    eg_one = gather_quads({0: eg_block}, up_one)
    edb_rest = gather_rest(edb_one, down_two)
    gu_rest, eda_rest = gather_rest(gu_one, up_two), gather_rest(eda_one, up_two)
    mixed = hidden_in + branch_sum.astype(F32)
    scale_two = norm_scale(mixed)
    unit_two = mixed * scale_two
    normed_two = (unit_two * gain_two).astype(BF16)
    group_two = gathered(flip_columns(normed_two, quad))
    cot_rows = join_rows(core, cot_group, cot_other)
    ed_full = place_quads(eda_one | eda_two, quad, 0, ed_full)
    (
        group_two, eg_one, edb_rest, gu_rest, eda_rest, eu_block, eg_block, eu_one, cot_rows,
        ed_full,
    ) = together(
        group_two, eg_one, edb_rest, gu_rest, eda_rest, eu_block, eg_block, eu_one, cot_rows,
        ed_full,
    )
    eu_two, eg_two = gather_quads({0: eu_block}, down_two), gather_quads({0: eg_block}, up_two)
    eu_rest, eg_rest = gather_rest(eu_one, down_two), gather_rest(eg_one, up_two)
    rows_two = join_rows(core, group_two, across(group_two, 1))
    gu_pieces = listed(gu_one | gu_two | gu_rest)

    def router(rows, weight):
        logits = dot(rows, weight)
        return jax.nn.softmax(logits[:, :expert_count], axis=-1), jax.nn.sigmoid(
            logits[:, expert_count:]
        )

    chosen_rows = cot_rows[:, width : width + expert_count].astype(F32)
    probs_rows, shared_scale_rows = router(rows_two, router_flipped)
    router_probs, shared_scale = router(normed_two, router_all)
    mine = (experts == ep * 2 + core).astype(F32)[None, :]
    gate = jnp.sum(probs_rows * chosen_rows * mine, axis=1, keepdims=True)

    shared_active, grad_shared_out, part, grad_part, shared_dot, grad_gu = expert(
        core, rows_two, gu_pieces, down_full, ffs_half, cot_rows, shared_scale_rows
    )
    gu_cut = 2 * ffs_half * 3 // 4 // LANES * LANES
    (gua_grad, gua_out), (gub_grad, gub_out) = row_grads(
        rows_two, grad_gu, quads, [(0, gu_cut, True, True), (gu_cut, 2 * ffs_half, False, True)]
    )
    sd_grad, sd_out = column_grads(shared_active, grad_shared_out, quad, quads, False)
    gua_grad, eda_rest, edb_rest, ed_full = together(gua_grad, eda_rest, edb_rest, ed_full)
    ed_full = place_quads(eda_rest, quad, 0, ed_full)
    ed_full = place_quads(edb_rest, quad, 0, ed_full, ed_cut)
    (
        grad_part, part, eu_two, eg_two, eu_rest, eg_rest, ed_full, gua_grad, gua_out, gub_grad,
        gub_out, sd_grad, sd_out, gate,
    ) = together(
        grad_part, part, eu_two, eg_two, eu_rest, eg_rest, ed_full, gua_grad, gua_out, gub_grad,
        gub_out, sd_grad, sd_out, gate,
    )
    eg_pieces, eu_pieces = eg_one | eg_two | eg_rest, eu_one | eu_two | eu_rest

    def sent(blocks, bit):
        return [across(part, 2 * bit) for part in blocks]

    gua_sent, gub_sent = sent(gua_out, up_order[0]), sent(gub_out, down_order[0])
    sd_sent = sent(sd_out, down_order[0])

    lanes = jnp.arange(LANES, dtype=jnp.int32)
    lanes = jnp.where(lanes % expert_count == ep * 2 + core, lanes // expert_count, -1)[None, :]
    active, grad_result, *sums, grad_gate_pre, grad_up_pre = expert(
        core,
        rows_two,
        listed(eg_pieces) + listed(eu_pieces),
        ed_full,
        ffe,
        cot_rows,
        gate,
        (part, grad_part, shared_dot, lanes),
    )
    sums, gua_sent, gub_sent, sd_sent, gua_grad, gub_grad, sd_grad = together(
        sums, gua_sent, gub_sent, sd_sent, gua_grad, gub_grad, sd_grad
    )
    forward_part, packed = sums[:2], core_sum(*sums[2:])
    lead = [
        add_low(parts[1], arrived[0][parts[0].shape[0] :])
        for parts, arrived in ((gua_grad, gua_sent), (gub_grad, gub_sent), (sd_grad, sd_sent))
    ]
    (
        packed, lead, gua_grad, gua_sent, gub_grad, gub_sent, sd_grad, sd_sent, active, grad_result,
        grad_gate_pre, grad_up_pre,
    ) = together(
        packed, lead, gua_grad, gua_sent, gub_grad, gub_sent, sd_grad, sd_sent, active, grad_result,
        grad_gate_pre, grad_up_pre,
    )
    first_parts = [gua_grad[0], gua_sent[0], gub_grad[0], gub_sent[0], sd_grad[0], sd_sent[0]]
    spread = scattered(packed)
    gua_sent, gub_sent = across(lead[0], 2 * up_order[1]), across(lead[1], 2 * down_order[1])
    sd_sent = across(lead[2], 2 * down_order[1])
    (eda_grad, eda_out), (edb_grad, edb_out) = down_grads(active, grad_result, quad, quads)
    eda_out, edb_out, grad_gate_pre = together(eda_out, edb_out, grad_gate_pre)
    eda_sent, edb_sent = sent(eda_out, up_order[0]), sent(edb_out, down_order[0])
    ((eg_grad, eg_out),) = row_grads(rows_two, grad_gate_pre, quads, [(0, ffe, True, False)])
    eg_grad, eg_out, grad_up_pre, gua_sent, gub_sent, sd_sent, first_parts = together(
        eg_grad, eg_out, grad_up_pre, gua_sent, gub_sent, sd_sent, first_parts
    )
    gua_grad, gub_grad, sd_grad = [
        [add_low(kept, arrived[: kept.shape[0]])]
        for kept, arrived in zip(first_parts[::2], first_parts[1::2])
    ]
    ((eu_grad, eu_out),) = row_grads(rows_two, grad_up_pre, quads, [(0, ffe, False, False)])
    spread, eg_grad, eg_out = together(spread, eg_grad, eg_out)

    grad_normed_two = flip_columns(spread[:, :width], quad).astype(F32)
    side = spread[:, width : width + 4 * expert_count].astype(F32).reshape(rows_dev, 4, expert_count)
    grad_gate_own = side[:, 0] + side[:, 1]
    shared_dot_own = jnp.sum(side[:, 2] + side[:, 3], axis=1, keepdims=True)
    grad_logit = shared_dot_own * shared_scale * (1.0 - shared_scale)
    grad_probs = grad_gate_own * chosen
    grad_logits = router_probs * (
        grad_probs - jnp.sum(router_probs * grad_probs, axis=-1, keepdims=True)
    )
    grad_router = jnp.concatenate([grad_logits, grad_logit], axis=1)
    router_grad = dot_first(normed_two.astype(F32), grad_router)
    grad_normed_two = grad_normed_two + dot_last(grad_router, router_all.astype(F32))
    grad_norm_part, ff_gain_grad = norm_backward(grad_normed_two, unit_two, scale_two, gain_two)
    grad_mixed = grad_out + grad_norm_part
    (
        branch_low, eda_grad, eda_sent, edb_grad, edb_sent, gua_grad, gua_sent, gub_grad, gub_sent,
        sd_grad, sd_sent, eg_out, eu_grad, eu_out, forward_part,
    ) = together(
        grad_mixed.astype(BF16), eda_grad, eda_sent, edb_grad, edb_sent, gua_grad, gua_sent, gub_grad,
        gub_sent, sd_grad, sd_sent, eg_out, eu_grad, eu_out, forward_part,
    )
    group_branch = gathered(branch_low)
    eg_sent = sent(eg_out[:1], up_order[0])
    eu_sent = sent(eu_out[:1], down_order[0])
    forward_part = core_sum(*forward_part)
    forward_part, gua_grad, gua_sent, gub_grad, gub_sent, sd_grad, sd_sent = together(
        forward_part, gua_grad, gua_sent, gub_grad, gub_sent, sd_grad, sd_sent
    )
    eda_grad = first_sum(eda_grad, eda_sent)
    edb_grad = first_sum(edb_grad, edb_sent)
    eda_sent, edb_sent = across(eda_grad[1], 2 * up_order[1]), across(edb_grad[1], 2 * down_order[1])

    gua_mine, gua_arrived = finished(*rest_parts(gua_grad[0], gua_sent, up_order), 0)
    gub_mine, gub_arrived = finished(*rest_parts(gub_grad[0], gub_sent, down_order), 0)
    sd_mine, sd_arrived = finished(*rest_parts(sd_grad[0], sd_sent, down_order), 1)
    gu_mine = jnp.concatenate([gua_mine, gub_mine], axis=1)
    gu_arrived = jnp.concatenate([gua_arrived, gub_arrived], axis=1)
    sg_grad, su_grad = [
        merge_core(
            gu_mine[:, part * ffs_half : (part + 1) * ffs_half],
            gu_arrived[:, part * ffs_half : (part + 1) * ffs_half],
            core,
            1,
        ).astype(F32)
        for part in range(2)
    ]
    sd_grad = merge(core, sd_mine, sd_arrived, 0)
    (
        group_branch, forward_part, sg_grad, su_grad, sd_grad, eg_grad, eg_out, eg_sent, eu_grad, eu_out, eu_sent, eda_grad,
        eda_sent, edb_grad, edb_sent,
    ) = together(
        group_branch, forward_part, sg_grad, su_grad, sd_grad, eg_grad, eg_out, eg_sent, eu_grad, eu_out, eu_sent, eda_grad,
        eda_sent, edb_grad, edb_sent,
    )
    other_branch = across(group_branch, 1)
    eg_sent = eg_sent + sent(eg_out[1:], up_order[0])
    eu_sent = eu_sent + sent(eu_out[1:], down_order[0])

    layer_sum = scattered(forward_part)
    grad_query, grad_own, *grad_before = attend_back(
        core, query, group_branch, other_branch, output_rows, log_total, before, key_value, key_place,
        low, high, cosine, sine,
    )
    grad_query, grad_before, group_branch, other_branch, eg_grad, eu_grad = together(
        grad_query, grad_before, group_branch, other_branch, eg_grad, eu_grad
    )
    arrived = [shifted(sent, step - back) for step, sent in enumerate(grad_before)]
    cut = eg_grad[1].shape[0] // 2
    eg_grad = [
        add_low(eg_grad[0], eg_sent[0]),
        add_low(eg_grad[1][:cut], eg_sent[1][:cut]),
        add_low(eg_grad[1][cut:], eg_sent[1][cut:]),
    ]
    eu_grad = [
        add_low(eu_grad[0], eu_sent[0]),
        add_low(eu_grad[1][:cut], eu_sent[1][:cut]),
        add_low(eu_grad[1][cut:], eu_sent[1][cut:]),
    ]
    eg_rest = across(eg_grad[1], 2 * up_order[1])
    arrived, eg_grad, eu_grad, group_branch, other_branch = together(
        arrived, eg_grad, eu_grad, group_branch, other_branch
    )
    eu_rest = across(eu_grad[1], 2 * down_order[1])
    (*partial, att_gain_part, bias_part), (qkv_a_grad, qkv_a_out), (qkv_b_grad, qkv_b_out) = collect(
        core, grad_query, grad_own, cosine, sine, rows_one, arrived, qkv_a, qkv_b
    )
    partial, qkv_a_out, qkv_b_out, eg_grad, eg_rest, eu_grad, eu_rest = together(
        partial, qkv_a_out, qkv_b_out, eg_grad, eg_rest, eu_grad, eu_rest
    )
    eg_last, eu_last = across(eg_grad[2], 2 * up_order[1]), across(eu_grad[2], 2 * down_order[1])
    qkv_a_sent, qkv_b_sent = sent(qkv_a_out, up_order[0]), sent(qkv_b_out, down_order[0])
    partial_sum = core_sum(*partial)

    (
        partial_sum, att_gain_part, bias_part, group_branch, other_branch, qkv_a_grad, qkv_b_grad, eda_grad,
        eda_sent, edb_grad, edb_sent,
    ) = together(
        partial_sum, att_gain_part, bias_part, group_branch, other_branch, qkv_a_grad, qkv_b_grad, eda_grad,
        eda_sent, edb_grad, edb_sent,
    )
    grad_normed_one = scattered(partial_sum)
    grad_branch = join_rows(core, group_branch, other_branch)
    o_grad, o_out = column_grads(attended, grad_branch, quad, quads, False)
    att_gain_part = flip_columns(att_gain_part[0], quad) / gain_one
    late = jnp.concatenate([att_gain_part, ff_gain_grad, router_grad.T.reshape(-1)])
    late = sum_everywhere(late, [], ep_masks)
    o_sent = sent(o_out, down_order[0])
    (
        late, qkv_a_sent, qkv_b_sent, eg_last, eu_last, eda_sent, edb_sent,
    ) = together(
        late, qkv_a_sent, qkv_b_sent, eg_last, eu_last, eda_sent, edb_sent,
    )
    bias_part = bias_part.reshape(3, head_width)
    bias_part = jnp.concatenate(
        [jnp.where(core == 0, bias_part, 0.0), jnp.where(core == 0, 0.0, bias_part)], axis=1
    )
    late = sum_everywhere(jnp.concatenate([late, bias_part.reshape(-1)]), [1], [])
    lead = [
        add_low(parts[1], arrived[0][parts[0].shape[0] :])
        for parts, arrived in ((qkv_a_grad, qkv_a_sent), (qkv_b_grad, qkv_b_sent), (o_grad, o_sent))
    ]
    lead, qkv_a_grad, qkv_b_grad, o_grad, qkv_a_sent, qkv_b_sent, o_sent, eg_last, eu_last = together(
        lead, qkv_a_grad, qkv_b_grad, o_grad, qkv_a_sent, qkv_b_sent, o_sent, eg_last, eu_last
    )
    eda_sent, edb_sent, _ = together(eda_sent, edb_sent, lead)
    qkv_a_grad, qkv_b_grad, o_grad = [
        [add_low(parts[0], arrived[0][: parts[0].shape[0]]), ahead]
        for parts, arrived, ahead in zip(
            (qkv_a_grad, qkv_b_grad, o_grad), (qkv_a_sent, qkv_b_sent, o_sent), lead
        )
    ]
    eg_rest = jnp.concatenate([eg_rest, eg_last], axis=0)
    eu_rest = jnp.concatenate([eu_rest, eu_last], axis=0)
    qkv_a_rest = across(qkv_a_grad[1], 2 * up_order[1])
    qkv_b_rest = across(qkv_b_grad[1], 2 * down_order[1])
    o_rest = across(o_grad[1], 2 * down_order[1])
    late = sum_everywhere(late, quad_masks, [])
    last = [
        finish(core[None], *rest_parts(kept, arrived, order), 0)
        for kept, arrived, order in (
            (eg_grad[0], eg_rest, up_order),
            (eu_grad[0], eu_rest, down_order),
            (eda_grad[0], eda_sent, up_order),
            (edb_grad[0], edb_sent, down_order),
        )
    ]
    last, qkv_a_rest, qkv_b_rest, o_rest = together(last, qkv_a_rest, qkv_b_rest, o_rest)
    eg_grad, eu_grad, eda_grad, edb_grad = [merged(halves) for halves in last]
    ed_grad = jnp.concatenate([eda_grad, edb_grad], axis=2)
    layer_out = (mixed + layer_sum.astype(F32)).astype(BF16)
    qkv_a_mine, qkv_a_arrived = finished(*rest_parts(qkv_a_grad[0], qkv_a_rest, up_order), 0)
    qkv_b_mine, qkv_b_arrived = finished(*rest_parts(qkv_b_grad[0], qkv_b_rest, down_order), 0)
    o_mine, o_arrived = finished(*rest_parts(o_grad[0], o_rest, down_order), 1)
    (
        grad_normed_one, qkv_a_mine, qkv_a_arrived, qkv_b_mine, qkv_b_arrived, o_mine, o_arrived,
        late, eu_grad, eg_grad, ed_grad, layer_out,
    ) = together(
        grad_normed_one, qkv_a_mine, qkv_a_arrived, qkv_b_mine, qkv_b_arrived, o_mine, o_arrived,
        late, eu_grad, eg_grad, ed_grad, layer_out,
    )
    qkv_mine = jnp.concatenate([qkv_a_mine, qkv_b_mine], axis=1)
    qkv_arrived = jnp.concatenate([qkv_a_arrived, qkv_b_arrived], axis=1)
    q_grad, k_grad, v_grad = [merge(core, qkv_mine, qkv_arrived, 1, part, 3) for part in range(3)]
    o_grad = merge(core, o_mine, o_arrived, 0)
    att_gain_grad, ff_gain_grad = late[:width], late[width : 2 * width]
    router_grad = late[2 * width : (expert_count + 3) * width].reshape(expert_count + 1, width)
    bias_mine = late[(expert_count + 3) * width :].reshape(3, 2 * head_width)
    grad_norm_one, _ = norm_backward(
        flip_columns(grad_normed_one, quad).astype(F32), unit_one, scale_one, gain_one
    )
    input_grad = grad_mixed + grad_norm_one
    return (
        layer_out,
        input_grad,
        att_gain_grad,
        q_grad,
        bias_mine[0],
        k_grad,
        bias_mine[1],
        v_grad,
        bias_mine[2],
        o_grad,
        ff_gain_grad,
        router_grad[:expert_count].T,
        router_grad[expert_count],
        sg_grad,
        su_grad,
        sd_grad,
        eg_grad,
        eu_grad,
        ed_grad,
    )


def solution(mesh):
    tokens = P(("grp", "ep"), None)
    rows, columns, experts = P("grp", "ep"), P("ep", "grp"), P("ep", "grp", None)
    in_specs = (
        tokens, P(), rows, P("ep"), rows, P("ep"), rows, P("ep"), columns, P(), P(), P(),
        rows, rows, columns, experts, experts, experts, tokens, tokens, P(("grp", "ep")), P(),
    )
    out_specs = (
        tokens, tokens, P(), rows, P("ep"), rows, P("ep"), rows, P("ep"), columns, P(), P(), P(),
        rows, rows, columns, experts, experts, experts,
    )
    return jax.shard_map(local, mesh=mesh, in_specs=in_specs, out_specs=out_specs, check_vma=False)
```
